32 devices in a mesh: dp: 8 (over z, x), shard: 4 (over y, core).
Axes of the slice: x: 2, y: 2, z: 4, core: 2. Of those that a mesh axis runs over, the one named last changes fastest.
Arguments:
- tokens: bfloat16 [2048, 2048], P(('dp', 'shard')), may hold values from -6 to 6
- router_probs: float32 [2048, 8], P(('dp', 'shard')), may hold values from 0.05 to 1
- expert_ids: int32 [2048, 8], P(('dp', 'shard')), may hold values from 0 to 15, all different within a row; in each aligned block of 64 rows (0 to 63, 64 to 127, ...) at most 64 rows name the same one
- old_place: int32 [16], replicated, may hold values from 0 to 15, as said below
- new_place: int32 [16], replicated, may hold values from 0 to 15, as said below
- w_gate: bfloat16 [16, 2048, 1024], P('dp', 'shard'), may hold values from -0.125 to 0.125
- w_up: bfloat16 [16, 2048, 1024], P('dp', 'shard'), may hold values from -0.125 to 0.125
- w_down: bfloat16 [16, 2048, 1024], P('dp', 'shard'), may hold values from -0.1875 to 0.1875
Outputs:
- moe_output: bfloat16 [2048, 2048], P(('dp', 'shard'))
- new_gate: bfloat16 [16, 2048, 1024], P('dp', 'shard')
- new_up: bfloat16 [16, 2048, 1024], P('dp', 'shard')
- new_down: bfloat16 [16, 2048, 1024], P('dp', 'shard')
The draws below stay inside these ranges and needn't reach their ends.
Inputs may be any that keep to these rules, and one draw needn't show every extreme that they name: `expert_ids`: each token names 8 different experts; among the tokens of one device no expert is named by more than 64 tokens, a bound that some block reaches. `old_place`: a permutation of the 16 experts over the 16 slots. `new_place`: equal to old_place except at exactly one of the slots 2 k and 2 k + 1 for each k; the expert leaving the refilled slot of k moves to the refilled slot of (k + 1) mod (8), so that new_place is again a permutation.
All inputs are finite; a program needn't handle non-finite values.
Results may differ from the reference program's by a relative error of at most 0.0064.
Values may be sent and summed in bfloat16 or wider, within the bound.
No kernel may reach another device: no remote copies, remote signals or barrier semaphores. Data moves between devices by JAX's collectives and lax.ppermute only.
A program may use at most 128 MiB of HBM per device.

```python
import math
import jax
import jax.numpy as jnp
import numpy as np
from jax import lax

D = 2048
FF = 1024
TOP = 8
TOK_DEV = 64
SLOTS = 16
EXPERTS = 16
CAP = 64
TOKENS = 2048


def placements(key):
    row_total = SLOTS // 2
    old_slots = jax.random.permutation(jax.random.fold_in(key, 11), SLOTS).astype(jnp.int32)
    chosen = jax.random.randint(jax.random.fold_in(key, 12), (row_total,), 0, 2).astype(jnp.int32)
    refilled = 2 * jnp.arange(row_total, dtype=jnp.int32) + chosen
    target_row = ((jnp.arange(row_total, dtype=jnp.int32) + 1) % row_total).astype(jnp.int32)
    new_slots = old_slots.at[refilled[target_row]].set(old_slots[refilled])
    return (old_slots, new_slots)


def draw_old_place(key, part):
    return placements(key)[0]


def draw_new_place(key, part):
    return placements(key)[1]


def steps_of(rng, shape, cuts, low, top_value):
    def one(position, shards_of):
        draws = jax.random.uniform(jax.random.fold_in(jax.random.fold_in(rng, 6), position), (shards_of,), jnp.float32, low / len(cuts), top_value / len(cuts))
        return jnp.repeat(jnp.exp(draws), shape[position] // shards_of).reshape((-1,) + (1,) * (len(shape) - position - 1))

    gain = one(*cuts[0])
    for cut in cuts[1:]:
        gain = gain * one(*cut)
    return gain


def routed_block(stream_key, own, number, rows, number_of, top, limit, lean):
    ranking = jax.random.permutation(stream_key, number_of)
    heavy_load, usual = load_shares(number_of, rows * top, limit, lean, True), load_shares(number_of, rows * top, limit, lean, False)
    places = jnp.arange(number_of)

    def named(lengths, turn):
        used = int((lengths > 0).sum())
        fixed = max(1, used // 4)
        moved = fixed + (places - fixed + turn * (used - fixed)) % max(1, number_of - fixed)
        return jnp.zeros((number_of,), jnp.int32).at[ranking[jnp.where(places < fixed, places, moved)]].set(jnp.asarray(lengths, jnp.int32))

    lengths = jnp.where(number % 4 == 0, named(heavy_load, number // 4), named(usual, number - number // 4 - 1))
    mixed = jax.random.permutation(jax.random.fold_in(own, 3), number_of)
    donor, sink = mixed[0:number_of // 2 * 2:2], mixed[1:number_of // 2 * 2:2]
    slack = jnp.minimum(lengths[donor] - 1, limit - lengths[sink]) // 2
    slack = jnp.where((donor == ranking[0]) | (sink == ranking[0]) | (lengths[sink] == 0), 0, jnp.maximum(slack, 0))
    moved = jax.random.randint(jax.random.fold_in(own, 4), (number_of // 2,), 0, 1 << 20) % (slack + 1)
    lengths = lengths.at[donor].add(-moved).at[sink].add(moved)
    items = jnp.searchsorted(jnp.cumsum(lengths), jnp.arange(rows * top), side="right").astype(jnp.int32)
    table = items.reshape(top, rows).T
    table = table[jax.random.permutation(jax.random.fold_in(own, 1), rows)]
    turn = jax.random.randint(jax.random.fold_in(own, 2), (rows, 1), 0, top)
    return jnp.take_along_axis(table, (jnp.arange(top)[None, :] + turn) % top, axis=1)


def load_shares(amount, total, reach, lean, full):
    loads = [(1 << 20) // math.isqrt(grade ** lean) + 1 for grade in range(1, amount + 1)]
    largest = reach if full else min(reach, max(-(-total // amount), total * loads[0] // sum(loads)))
    least = 1 if total - largest >= amount - 1 else 0
    holding, surplus = [largest] + [least] * (amount - 1), total - largest - least * (amount - 1)
    while surplus > 0:
        free = [i for i in range(1, amount) if holding[i] < largest] or [i for i in range(1, amount) if holding[i] < reach]
        mass, budget = sum([loads[i] for i in free]), surplus
        for i in free:
            more = min(reach - holding[i], max(1, budget * loads[i] // mass), surplus)
            holding[i] = holding[i] + more
            surplus = surplus - more
    return np.array(holding)


def centred(rng, extent, deviation, limit, cuts=(), kind=jnp.bfloat16):
    factor_of = steps_of(rng, extent, cuts, -0.22, 0.18) if cuts else 1.0
    entries = jax.random.normal(rng, extent, jnp.float32) * deviation * factor_of
    return jnp.minimum(jnp.maximum(entries, -limit), limit).astype(kind)


def setup_inputs(seed: int = 0) -> dict:
    key_list = jax.random.split(jax.random.key(seed), 9)
    tokens = centred(key_list[0], (TOKENS, D), 1.0, 6.0, ((0, 32),))
    router_probs = jnp.clip(jnp.exp(math.log(1.0) - 2.9957323 * jax.random.uniform(key_list[1], (TOKENS, TOP), jnp.float32) ** steps_of(key_list[1], (TOKENS, TOP), ((0, 32),), -0.2, 0.2)), 0.05, 1.0)
    expert_ids_keys = jax.random.split(jax.random.fold_in(key_list[2], 1), TOKENS // TOK_DEV)
    expert_ids_turns = jax.random.permutation(jax.random.fold_in(key_list[2], 3), TOKENS // TOK_DEV)
    expert_ids = jax.vmap(lambda own, number: routed_block(jax.random.fold_in(key_list[2], 2), own, number, TOK_DEV, EXPERTS, TOP, CAP, 2))(expert_ids_keys, expert_ids_turns).reshape((TOKENS, TOP))
    old_place = draw_old_place(jax.random.fold_in(key_list[8], 71), 0)
    new_place = draw_new_place(jax.random.fold_in(key_list[8], 71), 0)
    w_gate = centred(key_list[5], (SLOTS, D, FF), D ** -0.5, 0.125, ((0, 8), (1, 4)))
    w_up = centred(key_list[6], (SLOTS, D, FF), D ** -0.5, 0.125, ((0, 8), (1, 4)))
    w_down = centred(key_list[7], (SLOTS, D, FF), FF ** -0.5, 0.1875, ((0, 8), (1, 4)))
    return {"tokens": tokens, "router_probs": router_probs, "expert_ids": expert_ids, "old_place": old_place, "new_place": new_place, "w_gate": w_gate, "w_up": w_up, "w_down": w_down}


def reference(tokens, router_probs, expert_ids, old_place, new_place, w_gate, w_up, w_down):
    pair_count = TOKENS * TOP
    block_rows = 512
    slot_index = jnp.arange(SLOTS, dtype=jnp.int32)
    expert_index = jnp.arange(EXPERTS, dtype=jnp.int32)
    owner_slot = jnp.sum(jnp.where(old_place[None, :] == expert_index[:, None], slot_index[None, :], 0), axis=1).astype(jnp.int32)
    slot_ids = owner_slot[expert_ids].reshape(-1).astype(jnp.int32)
    gate_weights = (router_probs / jnp.sum(router_probs, axis=1, keepdims=True)).astype(jnp.bfloat16).reshape(-1)
    order = jnp.argsort(slot_ids * pair_count + jnp.arange(pair_count, dtype=jnp.int32)).astype(jnp.int32)
    counts = jnp.zeros((SLOTS,), jnp.int32).at[slot_ids].add(1)
    starts = (jnp.cumsum(counts) - counts).astype(jnp.int32)
    padded = jnp.concatenate([order, jnp.zeros((block_rows,), jnp.int32)])
    total = jnp.zeros((TOKENS, D), jnp.float32)

    def slot_step(slot, total):
        slot = jnp.asarray(slot).astype(jnp.int32)

        def block_step(block, total):
            block = jnp.asarray(block).astype(jnp.int32)
            begin = (starts[slot] + block * block_rows).astype(jnp.int32)
            pairs = lax.dynamic_slice_in_dim(padded, begin, block_rows)
            live = (jnp.arange(block_rows, dtype=jnp.int32) + block * block_rows) < counts[slot]
            token_rows = tokens[pairs // TOP]
            gate_part = jnp.dot(token_rows, w_gate[slot], preferred_element_type=jnp.float32)
            up_part = jnp.dot(token_rows, w_up[slot], preferred_element_type=jnp.float32)
            hidden = (jax.nn.silu(gate_part) * up_part).astype(jnp.bfloat16)
            result = lax.dot_general(hidden, w_down[slot], (((1,), (1,)), ((), ())), preferred_element_type=jnp.float32).astype(jnp.bfloat16)
            weight = jnp.where(live, gate_weights[pairs].astype(jnp.float32), jnp.float32(0.0))
            return total.at[pairs // TOP].add(result.astype(jnp.float32) * weight[:, None])

        block_total = ((counts[slot] + block_rows - 1) // block_rows).astype(jnp.int32)
        return lax.fori_loop(jnp.int32(0), block_total, block_step, total)

    total = lax.fori_loop(0, SLOTS, slot_step, total)
    moe_output = total.astype(jnp.bfloat16)
    source = owner_slot[new_place]
    return (moe_output, w_gate[source], w_up[source], w_down[source])
```

```python
import jax
import jax.numpy as jnp
from jax import lax
from jax.sharding import PartitionSpec as P


def swap(x, axis, bit):
    return lax.ppermute(x, axis, [(i, i ^ bit) for i in range(lax.axis_size(axis))])


def passed_along(x, axis, by):
    size = lax.axis_size(axis)
    return lax.ppermute(x, axis, [(i, (i + by) % size) for i in range(size)])


def in_order(second, own, other, axis=0):
    return jnp.where(
        second, jnp.stack([other, own], axis=axis), jnp.stack([own, other], axis=axis)
    )


def pick(w, index):
    return lax.dynamic_index_in_dim(w, index, 0, keepdims=False)


def local(tokens, router_probs, expert_ids, old_place, new_place, w_gate, w_up, w_down):
    slots = old_place.shape[0]
    tok, top = expert_ids.shape
    width = tokens.shape[1]
    ff = w_gate.shape[2]
    n_shard = lax.axis_size("shard")
    n_rows = lax.axis_size("dp")
    half = n_shard // 2
    column = lax.axis_index("shard")
    row_id = lax.axis_index("dp")
    side = column // half

    gate_weights = (router_probs / jnp.sum(router_probs, axis=1, keepdims=True)).astype(
        jnp.bfloat16
    )
    named = expert_ids[:, :, None] == old_place[None, None, :]
    coef = jnp.sum(jnp.where(named, gate_weights[:, :, None], jnp.zeros((), jnp.bfloat16)), axis=1)
    coef = jnp.pad(coef, ((0, 0), (0, 128 - slots)))
    own = jnp.concatenate([tokens, coef], axis=1)
    other = swap(own, "shard", half)
    both = in_order(side == 1, own, other).reshape(2 * tok, width + 128)
    every = lax.all_gather(both, "dp", axis=0, tiled=True)

    def slot_rows(w):
        mine, theirs = pick(w, side), pick(w, 1 - side)
        arrived = swap(theirs, "shard", half)
        rows = in_order(side == 1, mine, arrived)[:, None]
        bit = 1
        while bit < half:
            more = swap(rows, "shard", bit)
            rows = in_order((column & bit) != 0, rows, more, axis=1).reshape(
                (2, -1) + w.shape[1:]
            )
            bit *= 2
        return rows.reshape(-1, w.shape[2])

    full_gate = slot_rows(w_gate)
    full_up = slot_rows(w_up)
    down = w_down[:, None]
    bit = 1
    while bit < half:
        more = swap(down, "shard", bit)
        down = in_order((column & bit) != 0, down, more, axis=1).reshape(
            (2, -1) + w_down.shape[1:]
        )
        bit *= 2
    down = down.reshape(2, -1, ff)

    rows = every[:, :width]
    mine_coef = lax.dynamic_slice_in_dim(every, width + 2 * row_id + side, 1, 1)
    gate_part = jnp.dot(rows, full_gate, preferred_element_type=jnp.float32)
    up_part = jnp.dot(rows, full_up, preferred_element_type=jnp.float32)
    hidden = (jax.nn.silu(gate_part) * up_part * mine_coef.astype(jnp.float32)).astype(jnp.bfloat16)
    hidden_other = swap(hidden, "shard", half)
    contract = (((1,), (1,)), ((), ()))
    part = lax.dot_general(
        hidden, pick(down, side), contract, preferred_element_type=jnp.float32
    ) + lax.dot_general(
        hidden_other, pick(down, 1 - side), contract, preferred_element_type=jnp.float32
    )
    part = part.astype(jnp.bfloat16)
    total = lax.psum_scatter(part, "dp", scatter_dimension=0, tiled=True)
    total = total.reshape(2, tok, width // 2)
    kept = pick(total, side)
    arrived = swap(pick(total, 1 - side), "shard", half)
    moe_output = in_order(side == 1, kept, arrived, axis=1).reshape(tok, width)

    base_slot = 2 * row_id
    second_old = pick(old_place, base_slot + 1)
    second_new = pick(new_place, base_slot + 1)
    moved = (second_new != second_old).astype(jnp.int32)

    def refilled(w):
        arrive = passed_along(pick(w, moved), "dp", 1)
        return lax.dynamic_update_index_in_dim(w, arrive, moved, 0)

    return (moe_output, refilled(w_gate), refilled(w_up), refilled(w_down))


def solution(mesh):
    in_specs = (
        P(("dp", "shard"), None),
        P(("dp", "shard"), None),
        P(("dp", "shard"), None),
        P(),
        P(),
        P("dp", "shard", None),
        P("dp", "shard", None),
        P("dp", "shard", None),
    )
    out_specs = (
        P(("dp", "shard"), None),
        P("dp", "shard", None),
        P("dp", "shard", None),
        P("dp", "shard", None),
    )
    return jax.shard_map(local, mesh=mesh, in_specs=in_specs, out_specs=out_specs, check_vma=False)
```

```python
import functools

import jax
import jax.numpy as jnp
from jax import lax
from jax.experimental import pallas as pl
from jax.experimental.pallas import tpu as pltpu
from jax.sharding import PartitionSpec as P

LANES = 128
VMEM_BYTES = 40 * 1024 * 1024


def swap(x, axis, bit):
    return lax.ppermute(x, axis, [(i, i ^ bit) for i in range(lax.axis_size(axis))])


def passed_along(x, axis, by):
    size = lax.axis_size(axis)
    return lax.ppermute(x, axis, [(i, (i + by) % size) for i in range(size)])


def shift_z(x, by):
    size = lax.axis_size("dp")
    return lax.ppermute(x, "dp", [(i, (i + 2 * by) % size) for i in range(size)])


def in_order(second, own, other, axis=0):
    return jnp.where(
        second, jnp.stack([other, own], axis=axis), jnp.stack([own, other], axis=axis)
    )


def pick(w, index):
    return lax.dynamic_index_in_dim(w, index, 0, keepdims=False)


def spread(pieces, half):
    bit = 1
    while bit < half:
        pieces = pieces + [swap(p, "shard", bit) for p in pieces]
        bit *= 2
    return pieces


def params():
    return pltpu.CompilerParams(vmem_limit_bytes=VMEM_BYTES)


def prep_kernel(tokens_ref, probs_ref, ids_ref, place_ref, out_ref):
    probs = probs_ref[...]
    weights = (probs / jnp.sum(probs, axis=1, keepdims=True)).astype(jnp.bfloat16)
    weights = weights.astype(jnp.float32)
    ids = ids_ref[...]
    place = place_ref[...]
    coef = jnp.zeros((ids.shape[0], LANES), jnp.float32)
    for k in range(ids.shape[1]):
        coef += jnp.where(ids[:, k : k + 1] == place, weights[:, k : k + 1], 0.0)
    width = tokens_ref.shape[1]
    out_ref[:, :width] = tokens_ref[...]
    out_ref[:, width:] = coef.astype(jnp.bfloat16)


def prep(tokens, probs, ids, old_place):
    place = jnp.pad(old_place, (0, LANES - old_place.shape[0]), constant_values=-1)[None]
    return pl.pallas_call(
        prep_kernel,
        out_shape=jax.ShapeDtypeStruct((tokens.shape[0], tokens.shape[1] + LANES), tokens.dtype),
        compiler_params=params(),
    )(tokens, probs, ids, place)


def hidden_kernel(count, meta, a_ref, b_ref, *refs):
    gates, ups, out_ref = refs[:count], refs[count : 2 * count], refs[2 * count]
    depth = gates[0].shape[-2]
    width = a_ref.shape[1] - LANES
    rows = a_ref.shape[0] + b_ref.shape[0]
    block = out_ref.shape[1]
    gate = jnp.zeros((rows, block), jnp.float32)
    up = jnp.zeros((rows, block), jnp.float32)
    for i in range(count):
        columns = pl.ds(pl.multiple_of(meta[2 + i], LANES), depth)
        x = jnp.concatenate([a_ref[:, columns], b_ref[:, columns]], axis=0)
        gate += jnp.dot(x, gates[i][...].reshape(depth, block), preferred_element_type=jnp.float32)
        up += jnp.dot(x, ups[i][...].reshape(depth, block), preferred_element_type=jnp.float32)
    coef = jnp.concatenate([a_ref[:, width:], b_ref[:, width:]], axis=0).astype(jnp.float32)
    lane = lax.broadcasted_iota(jnp.int32, coef.shape, 1)
    coef = jnp.sum(jnp.where(lane == meta[1], coef, 0.0), axis=1, keepdims=True)
    out_ref[...] = (gate / (1.0 + jnp.exp(-gate)) * up * coef).astype(out_ref.dtype)


def hidden_of(meta, a, b, gates, ups):
    count = len(gates)
    depth, ff = gates[0].shape[-2:]
    block = 256
    rows = a.shape[0] + b.shape[0]

    def weight_spec(w):
        if w.ndim == 3:
            return pl.BlockSpec((1, depth, block), lambda f, m: (m[0], 0, f))
        return pl.BlockSpec((depth, block), lambda f, m: (0, f))

    def whole(x):
        return pl.BlockSpec(x.shape, lambda f, m: (0, 0))

    return pl.pallas_call(
        functools.partial(hidden_kernel, count),
        grid_spec=pltpu.PrefetchScalarGridSpec(
            num_scalar_prefetch=1,
            grid=(ff // block,),
            in_specs=[whole(a), whole(b)] + [weight_spec(w) for w in gates + ups],
            out_specs=pl.BlockSpec((rows, block), lambda f, m: (0, f)),
        ),
        out_shape=jax.ShapeDtypeStruct((rows, ff), a.dtype),
        compiler_params=params(),
        cost_estimate=pl.CostEstimate(
            flops=4 * rows * count * depth * ff,
            bytes_accessed=4 * count * depth * ff + 4 * rows * count * depth,
            transcendentals=rows * ff,
        ),
    )(meta, a, b, *gates, *ups)


def down_kernel(count, meta, own_ref, other_ref, *refs):
    downs, out_ref = refs[:count], refs[count]
    depth = downs[0].shape[1]
    contract = (((1,), (1,)), ((), ()))
    own, other = own_ref[...], other_ref[...]
    for i in range(count):
        part = lax.dot_general(
            own, downs[i][meta[0]], contract, preferred_element_type=jnp.float32
        ) + lax.dot_general(
            other, downs[i][1 - meta[0]], contract, preferred_element_type=jnp.float32
        )
        columns = pl.ds(pl.multiple_of(meta[1 + i], LANES), depth)
        out_ref[:, columns] = part.astype(out_ref.dtype)


def down_of(meta, own, other, downs):
    count = len(downs)
    depth, ff = downs[0].shape[-2:]
    rows = own.shape[0]
    vmem = pl.BlockSpec(memory_space=pltpu.VMEM)
    return pl.pallas_call(
        functools.partial(down_kernel, count),
        in_specs=[pl.BlockSpec(memory_space=pltpu.SMEM)] + [vmem] * (2 + count),
        out_specs=vmem,
        out_shape=jax.ShapeDtypeStruct((rows, count * depth), own.dtype),
        compiler_params=params(),
        cost_estimate=pl.CostEstimate(
            flops=4 * rows * count * depth * ff,
            bytes_accessed=4 * count * depth * ff + 4 * rows * ff + 2 * rows * count * depth,
            transcendentals=0,
        ),
    )(meta, own, other, *downs)


def local(tokens, router_probs, expert_ids, old_place, new_place, w_gate, w_up, w_down):
    tok = tokens.shape[0]
    width = tokens.shape[1]
    depth = w_gate.shape[1]
    n_shard = lax.axis_size("shard")
    half = n_shard // 2
    n_z = lax.axis_size("dp") // 2
    column = lax.axis_index("shard")
    row_id = lax.axis_index("dp")
    side = column // half
    place_in_side = column % half

    own = prep(tokens, router_probs, expert_ids, old_place)
    other = swap(own, "shard", half)
    both = in_order(side == 1, own, other).reshape(2 * tok, width + LANES)

    gate_arrived = swap(pick(w_gate, 1 - side), "shard", half)
    up_arrived = swap(pick(w_up, 1 - side), "shard", half)
    gate_mine, up_mine = pick(w_gate, side), pick(w_up, side)
    gates = spread([gate_mine], half) + spread([gate_arrived], half)
    ups = spread([up_mine], half) + spread([up_arrived], half)
    gates[0], ups[0] = w_gate, w_up
    downs = spread([w_down], half)

    same = [(place_in_side ^ j) * depth for j in range(half)]
    meta_hidden = jnp.stack(
        [side, 2 * row_id + side]
        + [side * half * depth + s for s in same]
        + [(1 - side) * half * depth + s for s in same]
    ).astype(jnp.int32)
    meta_down = jnp.stack([side] + same).astype(jnp.int32)

    columns = [both] + [shift_z(both, s) for s in range(1, n_z)]
    pairs = [(c, swap(c, "dp", 1)) for c in columns]

    total = None
    for s in list(range(1, n_z)) + [0]:
        hidden = hidden_of(meta_hidden, pairs[s][0], pairs[s][1], gates, ups)
        hidden_other = swap(hidden, "shard", half)
        part = down_of(meta_down, hidden, hidden_other, downs)
        if s:
            part = shift_z(part, -s)
        part = part.astype(jnp.float32)
        total = part if total is None else total + part
    total = total.reshape(2, 2 * tok, width // 2)
    given = swap(total[1].astype(jnp.bfloat16), "dp", 1)
    total = (total[0] + given.astype(jnp.float32)).astype(jnp.bfloat16)
    total = total.reshape(2, tok, width // 2)
    kept = pick(total, side)
    arrived = swap(pick(total, 1 - side), "shard", half)
    moe_output = in_order(side == 1, kept, arrived, axis=1).reshape(tok, width)

    base_slot = 2 * row_id
    second_old = pick(old_place, base_slot + 1)
    second_new = pick(new_place, base_slot + 1)
    moved = (second_new != second_old).astype(jnp.int32)

    def refilled(w):
        arrive = passed_along(pick(w, moved), "dp", 1)
        return lax.dynamic_update_index_in_dim(w, arrive, moved, 0)

    return (moe_output, refilled(w_gate), refilled(w_up), refilled(w_down))


def solution(mesh):
    in_specs = (
        P(("dp", "shard"), None),
        P(("dp", "shard"), None),
        P(("dp", "shard"), None),
        P(),
        P(),
        P("dp", "shard", None),
        P("dp", "shard", None),
        P("dp", "shard", None),
    )
    out_specs = (
        P(("dp", "shard"), None),
        P("dp", "shard", None),
        P("dp", "shard", None),
        P("dp", "shard", None),
    )
    return jax.shard_map(local, mesh=mesh, in_specs=in_specs, out_specs=out_specs, check_vma=False)
```

```python
import functools

import jax
import jax.numpy as jnp
from jax import lax
from jax.experimental import pallas as pl
from jax.experimental.pallas import tpu as pltpu
from jax.sharding import PartitionSpec as P

LANES = 128
VMEM_BYTES = 20 * 1024 * 1024
MOST = 56 * 1024 * 1024


def swap(x, axis, bit):
    return lax.ppermute(x, axis, [(i, i ^ bit) for i in range(lax.axis_size(axis))])


def passed_along(x, axis, by):
    size = lax.axis_size(axis)
    return lax.ppermute(x, axis, [(i, (i + by) % size) for i in range(size)])


def shift_z(x, by):
    size = lax.axis_size("dp")
    return lax.ppermute(x, "dp", [(i, (i + 2 * by) % size) for i in range(size)])


def in_order(second, own, other, axis=0):
    return jnp.where(
        second, jnp.stack([other, own], axis=axis), jnp.stack([own, other], axis=axis)
    )


def pick(w, index):
    return lax.dynamic_index_in_dim(w, index, 0, keepdims=False)


def spread(pieces, half):
    bit = 1
    while bit < half:
        pieces = pieces + [swap(p, "shard", bit) for p in pieces]
        bit *= 2
    return pieces


def params(amount=VMEM_BYTES):
    return pltpu.CompilerParams(vmem_limit_bytes=amount)


def first_kernel(
    meta, tokens_ref, probs_ref, ids_ref, place_ref, gate_ref, up_ref, out_ref, sent_ref, sems
):
    copies = [
        pltpu.make_async_copy(w.at[1 - meta[0]], sent_ref.at[i], sems.at[i])
        for i, w in enumerate((gate_ref, up_ref))
    ]
    for c in copies:
        c.start()
    probs = probs_ref[...]
    weights = (probs / jnp.sum(probs, axis=1, keepdims=True)).astype(jnp.bfloat16)
    weights = weights.astype(jnp.float32)
    ids = ids_ref[...]
    place = place_ref[...]
    coef = jnp.zeros((ids.shape[0], LANES), jnp.float32)
    for k in range(ids.shape[1]):
        coef += jnp.where(ids[:, k : k + 1] == place, weights[:, k : k + 1], 0.0)
    width = tokens_ref.shape[1]
    out_ref[:, :width] = tokens_ref[...]
    out_ref[:, width:] = coef.astype(jnp.bfloat16)
    for c in copies:
        c.wait()


def first(meta, tokens, probs, ids, old_place, w_gate, w_up):
    place = jnp.pad(old_place, (0, LANES - old_place.shape[0]), constant_values=-1)[None]
    vmem = pl.BlockSpec(memory_space=pltpu.VMEM)
    anywhere = pl.BlockSpec(memory_space=pltpu.HBM)
    return pl.pallas_call(
        first_kernel,
        in_specs=[pl.BlockSpec(memory_space=pltpu.SMEM)] + [vmem] * 4 + [anywhere] * 2,
        out_specs=(vmem, anywhere),
        out_shape=(
            jax.ShapeDtypeStruct((tokens.shape[0], tokens.shape[1] + LANES), tokens.dtype),
            jax.ShapeDtypeStruct((2,) + w_gate.shape[1:], w_gate.dtype),
        ),
        scratch_shapes=[pltpu.SemaphoreType.DMA((2,))],
        compiler_params=params(MOST),
    )(meta, tokens, probs, ids, place, w_gate, w_up)


def mine_kernel(meta, gate_ref, up_ref, mine_ref, sems):
    copies = [
        pltpu.make_async_copy(w.at[meta[0]], mine_ref.at[i], sems.at[i])
        for i, w in enumerate((gate_ref, up_ref))
    ]
    for c in copies:
        c.start()
    for c in copies:
        c.wait()


def mine_of(meta, w_gate, w_up):
    anywhere = pl.BlockSpec(memory_space=pltpu.HBM)
    return pl.pallas_call(
        mine_kernel,
        in_specs=[pl.BlockSpec(memory_space=pltpu.SMEM)] + [anywhere] * 2,
        out_specs=anywhere,
        out_shape=jax.ShapeDtypeStruct((2,) + w_gate.shape[1:], w_gate.dtype),
        scratch_shapes=[pltpu.SemaphoreType.DMA((2,))],
        compiler_params=params(MOST),
    )(meta, w_gate, w_up)


def leave_kernel(meta, gate_ref, up_ref, down_ref, after_ref, leave_ref, *refs):
    news, sems = refs[:3], refs[3]
    copies = []
    for i, w in enumerate((gate_ref, up_ref, down_ref)):
        copies.append((w.at[meta[1]], leave_ref.at[i]))
        copies.append((w.at[1 - meta[1]], news[i].at[1 - meta[1]]))
    copies = [pltpu.make_async_copy(a, b, sems.at[i]) for i, (a, b) in enumerate(copies)]
    for c in copies:
        c.start()
    for c in copies:
        c.wait()


def leave_of(meta, w_gate, w_up, w_down, after):
    anywhere = pl.BlockSpec(memory_space=pltpu.HBM)
    slot = w_gate.shape[1:]
    return pl.pallas_call(
        leave_kernel,
        in_specs=[pl.BlockSpec(memory_space=pltpu.SMEM)] + [anywhere] * 4,
        out_specs=(anywhere,) * 4,
        out_shape=(jax.ShapeDtypeStruct((3,) + slot, w_gate.dtype),)
        + (jax.ShapeDtypeStruct((2,) + slot, w_gate.dtype),) * 3,
        scratch_shapes=[pltpu.SemaphoreType.DMA((6,))],
        compiler_params=params(MOST),
    )(meta, w_gate, w_up, w_down, after)


def join_kernel(*refs):
    pass


def joined(x, after):
    anywhere = pl.BlockSpec(memory_space=pltpu.HBM)
    return pl.pallas_call(
        join_kernel,
        in_specs=[anywhere] * (1 + len(after)),
        out_specs=anywhere,
        out_shape=jax.ShapeDtypeStruct(x.shape, x.dtype),
        input_output_aliases={0: 0},
        compiler_params=params(),
    )(x, *after)


def refill_kernel(meta, arrive_ref, *refs):
    news, sems = refs[3:6], refs[6]
    copies = [
        pltpu.make_async_copy(arrive_ref.at[i], news[i].at[meta[1]], sems.at[i]) for i in range(3)
    ]
    for c in copies:
        c.start()
    for c in copies:
        c.wait()


def refill(meta, arrive, news):
    anywhere = pl.BlockSpec(memory_space=pltpu.HBM)
    return pl.pallas_call(
        refill_kernel,
        in_specs=[pl.BlockSpec(memory_space=pltpu.SMEM)] + [anywhere] * 4,
        out_specs=(anywhere,) * 3,
        out_shape=tuple(jax.ShapeDtypeStruct(w.shape, w.dtype) for w in news),
        input_output_aliases={2: 0, 3: 1, 4: 2},
        scratch_shapes=[pltpu.SemaphoreType.DMA((3,))],
        compiler_params=params(MOST),
    )(meta, arrive, *news)


def hidden_kernel(meta, a_ref, b_ref, mine_ref, *refs):
    others, out_ref = refs[:-1], refs[-1]
    half, _, depth, block = mine_ref.shape
    width = a_ref.shape[1] - LANES
    rows = a_ref.shape[0] + b_ref.shape[0]
    gate = jnp.zeros((rows, block), jnp.float32)
    up = jnp.zeros((rows, block), jnp.float32)
    for i in range(2 * half):
        columns = pl.ds(pl.multiple_of(meta[2 + i], LANES), depth)
        x = jnp.concatenate([a_ref[:, columns], b_ref[:, columns]], axis=0)
        w = mine_ref.at[i] if i < half else others[i - half]
        gate += jnp.dot(x, w[0], preferred_element_type=jnp.float32)
        up += jnp.dot(x, w[1], preferred_element_type=jnp.float32)
    coef = jnp.concatenate([a_ref[:, width:], b_ref[:, width:]], axis=0).astype(jnp.float32)
    lane = lax.broadcasted_iota(jnp.int32, coef.shape, 1)
    coef = jnp.sum(jnp.where(lane == meta[1], coef, 0.0), axis=1, keepdims=True)
    out_ref[...] = (gate / (1.0 + jnp.exp(-gate)) * up * coef).astype(out_ref.dtype)


def hidden_of(meta, a, b, mine, others):
    half, _, depth, ff = mine.shape
    block = 256
    rows = a.shape[0] + b.shape[0]

    def whole(x):
        return pl.BlockSpec(x.shape, lambda f, m: (0, 0))

    own = pl.BlockSpec((half, 2, depth, block), lambda f, m: (0, 0, 0, f))
    other = pl.BlockSpec((2, depth, block), lambda f, m: (0, 0, f))
    return pl.pallas_call(
        hidden_kernel,
        grid_spec=pltpu.PrefetchScalarGridSpec(
            num_scalar_prefetch=1,
            grid=(ff // block,),
            in_specs=[whole(a), whole(b), own] + [other] * half,
            out_specs=pl.BlockSpec((rows, block), lambda f, m: (0, f)),
        ),
        out_shape=jax.ShapeDtypeStruct((rows, ff), a.dtype),
        compiler_params=params(),
        cost_estimate=pl.CostEstimate(flops=0, bytes_accessed=0, transcendentals=0),
    )(meta, a, b, mine, *others)


def down_kernel(meta, own_ref, other_ref, downs_ref, out_ref):
    half, _, depth, _ = downs_ref.shape
    contract = (((1,), (1,)), ((), ()))
    own, other = own_ref[...], other_ref[...]
    for i in range(half):
        part = lax.dot_general(
            own, downs_ref[i, meta[0]], contract, preferred_element_type=jnp.float32
        ) + lax.dot_general(
            other, downs_ref[i, 1 - meta[0]], contract, preferred_element_type=jnp.float32
        )
        out_ref[:, i * depth : (i + 1) * depth] = part.astype(out_ref.dtype)


def down_of(meta, own, other, downs):
    half, _, depth, ff = downs.shape
    rows = own.shape[0]
    vmem = pl.BlockSpec(memory_space=pltpu.VMEM)
    return pl.pallas_call(
        down_kernel,
        in_specs=[pl.BlockSpec(memory_space=pltpu.SMEM)] + [vmem] * 3,
        out_specs=vmem,
        out_shape=jax.ShapeDtypeStruct((rows, half * depth), own.dtype),
        compiler_params=params(),
        cost_estimate=pl.CostEstimate(flops=0, bytes_accessed=0, transcendentals=0),
    )(meta, own, other, downs)


def local(tokens, router_probs, expert_ids, old_place, new_place, w_gate, w_up, w_down):
    tok = tokens.shape[0]
    width = tokens.shape[1]
    depth = w_gate.shape[1]
    n_shard = lax.axis_size("shard")
    half = n_shard // 2
    n_z = lax.axis_size("dp") // 2
    column = lax.axis_index("shard")
    row_id = lax.axis_index("dp")
    side = column // half
    place_in_side = column % half

    base_slot = 2 * row_id
    moved = (pick(old_place, base_slot + 1) != pick(new_place, base_slot + 1)).astype(jnp.int32)
    groups = [[g * half + j for j in range(half)] for g in range(2)]
    flipped = [(place_in_side ^ j) * depth for j in range(half)]
    straight = [jnp.int32(j * depth) for j in range(half)]
    meta_copy = jnp.stack([side, moved]).astype(jnp.int32)
    meta_hidden = jnp.stack(
        [side, base_slot + side]
        + [side * half * depth + s for s in straight]
        + [(1 - side) * half * depth + s for s in flipped]
    ).astype(jnp.int32)
    meta_down = side.reshape(1).astype(jnp.int32)

    own, sent = first(meta_copy, tokens, router_probs, expert_ids, old_place, w_gate, w_up)
    other = swap(own, "shard", half)
    both = in_order(side == 1, own, other).reshape(2 * tok, width + LANES)
    columns = [both] + [shift_z(both, s) for s in range(1, n_z)]
    pairs = [(c, swap(c, "dp", 1)) for c in columns]

    mine = mine_of(meta_copy, w_gate, w_up)
    mine = lax.all_gather(mine, "shard", axis_index_groups=groups)
    downs = lax.all_gather(w_down, "shard", axis_index_groups=groups)
    arrived = joined(swap(sent, "shard", half), columns[2:] + [pairs[0][1], pairs[1][1]])
    others = spread([arrived], half)
    leave, *news = leave_of(meta_copy, w_gate, w_up, w_down, other)

    total = None
    for s in list(range(1, n_z)) + [0]:
        hidden = hidden_of(meta_hidden, pairs[s][0], pairs[s][1], mine, others)
        hidden_other = swap(hidden, "shard", half)
        part = down_of(meta_down, hidden, hidden_other, downs)
        if s:
            part = shift_z(part, -s)
        part = part.astype(jnp.float32)
        total = part if total is None else total + part
    total = total.reshape(2, 2 * tok, width // 2)
    given = swap(total[1].astype(jnp.bfloat16), "dp", 1)
    total = (total[0] + given.astype(jnp.float32)).astype(jnp.bfloat16)
    total = total.reshape(2, tok, width // 2)
    kept = pick(total, side)
    arrived = swap(pick(total, 1 - side), "shard", half)
    moe_output = in_order(side == 1, kept, arrived, axis=1).reshape(tok, width)

    new_gate, new_up, new_down = refill(meta_copy, passed_along(leave, "dp", 1), news)
    return (moe_output, new_gate, new_up, new_down)


def solution(mesh):
    in_specs = (
        P(("dp", "shard"), None),
        P(("dp", "shard"), None),
        P(("dp", "shard"), None),
        P(),
        P(),
        P("dp", "shard", None),
        P("dp", "shard", None),
        P("dp", "shard", None),
    )
    out_specs = (
        P(("dp", "shard"), None),
        P("dp", "shard", None),
        P("dp", "shard", None),
        P("dp", "shard", None),
    )
    return jax.shard_map(local, mesh=mesh, in_specs=in_specs, out_specs=out_specs, check_vma=False)
```

```python
import functools

import jax
import jax.numpy as jnp
from jax import lax
from jax.experimental import pallas as pl
from jax.experimental.pallas import tpu as pltpu
from jax.sharding import PartitionSpec as P

LANES = 128
GROUP = 2
VMEM_BYTES = 20 * 1024 * 1024
MOST = 56 * 1024 * 1024
NOTHING = pl.CostEstimate(flops=0, bytes_accessed=0, transcendentals=0)


def swap(x, axis, bit):
    return lax.ppermute(x, axis, [(i, i ^ bit) for i in range(lax.axis_size(axis))])


def passed_along(x, axis, by):
    size = lax.axis_size(axis)
    return lax.ppermute(x, axis, [(i, (i + by) % size) for i in range(size)])


def shift_z(x, by):
    size = lax.axis_size("dp")
    return lax.ppermute(x, "dp", [(i, (i + 2 * by) % size) for i in range(size)])


def in_order(second, own, other, axis=0):
    return jnp.where(
        second, jnp.stack([other, own], axis=axis), jnp.stack([own, other], axis=axis)
    )


def spread(pieces, half):
    bit = 1
    while bit < half:
        pieces = pieces + [swap(p, "shard", bit) for p in pieces]
        bit *= 2
    return pieces


def params(amount=VMEM_BYTES):
    return pltpu.CompilerParams(vmem_limit_bytes=amount)


def position():
    half = lax.axis_size("shard") // 2
    column = lax.axis_index("shard")
    return lax.div(column, half), lax.rem(column, half), lax.axis_index("dp")


def first_kernel(tokens_ref, probs_ref, ids_ref, place_ref, out_ref, coef_ref):
    probs = probs_ref[...]
    weights = (probs / jnp.sum(probs, axis=0, keepdims=True)).astype(jnp.bfloat16)
    weights = weights.astype(jnp.float32)
    ids = ids_ref[...]
    tok, width = tokens_ref.shape
    coef_ref[...] = jnp.zeros_like(coef_ref)
    for slot in range(place_ref.shape[0]):
        named = jnp.where(ids == place_ref[slot], weights, 0.0)
        coef_ref[slot : slot + 1, :tok] = jnp.sum(named, axis=0, keepdims=True)
    out_ref[:, :width] = tokens_ref[...]
    out_ref[:, width:] = jnp.transpose(coef_ref[...])[:tok].astype(jnp.bfloat16)


def first(tokens, probs, ids, old_place):
    vmem = pl.BlockSpec(memory_space=pltpu.VMEM)
    return pl.pallas_call(
        first_kernel,
        in_specs=[vmem] * 3 + [pl.BlockSpec(memory_space=pltpu.SMEM)],
        out_specs=vmem,
        out_shape=jax.ShapeDtypeStruct((tokens.shape[0], tokens.shape[1] + LANES), tokens.dtype),
        scratch_shapes=[pltpu.VMEM((LANES, LANES), jnp.float32)],
        compiler_params=params(),
        cost_estimate=NOTHING,
    )(tokens, probs.T, ids.T, old_place)


def copy_kernel(plan, n_in, n_out, *refs):
    old_ref, new_ref = refs[:2]
    ins, refs = refs[2 : 2 + n_in], refs[-n_out - 3 :]
    outs, (held, in_sems, out_sems) = refs[:n_out], refs[n_out:]
    side, _, row = position()
    second = 2 * row + 1
    moved = (old_ref[second] != new_ref[second]).astype(jnp.int32)
    slots = {"mine": side, "theirs": 1 - side, "leaves": moved, "stays": 1 - moved}
    slots.update({i: i for i in range(3)})
    loads = [
        pltpu.make_async_copy(ins[i].at[slots[a]], held.at[n], in_sems.at[n])
        for n, (i, a, o, b) in enumerate(plan)
    ]
    stores = [
        pltpu.make_async_copy(held.at[n], outs[o].at[slots[b]], out_sems.at[n])
        for n, (i, a, o, b) in enumerate(plan)
    ]
    for c in loads:
        c.start()
    for n, c in enumerate(stores):
        loads[n].wait()
        c.start()
    for c in stores:
        c.wait()


def copies(plan, places, ins, counts, after=(), aliases=()):
    slot, kind = ins[0].shape[1:], ins[0].dtype
    smem, anywhere = pl.BlockSpec(memory_space=pltpu.SMEM), pl.BlockSpec(memory_space=pl.ANY)
    return pl.pallas_call(
        functools.partial(copy_kernel, plan, len(ins), len(counts)),
        in_specs=[smem] * 2 + [anywhere] * (len(ins) + len(aliases) + len(after)),
        out_specs=(anywhere,) * len(counts),
        out_shape=tuple(jax.ShapeDtypeStruct((n,) + slot, kind) for n in counts),
        input_output_aliases={2 + len(ins) + i: i for i in range(len(aliases))},
        scratch_shapes=[
            pltpu.VMEM((len(plan),) + slot, kind),
            pltpu.SemaphoreType.DMA((len(plan),)),
            pltpu.SemaphoreType.DMA((len(plan),)),
        ],
        compiler_params=params(MOST),
        cost_estimate=NOTHING,
    )(*places, *ins, *aliases, *after)


def join_kernel(*refs):
    pass


def joined(x, after):
    anywhere = pl.BlockSpec(memory_space=pl.ANY)
    return pl.pallas_call(
        join_kernel,
        in_specs=[anywhere] * (1 + len(after)),
        out_specs=anywhere,
        out_shape=jax.ShapeDtypeStruct(x.shape, x.dtype),
        input_output_aliases={0: 0},
        compiler_params=params(),
    )(x, *after)


def refill_kernel(meta, arrive_ref, *refs):
    news, sems = refs[3:6], refs[6]
    copies = [
        pltpu.make_async_copy(arrive_ref.at[i], news[i].at[meta[1]], sems.at[i]) for i in range(3)
    ]
    for c in copies:
        c.start()
    for c in copies:
        c.wait()


def refill(meta, arrive, news):
    anywhere = pl.BlockSpec(memory_space=pl.ANY)
    return pl.pallas_call(
        refill_kernel,
        in_specs=[pl.BlockSpec(memory_space=pltpu.SMEM)] + [anywhere] * 4,
        out_specs=(anywhere,) * 3,
        out_shape=tuple(jax.ShapeDtypeStruct(w.shape, w.dtype) for w in news),
        input_output_aliases={2: 0, 3: 1, 4: 2},
        scratch_shapes=[pltpu.SemaphoreType.DMA((3,))],
        compiler_params=params(MOST),
    )(meta, arrive, *news)


def hidden_kernel(n_pieces, *refs):
    pieces, mine_ref, others, out_ref = (
        refs[:n_pieces], refs[n_pieces], refs[n_pieces + 1 : -1], refs[-1],
    )
    half, _, depth, block = mine_ref.shape
    width = pieces[0].shape[1] - LANES
    rows = out_ref.shape[0]
    gate = jnp.zeros((rows, block), jnp.float32)
    up = jnp.zeros((rows, block), jnp.float32)
    side, place, row = position()
    for i in range(2 * half):
        if i < half:
            start = (side * half + i) * depth
        else:
            start = ((1 - side) * half + (place ^ (i - half))) * depth
        columns = pl.ds(pl.multiple_of(start, LANES), depth)
        x = jnp.concatenate([p[:, columns] for p in pieces], axis=0)
        w = mine_ref.at[i] if i < half else others[i - half]
        gate += jnp.dot(x, w[0], preferred_element_type=jnp.float32)
        up += jnp.dot(x, w[1], preferred_element_type=jnp.float32)
    coef = jnp.concatenate([p[:, width:] for p in pieces], axis=0).astype(jnp.float32)
    lane = lax.broadcasted_iota(jnp.int32, coef.shape, 1)
    coef = jnp.sum(jnp.where(lane == 2 * row + side, coef, 0.0), axis=1, keepdims=True)
    out_ref[...] = (gate / (1.0 + jnp.exp(-gate)) * up * coef).astype(out_ref.dtype)


def hidden_of(pieces, mine, others):
    half, _, depth, ff = mine.shape
    block = 256
    rows = sum(p.shape[0] for p in pieces)
    piece = pl.BlockSpec(pieces[0].shape, lambda f: (0, 0))
    own = pl.BlockSpec((half, 2, depth, block), lambda f: (0, 0, 0, f))
    other = pl.BlockSpec((2, depth, block), lambda f: (0, 0, f))
    return pl.pallas_call(
        functools.partial(hidden_kernel, len(pieces)),
        grid=(ff // block,),
        in_specs=[piece] * len(pieces) + [own] + [other] * half,
        out_specs=pl.BlockSpec((rows, block), lambda f: (0, f)),
        out_shape=jax.ShapeDtypeStruct((rows, ff), pieces[0].dtype),
        compiler_params=params(),
        cost_estimate=NOTHING,
    )(*pieces, mine, *others)


def down_kernel(own_ref, other_ref, downs_ref, *outs):
    half, _, depth, _ = downs_ref.shape
    contract = (((1,), (1,)), ((), ()))
    own, other = own_ref[...], other_ref[...]
    side = position()[0]
    rows = outs[0].shape[0]
    for i in range(half):
        part = lax.dot_general(
            own, downs_ref[i, side], contract, preferred_element_type=jnp.float32
        ) + lax.dot_general(
            other, downs_ref[i, 1 - side], contract, preferred_element_type=jnp.float32
        )
        part = part.astype(outs[0].dtype)
        for n, out in enumerate(outs):
            out[:, i * depth : (i + 1) * depth] = part[n * rows : (n + 1) * rows]


def down_of(own, other, downs):
    half, _, depth, ff = downs.shape
    rows = own.shape[0] // GROUP
    vmem = pl.BlockSpec(memory_space=pltpu.VMEM)
    return pl.pallas_call(
        down_kernel,
        in_specs=[vmem] * 3,
        out_specs=(vmem,) * GROUP,
        out_shape=(jax.ShapeDtypeStruct((rows, half * depth), own.dtype),) * GROUP,
        compiler_params=params(),
        cost_estimate=NOTHING,
    )(own, other, downs)


def local(tokens, router_probs, expert_ids, old_place, new_place, w_gate, w_up, w_down):
    tok, width = tokens.shape
    half = lax.axis_size("shard") // 2
    n_z = lax.axis_size("dp") // 2
    side = lax.axis_index("shard") // half
    groups = [[g * half + j for j in range(half)] for g in range(2)]
    places = (old_place, new_place)

    own = first(tokens, router_probs, expert_ids, old_place)
    sent, leave_gate = copies(
        ((0, "theirs", 0, 0), (1, "theirs", 0, 1), (0, "leaves", 1, 0)),
        places, (w_gate, w_up), (2, 1), (own,),
    )
    other = swap(own, "shard", half)
    both = in_order(side == 1, own, other).reshape(2 * tok, width + LANES)
    columns = [both] + [shift_z(both, s) for s in range(1, n_z)]
    arrive_gate = passed_along(leave_gate, "dp", 1)
    pairs = [(c, swap(joined(c, [arrive_gate]) if i == 0 else c, "dp", 1))
             for i, c in enumerate(columns)]

    (mine,) = copies(((0, "mine", 0, 0), (1, "mine", 0, 1)), places, (w_gate, w_up), (2,), (own,))
    mine = lax.all_gather(mine, "shard", axis_index_groups=groups)
    downs = lax.all_gather(w_down, "shard", axis_index_groups=groups)
    arrived = joined(
        swap(joined(sent, [other]), "shard", half), columns[2:] + [p[1] for p in pairs[:3]]
    )
    others = spread([arrived], half)

    leave, *news = copies(
        tuple((i, "leaves", 0, i - 1) for i in (1, 2))
        + tuple((i, "stays", i + 1, "stays") for i in range(3)),
        places, (w_gate, w_up, w_down), (2, 2, 2, 2), (pairs[-1][1],),
    )
    arrive = (arrive_gate, passed_along(leave, "dp", 1))

    total = None
    order = list(range(1, n_z)) + [0]
    groups = [order[i : i + GROUP] for i in range(0, n_z, GROUP)]
    hiddens = [hidden_of([p for s in g for p in pairs[s]], mine, others) for g in groups]
    for g, hidden in zip(groups, hiddens):
        parts = down_of(hidden, swap(hidden, "shard", half), downs)
        for s, part in zip(g, parts):
            part = (shift_z(part, -s) if s else part).astype(jnp.float32)
            total = part if total is None else total + part
    total = total.reshape(2, 2 * tok, width // 2)
    given = swap(total[1].astype(jnp.bfloat16), "dp", 1)
    total = (total[0] + given.astype(jnp.float32)).astype(jnp.bfloat16)
    total = total.reshape(2, tok, width // 2)
    kept = jnp.where(side == 1, total[1], total[0])
    arrived = swap(jnp.where(side == 1, total[0], total[1]), "shard", half)
    moe_output = in_order(side == 1, kept, arrived, axis=1).reshape(tok, width)

    news = copies(
        ((0, 0, 0, "leaves"), (1, 0, 1, "leaves"), (1, 1, 2, "leaves")),
        places, arrive, (2, 2, 2), (), news,
    )
    return (moe_output, *news)


def solution(mesh):
    in_specs = (
        P(("dp", "shard"), None),
        P(("dp", "shard"), None),
        P(("dp", "shard"), None),
        P(),
        P(),
        P("dp", "shard", None),
        P("dp", "shard", None),
        P("dp", "shard", None),
    )
    out_specs = (
        P(("dp", "shard"), None),
        P("dp", "shard", None),
        P("dp", "shard", None),
        P("dp", "shard", None),
    )
    return jax.shard_map(local, mesh=mesh, in_specs=in_specs, out_specs=out_specs, check_vma=False)
```

```python
import functools

import jax
import jax.numpy as jnp
from jax import lax
from jax.experimental import pallas as pl
from jax.experimental.pallas import tpu as pltpu
from jax.sharding import PartitionSpec as P

LANES = 128
VMEM_BYTES = 32 * 1024 * 1024
MOST = 56 * 1024 * 1024
NOTHING = pl.CostEstimate(flops=0, bytes_accessed=0, transcendentals=0)


def swap(x, axis, bit):
    return lax.ppermute(x, axis, [(i, i ^ bit) for i in range(lax.axis_size(axis))])


def passed_along(x, axis, by):
    size = lax.axis_size(axis)
    return lax.ppermute(x, axis, [(i, (i + by) % size) for i in range(size)])


def shift_z(x, by):
    size = lax.axis_size("dp")
    return lax.ppermute(x, "dp", [(i, (i + 2 * by) % size) for i in range(size)])


def spread(pieces):
    bit = 2
    while bit < lax.axis_size("shard"):
        pieces = pieces + [swap(p, "shard", bit) for p in pieces]
        bit *= 2
    return pieces


def params(amount=VMEM_BYTES):
    return pltpu.CompilerParams(vmem_limit_bytes=amount)


def position():
    column = lax.axis_index("shard")
    return lax.div(column, 2), lax.rem(column, 2), lax.axis_index("dp")


def first_kernel(tokens_ref, probs_ref, ids_ref, place_ref, out_ref, coef_ref):
    probs = probs_ref[...]
    weights = (probs / jnp.sum(probs, axis=0, keepdims=True)).astype(jnp.bfloat16)
    weights = weights.astype(jnp.float32)
    ids = ids_ref[...]
    tok, width = tokens_ref.shape
    coef_ref[...] = jnp.zeros_like(coef_ref)
    for slot in range(place_ref.shape[0]):
        named = jnp.where(ids == place_ref[slot], weights, 0.0)
        coef_ref[slot : slot + 1, :tok] = jnp.sum(named, axis=0, keepdims=True)
    out_ref[:, :width] = tokens_ref[...]
    out_ref[:, width:] = jnp.transpose(coef_ref[...])[:tok].astype(jnp.bfloat16)


def first(tokens, probs, ids, old_place):
    vmem = pl.BlockSpec(memory_space=pltpu.VMEM)
    return pl.pallas_call(
        first_kernel,
        in_specs=[vmem] * 3 + [pl.BlockSpec(memory_space=pltpu.SMEM)],
        out_specs=vmem,
        out_shape=jax.ShapeDtypeStruct((tokens.shape[0], tokens.shape[1] + LANES), tokens.dtype),
        scratch_shapes=[pltpu.VMEM((LANES, LANES), jnp.float32)],
        compiler_params=params(),
        cost_estimate=NOTHING,
    )(tokens, probs.T, ids.T, old_place)


def copy_kernel(plan, n_in, n_out, *refs):
    old_ref, new_ref = refs[:2]
    ins, refs = refs[2 : 2 + n_in], refs[-n_out - 3 :]
    outs, (held, in_sems, out_sems) = refs[:n_out], refs[n_out:]
    _, core, row = position()
    second = 2 * row + 1
    moved = (old_ref[second] != new_ref[second]).astype(jnp.int32)
    slots = {"mine": core, "theirs": 1 - core, "leaves": moved, "stays": 1 - moved}
    slots.update({i: i for i in range(3)})
    loads = [
        pltpu.make_async_copy(ins[i].at[slots[a]], held.at[n], in_sems.at[n])
        for n, (i, a, o, b) in enumerate(plan)
    ]
    stores = [
        pltpu.make_async_copy(held.at[n], outs[o].at[slots[b]], out_sems.at[n])
        for n, (i, a, o, b) in enumerate(plan)
    ]
    for c in loads:
        c.start()
    for n, c in enumerate(stores):
        loads[n].wait()
        c.start()
    for c in stores:
        c.wait()


def copies(plan, places, ins, counts, after=(), aliases=()):
    slot, kind = ins[0].shape[1:], ins[0].dtype
    smem, anywhere = pl.BlockSpec(memory_space=pltpu.SMEM), pl.BlockSpec(memory_space=pl.ANY)
    return pl.pallas_call(
        functools.partial(copy_kernel, plan, len(ins), len(counts)),
        in_specs=[smem] * 2 + [anywhere] * (len(ins) + len(aliases) + len(after)),
        out_specs=(anywhere,) * len(counts),
        out_shape=tuple(jax.ShapeDtypeStruct((n,) + slot, kind) for n in counts),
        input_output_aliases={2 + len(ins) + i: i for i in range(len(aliases))},
        scratch_shapes=[
            pltpu.VMEM((len(plan),) + slot, kind),
            pltpu.SemaphoreType.DMA((len(plan),)),
            pltpu.SemaphoreType.DMA((len(plan),)),
        ],
        compiler_params=params(MOST),
        cost_estimate=NOTHING,
    )(*places, *ins, *aliases, *after)


def order_kernel(mine_ref, other_ref, first_ref, second_ref, held, in_sems, out_sems):
    _, core, _ = position()
    loads = [
        pltpu.make_async_copy(mine_ref.at[core], held.at[core], in_sems.at[0]),
        pltpu.make_async_copy(other_ref.at[0], held.at[1 - core], in_sems.at[1]),
    ]
    stores = [
        pltpu.make_async_copy(held.at[n], out, out_sems.at[n])
        for n, out in enumerate((first_ref, second_ref))
    ]
    for c in loads:
        c.start()
    for c in loads:
        c.wait()
    for c in stores:
        c.start()
    for c in stores:
        c.wait()


def in_order(w_down, other):
    anywhere = pl.BlockSpec(memory_space=pl.ANY)
    slot = w_down.shape[1:]
    return pl.pallas_call(
        order_kernel,
        in_specs=[anywhere] * 2,
        out_specs=(anywhere,) * 2,
        out_shape=(jax.ShapeDtypeStruct(slot, w_down.dtype),) * 2,
        scratch_shapes=[
            pltpu.VMEM((2,) + slot, w_down.dtype),
            pltpu.SemaphoreType.DMA((2,)),
            pltpu.SemaphoreType.DMA((2,)),
        ],
        compiler_params=params(MOST),
        cost_estimate=NOTHING,
    )(w_down, other)


def join_kernel(*refs):
    pass


def joined(x, *after):
    anywhere = pl.BlockSpec(memory_space=pl.ANY)
    return pl.pallas_call(
        join_kernel,
        in_specs=[anywhere] * (1 + len(after)),
        out_specs=anywhere,
        out_shape=jax.ShapeDtypeStruct(x.shape, x.dtype),
        input_output_aliases={0: 0},
        compiler_params=params(),
        cost_estimate=NOTHING,
    )(x, *after)


def hidden_kernel(n_pieces, *refs):
    pieces, weights, (out_ref, x_ref, coef_ref) = refs[:n_pieces], refs[n_pieces:-3], refs[-3:]
    _, depth, block = weights[0].shape
    rows, width = x_ref.shape
    tall = rows // n_pieces
    pair, core, row = position()

    @pl.when(pl.program_id(0) == 0)
    def _():
        for n, p in enumerate(pieces):
            x_ref[n * tall : (n + 1) * tall] = p[:, :width]
            coef = p[:, width:].astype(jnp.float32)
            lane = lax.broadcasted_iota(jnp.int32, coef.shape, 1)
            coef = jnp.sum(jnp.where(lane == 2 * row + core, coef, 0.0), axis=1, keepdims=True)
            coef_ref[n * tall : (n + 1) * tall] = jnp.broadcast_to(coef, (tall, LANES))

    tile = min(rows, 512)
    for top in range(0, rows, tile):
        gate = jnp.zeros((tile, block), jnp.float32)
        up = jnp.zeros((tile, block), jnp.float32)
        for i, w in enumerate(weights):
            start = (2 * (pair ^ (i // 2)) + (core ^ (i % 2))) * depth
            x = x_ref[top : top + tile, pl.ds(pl.multiple_of(start, LANES), depth)]
            gate += jnp.dot(x, w[0], preferred_element_type=jnp.float32)
            up += jnp.dot(x, w[1], preferred_element_type=jnp.float32)
        coef = coef_ref[top : top + tile, :1]
        hidden = gate / (1.0 + jnp.exp(-gate)) * up * coef
        out_ref[top : top + tile] = hidden.astype(out_ref.dtype)


def hidden_of(pieces, weights):
    _, depth, ff = weights[0].shape
    block = 256
    tall, wide = pieces[0].shape
    rows = tall * len(pieces)
    return pl.pallas_call(
        functools.partial(hidden_kernel, len(pieces)),
        grid=(ff // block,),
        in_specs=[pl.BlockSpec((tall, wide), lambda f: (0, 0))] * len(pieces)
        + [pl.BlockSpec((2, depth, block), lambda f: (0, 0, f))] * len(weights),
        out_specs=pl.BlockSpec((rows, block), lambda f: (0, f)),
        out_shape=jax.ShapeDtypeStruct((rows, ff), pieces[0].dtype),
        scratch_shapes=[
            pltpu.VMEM((rows, wide - LANES), pieces[0].dtype),
            pltpu.VMEM((rows, LANES), jnp.float32),
        ],
        compiler_params=params(),
        cost_estimate=NOTHING,
    )(*pieces, *weights)


def down_kernel(n_downs, hidden_ref, *refs):
    downs, (kept_ref, sent_ref) = refs[:n_downs], refs[-2:]
    depth = downs[0].shape[0]
    rows = kept_ref.shape[0]
    tile = min(rows, 512)
    contract = (((1,), (1,)), ((), ()))
    for i, w in enumerate(downs):
        for out, base in ((kept_ref, 0), (sent_ref, rows)):
            for top in range(0, rows, tile):
                part = lax.dot_general(
                    hidden_ref[base + top : base + top + tile], w[...], contract,
                    preferred_element_type=jnp.float32,
                )
                out[top : top + tile, i * depth : (i + 1) * depth] = part.astype(out.dtype)


def down_of(hidden, downs, after):
    depth, ff = downs[0].shape
    rows = hidden.shape[0] // 2
    vmem = pl.BlockSpec(memory_space=pltpu.VMEM)
    out = jax.ShapeDtypeStruct((rows, len(downs) * depth), hidden.dtype)
    return pl.pallas_call(
        functools.partial(down_kernel, len(downs)),
        in_specs=[vmem] * (1 + len(downs)) + [pl.BlockSpec(memory_space=pl.ANY)] * len(after),
        out_specs=(vmem, vmem),
        out_shape=(out, out),
        compiler_params=params(),
        cost_estimate=NOTHING,
    )(hidden, *downs, *after)


def over_core(kept, sent):
    return kept.astype(jnp.float32) + swap(sent, "shard", 1).astype(jnp.float32)


def over_x(total, tok):
    total = total.reshape(-1, 2, tok, total.shape[-1])
    given = swap(total[:, 1].astype(jnp.bfloat16), "dp", 1)
    return total[:, 0] + given.astype(jnp.float32)


def over_z(total):
    out = total[0]
    for s in range(1, total.shape[0]):
        out += shift_z(total[s].astype(jnp.bfloat16), -s).astype(jnp.float32)
    return out.astype(jnp.bfloat16)


def place_kernel(depth, *refs):
    parts, out_ref = refs[:-1], refs[-1]
    pair, _, _ = position()
    for part, (blocks) in zip(parts, out_blocks(depth, [p.shape[1] for p in parts])):
        for n, (j, core) in enumerate(blocks):
            start = pl.multiple_of((2 * (pair ^ j) + core) * depth, LANES)
            out_ref[:, pl.ds(start, depth)] = part[:, n * depth : (n + 1) * depth]


def out_blocks(depth, widths):
    own, others = [(0, 0), (0, 1)], widths[1] // depth
    return [own] + [[(j + 1, core) for j in range(others)] for core in range(2)]


def placed(parts, depth, width):
    vmem = pl.BlockSpec(memory_space=pltpu.VMEM)
    return pl.pallas_call(
        functools.partial(place_kernel, depth),
        in_specs=[vmem] * len(parts),
        out_specs=vmem,
        out_shape=jax.ShapeDtypeStruct((parts[0].shape[0], width), parts[0].dtype),
        compiler_params=params(),
        cost_estimate=NOTHING,
    )(*parts)


def local(tokens, router_probs, expert_ids, old_place, new_place, w_gate, w_up, w_down):
    tok, width = tokens.shape
    depth = w_gate.shape[1]
    n_z = lax.axis_size("dp") // 2
    places = (old_place, new_place)

    (mine,) = copies(((0, "mine", 0, 0), (1, "mine", 0, 1)), places, (w_gate, w_up), (2,))
    theirs, theirs_down = copies(
        ((0, "theirs", 0, 0), (1, "theirs", 0, 1), (2, "theirs", 1, 0)),
        places, (w_gate, w_up, w_down), (2, 1),
    )
    near_weights = [mine, swap(theirs, "shard", 1)]
    weights = spread(near_weights)
    downs = [spread([d]) for d in in_order(w_down, swap(theirs_down, "shard", 1))]

    own = first(tokens, router_probs, expert_ids, old_place)
    columns = [own] + [shift_z(own, s) for s in range(1, n_z)]
    near = [jnp.concatenate([c, swap(c, "dp", 1)], axis=0) for c in columns]
    near = [joined(p, weights[2]) for p in near]
    far = [swap(p, "shard", 1) for p in near]

    hidden = hidden_of(near + far, weights)
    groups = [[d[0] for d in downs]] + [d[1:] for d in downs]
    kept, sent = down_of(hidden, groups[0], ())
    at_core = over_core(kept, sent)
    kept, sent = down_of(hidden, groups[1], (at_core,))
    at_x = over_x(at_core, tok)
    at_core = over_core(kept, sent)
    kept, last = down_of(hidden, groups[2], (at_x, at_core))
    parts = [over_z(at_x), over_z(over_x(at_core, tok)), over_z(over_x(over_core(kept, last), tok))]
    moe_output = placed(parts, depth, width)

    leave, *news = copies(
        tuple((i, "leaves", 0, i) for i in range(3))
        + tuple((i, "stays", i + 1, "stays") for i in range(3)),
        places, (w_gate, w_up, w_down), (3, 2, 2, 2), near,
    )
    news = copies(
        tuple((0, i, i, "leaves") for i in range(3)),
        places, (passed_along(leave, "dp", 1),), (2, 2, 2), (last,), news,
    )
    return (moe_output, *news)


def solution(mesh):
    in_specs = (
        P(("dp", "shard"), None),
        P(("dp", "shard"), None),
        P(("dp", "shard"), None),
        P(),
        P(),
        P("dp", "shard", None),
        P("dp", "shard", None),
        P("dp", "shard", None),
    )
    out_specs = (
        P(("dp", "shard"), None),
        P("dp", "shard", None),
        P("dp", "shard", None),
        P("dp", "shard", None),
    )
    return jax.shard_map(local, mesh=mesh, in_specs=in_specs, out_specs=out_specs, check_vma=False)
```

```python
import functools

import jax
import jax.numpy as jnp
from jax import lax
from jax.experimental import pallas as pl
from jax.experimental.pallas import tpu as pltpu
from jax.sharding import PartitionSpec as P

LANES = 128
VMEM_BYTES = 32 * 1024 * 1024
MOST = 56 * 1024 * 1024
NOTHING = pl.CostEstimate(flops=0, bytes_accessed=0, transcendentals=0)


def swap(x, axis, bit):
    return lax.ppermute(x, axis, [(i, i ^ bit) for i in range(lax.axis_size(axis))])


def passed_along(x, axis, by):
    size = lax.axis_size(axis)
    return lax.ppermute(x, axis, [(i, (i + by) % size) for i in range(size)])


def shift_z(x, by):
    size = lax.axis_size("dp")
    return lax.ppermute(x, "dp", [(i, (i + 2 * by) % size) for i in range(size)])


def spread(pieces):
    bit = 2
    while bit < lax.axis_size("shard"):
        pieces = pieces + [swap(p, "shard", bit) for p in pieces]
        bit *= 2
    return pieces


def params(amount=VMEM_BYTES):
    return pltpu.CompilerParams(vmem_limit_bytes=amount)


def position():
    column = lax.axis_index("shard")
    return lax.div(column, 2), lax.rem(column, 2), lax.axis_index("dp")


def first_kernel(tokens_ref, probs_ref, ids_ref, place_ref, out_ref, coef_ref):
    probs = probs_ref[...]
    weights = (probs / jnp.sum(probs, axis=0, keepdims=True)).astype(jnp.bfloat16)
    weights = weights.astype(jnp.float32)
    ids = ids_ref[...]
    tok, width = tokens_ref.shape
    coef_ref[...] = jnp.zeros_like(coef_ref)
    for slot in range(place_ref.shape[0]):
        named = jnp.where(ids == place_ref[slot], weights, 0.0)
        coef_ref[slot : slot + 1, :tok] = jnp.sum(named, axis=0, keepdims=True)
    out_ref[:, :width] = tokens_ref[...]
    out_ref[:, width:] = jnp.transpose(coef_ref[...])[:tok].astype(jnp.bfloat16)


def first(tokens, probs, ids, old_place):
    vmem = pl.BlockSpec(memory_space=pltpu.VMEM)
    return pl.pallas_call(
        first_kernel,
        in_specs=[vmem] * 3 + [pl.BlockSpec(memory_space=pltpu.SMEM)],
        out_specs=vmem,
        out_shape=jax.ShapeDtypeStruct((tokens.shape[0], tokens.shape[1] + LANES), tokens.dtype),
        scratch_shapes=[pltpu.VMEM((LANES, LANES), jnp.float32)],
        compiler_params=params(),
        cost_estimate=NOTHING,
    )(tokens, probs.T, ids.T, old_place)


def copy_kernel(plan, n_in, n_out, *refs):
    old_ref, new_ref = refs[:2]
    ins, refs = refs[2 : 2 + n_in], refs[-n_out - 3 :]
    outs, (held, in_sems, out_sems) = refs[:n_out], refs[n_out:]
    _, core, row = position()
    second = 2 * row + 1
    moved = (old_ref[second] != new_ref[second]).astype(jnp.int32)
    slots = {"mine": core, "theirs": 1 - core, "leaves": moved, "stays": 1 - moved}
    slots.update({i: i for i in range(3)})
    loads = [
        pltpu.make_async_copy(ins[i].at[slots[a]], held.at[n], in_sems.at[n])
        for n, (i, a, o, b) in enumerate(plan)
    ]
    stores = [
        pltpu.make_async_copy(held.at[n], outs[o].at[slots[b]], out_sems.at[n])
        for n, (i, a, o, b) in enumerate(plan)
    ]
    for c in loads:
        c.start()
    for n, c in enumerate(stores):
        loads[n].wait()
        c.start()
    for c in stores:
        c.wait()


def copies(plan, places, ins, counts, after=(), aliases=()):
    slot, kind = ins[0].shape[1:], ins[0].dtype
    smem, anywhere = pl.BlockSpec(memory_space=pltpu.SMEM), pl.BlockSpec(memory_space=pl.ANY)
    return pl.pallas_call(
        functools.partial(copy_kernel, plan, len(ins), len(counts)),
        in_specs=[smem] * 2 + [anywhere] * (len(ins) + len(aliases) + len(after)),
        out_specs=(anywhere,) * len(counts),
        out_shape=tuple(jax.ShapeDtypeStruct((n,) + slot, kind) for n in counts),
        input_output_aliases={2 + len(ins) + i: i for i in range(len(aliases))},
        scratch_shapes=[
            pltpu.VMEM((len(plan),) + slot, kind),
            pltpu.SemaphoreType.DMA((len(plan),)),
            pltpu.SemaphoreType.DMA((len(plan),)),
        ],
        compiler_params=params(MOST),
        cost_estimate=NOTHING,
    )(*places, *ins, *aliases, *after)


def order_kernel(mine_ref, other_ref, first_ref, second_ref, held, in_sems, out_sems):
    _, core, _ = position()
    loads = [
        pltpu.make_async_copy(mine_ref.at[core], held.at[core], in_sems.at[0]),
        pltpu.make_async_copy(other_ref.at[0], held.at[1 - core], in_sems.at[1]),
    ]
    stores = [
        pltpu.make_async_copy(held.at[n], out, out_sems.at[n])
        for n, out in enumerate((first_ref, second_ref))
    ]
    for c in loads:
        c.start()
    for c in loads:
        c.wait()
    for c in stores:
        c.start()
    for c in stores:
        c.wait()


def in_order(w_down, other):
    anywhere = pl.BlockSpec(memory_space=pl.ANY)
    slot = w_down.shape[1:]
    return pl.pallas_call(
        order_kernel,
        in_specs=[anywhere] * 2,
        out_specs=(anywhere,) * 2,
        out_shape=(jax.ShapeDtypeStruct(slot, w_down.dtype),) * 2,
        scratch_shapes=[
            pltpu.VMEM((2,) + slot, w_down.dtype),
            pltpu.SemaphoreType.DMA((2,)),
            pltpu.SemaphoreType.DMA((2,)),
        ],
        compiler_params=params(MOST),
        cost_estimate=NOTHING,
    )(w_down, other)


def join_kernel(*refs):
    pass


def joined(x, *after):
    anywhere = pl.BlockSpec(memory_space=pl.ANY)
    return pl.pallas_call(
        join_kernel,
        in_specs=[anywhere] * (1 + len(after)),
        out_specs=anywhere,
        out_shape=jax.ShapeDtypeStruct(x.shape, x.dtype),
        input_output_aliases={0: 0},
        compiler_params=params(),
        cost_estimate=NOTHING,
    )(x, *after)


def hidden_kernel(n_pieces, *refs):
    pieces, weights, (out_ref, x_ref, coef_ref) = refs[:n_pieces], refs[n_pieces:-3], refs[-3:]
    _, depth, block = weights[0].shape
    rows, width = x_ref.shape
    tall = rows // n_pieces
    pair, core, row = position()

    @pl.when(pl.program_id(0) == 0)
    def _():
        for n, p in enumerate(pieces):
            x_ref[n * tall : (n + 1) * tall] = p[:, :width]
            coef = p[:, width:].astype(jnp.float32)
            lane = lax.broadcasted_iota(jnp.int32, coef.shape, 1)
            coef = jnp.sum(jnp.where(lane == 2 * row + core, coef, 0.0), axis=1, keepdims=True)
            coef_ref[n * tall : (n + 1) * tall] = jnp.broadcast_to(coef, (tall, LANES))

    tile = min(rows, 512)
    for top in range(0, rows, tile):
        gate = jnp.zeros((tile, block), jnp.float32)
        up = jnp.zeros((tile, block), jnp.float32)
        for i, w in enumerate(weights):
            start = (2 * (pair ^ (i // 2)) + (core ^ (i % 2))) * depth
            x = x_ref[top : top + tile, pl.ds(pl.multiple_of(start, LANES), depth)]
            gate += jnp.dot(x, w[0], preferred_element_type=jnp.float32)
            up += jnp.dot(x, w[1], preferred_element_type=jnp.float32)
        coef = coef_ref[top : top + tile, :1]
        hidden = gate / (1.0 + jnp.exp(-gate)) * up * coef
        out_ref[top : top + tile] = hidden.astype(out_ref.dtype)


def hidden_of(pieces, weights):
    _, depth, ff = weights[0].shape
    block = 256
    tall, wide = pieces[0].shape
    rows = tall * len(pieces)
    return pl.pallas_call(
        functools.partial(hidden_kernel, len(pieces)),
        grid=(ff // block,),
        in_specs=[pl.BlockSpec((tall, wide), lambda f: (0, 0))] * len(pieces)
        + [pl.BlockSpec((2, depth, block), lambda f: (0, 0, f))] * len(weights),
        out_specs=pl.BlockSpec((rows, block), lambda f: (0, f)),
        out_shape=jax.ShapeDtypeStruct((rows, ff), pieces[0].dtype),
        scratch_shapes=[
            pltpu.VMEM((rows, wide - LANES), pieces[0].dtype),
            pltpu.VMEM((rows, LANES), jnp.float32),
        ],
        compiler_params=params(),
        cost_estimate=pl.CostEstimate(flops=1, bytes_accessed=1, transcendentals=0),
    )(*pieces, *weights)


def down_kernel(n_downs, hidden_ref, *refs):
    downs, (kept_ref, sent_ref) = refs[:n_downs], refs[-2:]
    depth = downs[0].shape[0]
    rows = kept_ref.shape[0]
    tile = min(rows, 512)
    contract = (((1,), (1,)), ((), ()))
    for i, w in enumerate(downs):
        for out, base in ((kept_ref, 0), (sent_ref, rows)):
            for top in range(0, rows, tile):
                part = lax.dot_general(
                    hidden_ref[base + top : base + top + tile], w[...], contract,
                    preferred_element_type=jnp.float32,
                )
                out[top : top + tile, i * depth : (i + 1) * depth] = part.astype(out.dtype)


def down_of(hidden, downs, after):
    depth, ff = downs[0].shape
    rows = hidden.shape[0] // 2
    vmem = pl.BlockSpec(memory_space=pltpu.VMEM)
    out = jax.ShapeDtypeStruct((rows, len(downs) * depth), hidden.dtype)
    return pl.pallas_call(
        functools.partial(down_kernel, len(downs)),
        in_specs=[vmem] * (1 + len(downs)) + [pl.BlockSpec(memory_space=pl.ANY)] * len(after),
        out_specs=(vmem, vmem),
        out_shape=(out, out),
        compiler_params=params(),
        cost_estimate=pl.CostEstimate(flops=1, bytes_accessed=1, transcendentals=0),
    )(hidden, *downs, *after)


def over_core(kept, sent):
    return kept.astype(jnp.float32) + swap(sent, "shard", 1).astype(jnp.float32)


def over_x(total, tok):
    total = total.reshape(-1, 2, tok, total.shape[-1])
    given = swap(total[:, 1].astype(jnp.bfloat16), "dp", 1)
    return total[:, 0] + given.astype(jnp.float32)


def over_z(total):
    out = total[0]
    for s in range(1, total.shape[0]):
        out += shift_z(total[s].astype(jnp.bfloat16), -s).astype(jnp.float32)
    return out.astype(jnp.bfloat16)


def place_kernel(depth, *refs):
    parts, out_ref = refs[:-1], refs[-1]
    pair, _, _ = position()
    for part, (blocks) in zip(parts, out_blocks(depth, [p.shape[1] for p in parts])):
        for n, (j, core) in enumerate(blocks):
            start = pl.multiple_of((2 * (pair ^ j) + core) * depth, LANES)
            out_ref[:, pl.ds(start, depth)] = part[:, n * depth : (n + 1) * depth]


def out_blocks(depth, widths):
    own, others = [(0, 0), (0, 1)], widths[1] // depth
    return [own] + [[(j + 1, core) for j in range(others)] for core in range(2)]


def placed(parts, depth, width):
    vmem = pl.BlockSpec(memory_space=pltpu.VMEM)
    return pl.pallas_call(
        functools.partial(place_kernel, depth),
        in_specs=[vmem] * len(parts),
        out_specs=vmem,
        out_shape=jax.ShapeDtypeStruct((parts[0].shape[0], width), parts[0].dtype),
        compiler_params=params(),
        cost_estimate=NOTHING,
    )(*parts)


def local(tokens, router_probs, expert_ids, old_place, new_place, w_gate, w_up, w_down):
    tok, width = tokens.shape
    depth = w_gate.shape[1]
    n_z = lax.axis_size("dp") // 2
    places = (old_place, new_place)

    (mine,) = copies(((0, "mine", 0, 0), (1, "mine", 0, 1)), places, (w_gate, w_up), (2,))
    theirs, theirs_down = copies(
        ((0, "theirs", 0, 0), (1, "theirs", 0, 1), (2, "theirs", 1, 0)),
        places, (w_gate, w_up, w_down), (2, 1),
    )
    near_weights = [mine, swap(theirs, "shard", 1)]
    weights = spread(near_weights)
    downs = [spread([d]) for d in in_order(w_down, swap(theirs_down, "shard", 1))]

    own = first(tokens, router_probs, expert_ids, old_place)
    columns = [own] + [shift_z(own, s) for s in range(1, n_z)]
    near = [jnp.concatenate([c, swap(c, "dp", 1)], axis=0) for c in columns]
    near = [joined(p, weights[2]) for p in near]
    far = [swap(p, "shard", 1) for p in near]

    hidden = hidden_of(near + far, weights)
    leave, *news = copies(
        tuple((i, "leaves", 0, i) for i in range(3))
        + tuple((i, "stays", i + 1, "stays") for i in range(3)),
        places, (w_gate, w_up, w_down), (3, 2, 2, 2), near,
    )
    arrive = passed_along(leave, "dp", 1)

    groups = [[d[0] for d in downs]] + [d[1:] for d in downs]
    kept, sent = down_of(hidden, groups[0], ())
    at_core = over_core(kept, sent)
    kept, sent = down_of(hidden, groups[1], (sent,))
    at_x = over_x(at_core, tok)
    at_core = over_core(kept, sent)
    kept, last = down_of(hidden, groups[2], (sent, arrive, at_x))
    parts = [over_z(at_x), over_z(over_x(at_core, tok)), over_z(over_x(over_core(kept, last), tok))]
    moe_output = placed(parts, depth, width)

    news = copies(
        tuple((0, i, i, "leaves") for i in range(3)),
        places, (arrive,), (2, 2, 2), (last,), news,
    )
    return (moe_output, *news)


def solution(mesh):
    in_specs = (
        P(("dp", "shard"), None),
        P(("dp", "shard"), None),
        P(("dp", "shard"), None),
        P(),
        P(),
        P("dp", "shard", None),
        P("dp", "shard", None),
        P("dp", "shard", None),
    )
    out_specs = (
        P(("dp", "shard"), None),
        P("dp", "shard", None),
        P("dp", "shard", None),
        P("dp", "shard", None),
    )
    return jax.shard_map(local, mesh=mesh, in_specs=in_specs, out_specs=out_specs, check_vma=False)
```

```python
import functools

import jax
import jax.numpy as jnp
from jax import lax
from jax.experimental import pallas as pl
from jax.experimental.pallas import tpu as pltpu
from jax.sharding import PartitionSpec as P

LANES = 128
VMEM_BYTES = 32 * 1024 * 1024
MOST = 56 * 1024 * 1024
NOTHING = pl.CostEstimate(flops=0, bytes_accessed=0, transcendentals=0)


def swap(x, axis, bit):
    return lax.ppermute(x, axis, [(i, i ^ bit) for i in range(lax.axis_size(axis))])


def passed_along(x, axis, by):
    size = lax.axis_size(axis)
    return lax.ppermute(x, axis, [(i, (i + by) % size) for i in range(size)])


def flip_z(x, bits):
    return swap(x, "dp", 2 * bits)


def spread(pieces):
    bit = 2
    while bit < lax.axis_size("shard"):
        pieces = pieces + [swap(p, "shard", bit) for p in pieces]
        bit *= 2
    return pieces


def params(amount=VMEM_BYTES):
    return pltpu.CompilerParams(vmem_limit_bytes=amount)


def position():
    column = lax.axis_index("shard")
    return lax.div(column, 2), lax.rem(column, 2), lax.axis_index("dp")


def first_kernel(tokens_ref, probs_ref, ids_ref, place_ref, out_ref, coef_ref):
    probs = probs_ref[...]
    weights = (probs / jnp.sum(probs, axis=0, keepdims=True)).astype(jnp.bfloat16)
    weights = weights.astype(jnp.float32)
    ids = ids_ref[...]
    tok, width = tokens_ref.shape
    coef_ref[...] = jnp.zeros_like(coef_ref)
    for slot in range(place_ref.shape[0]):
        named = jnp.where(ids == place_ref[slot], weights, 0.0)
        coef_ref[slot : slot + 1, :tok] = jnp.sum(named, axis=0, keepdims=True)
    out_ref[:, :width] = tokens_ref[...]
    out_ref[:, width:] = jnp.transpose(coef_ref[...])[:tok].astype(jnp.bfloat16)


def first(tokens, probs, ids, old_place):
    vmem = pl.BlockSpec(memory_space=pltpu.VMEM)
    return pl.pallas_call(
        first_kernel,
        in_specs=[vmem] * 3 + [pl.BlockSpec(memory_space=pltpu.SMEM)],
        out_specs=vmem,
        out_shape=jax.ShapeDtypeStruct((tokens.shape[0], tokens.shape[1] + LANES), tokens.dtype),
        scratch_shapes=[pltpu.VMEM((LANES, LANES), jnp.float32)],
        compiler_params=params(),
        cost_estimate=NOTHING,
    )(tokens, probs.T, ids.T, old_place)


def copy_kernel(plan, n_in, n_out, *refs):
    old_ref, new_ref = refs[:2]
    ins, refs = refs[2 : 2 + n_in], refs[-n_out - 3 :]
    outs, (held, in_sems, out_sems) = refs[:n_out], refs[n_out:]
    _, core, row = position()
    second = 2 * row + 1
    moved = (old_ref[second] != new_ref[second]).astype(jnp.int32)
    slots = {"mine": core, "theirs": 1 - core, "leaves": moved, "stays": 1 - moved}
    slots.update({i: i for i in range(3)})
    loads = [
        pltpu.make_async_copy(ins[i].at[slots[a]], held.at[n], in_sems.at[n])
        for n, (i, a, o, b) in enumerate(plan)
    ]
    stores = [
        pltpu.make_async_copy(held.at[n], outs[o].at[slots[b]], out_sems.at[n])
        for n, (i, a, o, b) in enumerate(plan)
    ]
    for c in loads:
        c.start()
    for n, c in enumerate(stores):
        loads[n].wait()
        c.start()
    for c in stores:
        c.wait()


def copies(plan, places, ins, counts, after=(), aliases=()):
    slot, kind = ins[0].shape[1:], ins[0].dtype
    smem, anywhere = pl.BlockSpec(memory_space=pltpu.SMEM), pl.BlockSpec(memory_space=pl.ANY)
    return pl.pallas_call(
        functools.partial(copy_kernel, plan, len(ins), len(counts)),
        in_specs=[smem] * 2 + [anywhere] * (len(ins) + len(aliases) + len(after)),
        out_specs=(anywhere,) * len(counts),
        out_shape=tuple(jax.ShapeDtypeStruct((n,) + slot, kind) for n in counts),
        input_output_aliases={2 + len(ins) + i: i for i in range(len(aliases))},
        scratch_shapes=[
            pltpu.VMEM((len(plan),) + slot, kind),
            pltpu.SemaphoreType.DMA((len(plan),)),
            pltpu.SemaphoreType.DMA((len(plan),)),
        ],
        compiler_params=params(MOST),
        cost_estimate=NOTHING,
    )(*places, *ins, *aliases, *after)


def order_kernel(mine_ref, other_ref, first_ref, second_ref, held, in_sems, out_sems):
    _, core, _ = position()
    loads = [
        pltpu.make_async_copy(mine_ref.at[core], held.at[core], in_sems.at[0]),
        pltpu.make_async_copy(other_ref.at[0], held.at[1 - core], in_sems.at[1]),
    ]
    stores = [
        pltpu.make_async_copy(held.at[n], out, out_sems.at[n])
        for n, out in enumerate((first_ref, second_ref))
    ]
    for c in loads:
        c.start()
    for c in loads:
        c.wait()
    for c in stores:
        c.start()
    for c in stores:
        c.wait()


def in_order(w_down, other):
    anywhere = pl.BlockSpec(memory_space=pl.ANY)
    slot = w_down.shape[1:]
    return pl.pallas_call(
        order_kernel,
        in_specs=[anywhere] * 2,
        out_specs=(anywhere,) * 2,
        out_shape=(jax.ShapeDtypeStruct(slot, w_down.dtype),) * 2,
        scratch_shapes=[
            pltpu.VMEM((2,) + slot, w_down.dtype),
            pltpu.SemaphoreType.DMA((2,)),
            pltpu.SemaphoreType.DMA((2,)),
        ],
        compiler_params=params(MOST),
        cost_estimate=NOTHING,
    )(w_down, other)


def join_kernel(*refs):
    pass


def joined(x, *after):
    if not after:
        return x
    anywhere = pl.BlockSpec(memory_space=pl.ANY)
    return pl.pallas_call(
        join_kernel,
        in_specs=[anywhere] * (1 + len(after)),
        out_specs=anywhere,
        out_shape=jax.ShapeDtypeStruct(x.shape, x.dtype),
        input_output_aliases={0: 0},
        compiler_params=params(),
        cost_estimate=NOTHING,
    )(x, *after)


def hidden_kernel(n_pieces, *refs):
    pieces, weights, (out_ref, x_ref, coef_ref) = refs[:n_pieces], refs[n_pieces:-3], refs[-3:]
    _, depth, block = weights[0].shape
    rows, width = x_ref.shape
    tall = rows // n_pieces
    pair, core, row = position()

    @pl.when(pl.program_id(0) == 0)
    def _():
        for n, p in enumerate(pieces):
            x_ref[n * tall : (n + 1) * tall] = p[:, :width]
            coef = p[:, width:].astype(jnp.float32)
            lane = lax.broadcasted_iota(jnp.int32, coef.shape, 1)
            coef = jnp.sum(jnp.where(lane == 2 * row + core, coef, 0.0), axis=1, keepdims=True)
            coef_ref[n * tall : (n + 1) * tall] = jnp.broadcast_to(coef, (tall, LANES))

    tile = min(rows, 512)
    for top in range(0, rows, tile):
        gate = jnp.zeros((tile, block), jnp.float32)
        up = jnp.zeros((tile, block), jnp.float32)
        for i, w in enumerate(weights):
            start = (2 * (pair ^ (i // 2)) + (core ^ (i % 2))) * depth
            x = x_ref[top : top + tile, pl.ds(pl.multiple_of(start, LANES), depth)]
            gate += jnp.dot(x, w[0], preferred_element_type=jnp.float32)
            up += jnp.dot(x, w[1], preferred_element_type=jnp.float32)
        coef = coef_ref[top : top + tile, :1]
        hidden = gate / (1.0 + jnp.exp(-gate)) * up * coef
        out_ref[top : top + tile] = hidden.astype(out_ref.dtype)


def hidden_of(pieces, weights):
    _, depth, ff = weights[0].shape
    block = 256
    tall, wide = pieces[0].shape
    rows = tall * len(pieces)
    return pl.pallas_call(
        functools.partial(hidden_kernel, len(pieces)),
        grid=(ff // block,),
        in_specs=[pl.BlockSpec((tall, wide), lambda f: (0, 0))] * len(pieces)
        + [pl.BlockSpec((2, depth, block), lambda f: (0, 0, f))] * len(weights),
        out_specs=pl.BlockSpec((rows, block), lambda f: (0, f)),
        out_shape=jax.ShapeDtypeStruct((rows, ff), pieces[0].dtype),
        scratch_shapes=[
            pltpu.VMEM((rows, wide - LANES), pieces[0].dtype),
            pltpu.VMEM((rows, LANES), jnp.float32),
        ],
        compiler_params=params(),
        cost_estimate=pl.CostEstimate(flops=1, bytes_accessed=1, transcendentals=0),
    )(*pieces, *weights)


def down_kernel(n_downs, hidden_ref, *refs):
    downs, (kept_ref, sent_ref) = refs[:n_downs], refs[-2:]
    depth = downs[0].shape[0]
    rows = kept_ref.shape[0]
    tile = min(rows, 512)
    contract = (((1,), (1,)), ((), ()))
    for i, w in enumerate(downs):
        for out, base in ((kept_ref, 0), (sent_ref, rows)):
            for top in range(0, rows, tile):
                part = lax.dot_general(
                    hidden_ref[base + top : base + top + tile], w[...], contract,
                    preferred_element_type=jnp.float32,
                )
                out[top : top + tile, i * depth : (i + 1) * depth] = part.astype(out.dtype)


def down_of(hidden, downs, after):
    depth, ff = downs[0].shape
    rows = hidden.shape[0] // 2
    vmem = pl.BlockSpec(memory_space=pltpu.VMEM)
    out = jax.ShapeDtypeStruct((rows, len(downs) * depth), hidden.dtype)
    return pl.pallas_call(
        functools.partial(down_kernel, len(downs)),
        in_specs=[vmem] * (1 + len(downs)) + [pl.BlockSpec(memory_space=pl.ANY)] * len(after),
        out_specs=(vmem, vmem),
        out_shape=(out, out),
        compiler_params=params(),
        cost_estimate=pl.CostEstimate(flops=1, bytes_accessed=1, transcendentals=0),
    )(hidden, *downs, *after)


def over_core(kept, sent):
    return kept.astype(jnp.float32) + swap(sent, "shard", 1).astype(jnp.float32)


def over_x(total, tok, *after):
    total = total.reshape(-1, 2, tok, total.shape[-1])
    given = swap(joined(total[:, 1].astype(jnp.bfloat16), *after), "dp", 1)
    return total[:, 0] + given.astype(jnp.float32)


def over_z(total):
    while total.shape[0] > 1:
        half = total.shape[0] // 2
        given = flip_z(total[half:].astype(jnp.bfloat16), half)
        total = total[:half] + given.astype(jnp.float32)
    return total[0].astype(jnp.bfloat16)


def place_kernel(depth, *refs):
    parts, out_ref = refs[:-1], refs[-1]
    pair, _, _ = position()
    for part, (blocks) in zip(parts, out_blocks(depth, [p.shape[1] for p in parts])):
        for n, (j, core) in enumerate(blocks):
            start = pl.multiple_of((2 * (pair ^ j) + core) * depth, LANES)
            out_ref[:, pl.ds(start, depth)] = part[:, n * depth : (n + 1) * depth]


def out_blocks(depth, widths):
    own, others = [(0, 0), (0, 1)], widths[1] // depth
    return [own] + [[(j + 1, core) for j in range(others)] for core in range(2)]


def placed(parts, depth, width):
    vmem = pl.BlockSpec(memory_space=pltpu.VMEM)
    return pl.pallas_call(
        functools.partial(place_kernel, depth),
        in_specs=[vmem] * len(parts),
        out_specs=vmem,
        out_shape=jax.ShapeDtypeStruct((parts[0].shape[0], width), parts[0].dtype),
        compiler_params=params(),
        cost_estimate=NOTHING,
    )(*parts)


def local(tokens, router_probs, expert_ids, old_place, new_place, w_gate, w_up, w_down):
    tok, width = tokens.shape
    depth = w_gate.shape[1]
    n_z = lax.axis_size("dp") // 2
    places = (old_place, new_place)

    (mine,) = copies(((0, "mine", 0, 0), (1, "mine", 0, 1)), places, (w_gate, w_up), (2,))
    theirs, theirs_down = copies(
        ((0, "theirs", 0, 0), (1, "theirs", 0, 1), (2, "theirs", 1, 0)),
        places, (w_gate, w_up, w_down), (2, 1), (mine,),
    )
    near_weights = [mine, swap(theirs, "shard", 1)]
    weights = spread(near_weights)
    downs = [spread([d]) for d in in_order(w_down, swap(theirs_down, "shard", 1))]

    own = first(tokens, router_probs, expert_ids, old_place)
    columns = [own] + [flip_z(own, j) for j in range(1, n_z)]
    across = [swap(c, "dp", 1) for c in columns]
    near = [joined(jnp.concatenate(p, axis=0), weights[2]) for p in zip(columns, across)]
    far = [swap(p, "shard", 1) for p in near]

    hidden = hidden_of(near + far, weights)
    leave, *news = copies(
        tuple((i, "leaves", 0, i) for i in range(3))
        + tuple((i, "stays", i + 1, "stays") for i in range(3)),
        places, (w_gate, w_up, w_down), (3, 2, 2, 2), near,
    )
    arrive = passed_along(leave, "dp", 1)

    leave, *news = copies(
        tuple((i, "leaves", 0, i) for i in range(3))
        + tuple((i, "stays", i + 1, "stays") for i in range(3)),
        places, (w_gate, w_up, w_down), (3, 2, 2, 2), across,
    )
    arrive = passed_along(leave, "dp", 1)
    news = copies(
        tuple((0, i, i, "leaves") for i in range(3)), places, (arrive,), (2, 2, 2), (), news
    )

    groups = [[d[0] for d in downs]] + [d[1:] for d in downs]
    kept, sent = down_of(hidden, groups[0], ())
    at_core = over_core(kept, sent)
    kept, sent = down_of(hidden, groups[1], (sent, news[0]))
    own_part = over_z(over_x(at_core, tok, sent))
    at_x = over_x(over_core(kept, sent), tok)
    kept, sent = down_of(hidden, groups[2], (sent, own_part, at_x))
    parts = [own_part, over_z(at_x), over_z(over_x(over_core(kept, sent), tok))]
    moe_output = placed(parts, depth, width)

    return (moe_output, *news)


def solution(mesh):
    in_specs = (
        P(("dp", "shard"), None),
        P(("dp", "shard"), None),
        P(("dp", "shard"), None),
        P(),
        P(),
        P("dp", "shard", None),
        P("dp", "shard", None),
        P("dp", "shard", None),
    )
    out_specs = (
        P(("dp", "shard"), None),
        P("dp", "shard", None),
        P("dp", "shard", None),
        P("dp", "shard", None),
    )
    return jax.shard_map(local, mesh=mesh, in_specs=in_specs, out_specs=out_specs, check_vma=False)
```

```python
import functools

import jax
import jax.numpy as jnp
from jax import lax
from jax.experimental import pallas as pl
from jax.experimental.pallas import tpu as pltpu
from jax.sharding import PartitionSpec as P

LANES = 128
VMEM_BYTES = 32 * 1024 * 1024
MOST = 56 * 1024 * 1024
NOTHING = pl.CostEstimate(flops=0, bytes_accessed=0, transcendentals=0)


def swap(x, axis, bit):
    return lax.ppermute(x, axis, [(i, i ^ bit) for i in range(lax.axis_size(axis))])


def passed_along(x, axis, by):
    size = lax.axis_size(axis)
    return lax.ppermute(x, axis, [(i, (i + by) % size) for i in range(size)])


def flip_z(x, bits):
    return swap(x, "dp", 2 * bits)


def spread(pieces):
    bit = 2
    while bit < lax.axis_size("shard"):
        pieces = pieces + [swap(p, "shard", bit) for p in pieces]
        bit *= 2
    return pieces


def params(amount=VMEM_BYTES):
    return pltpu.CompilerParams(vmem_limit_bytes=amount)


def position():
    column = lax.axis_index("shard")
    return lax.div(column, 2), lax.rem(column, 2), lax.axis_index("dp")


def first_kernel(tokens_ref, probs_ref, ids_ref, place_ref, out_ref, coef_ref):
    probs = probs_ref[...]
    weights = (probs / jnp.sum(probs, axis=0, keepdims=True)).astype(jnp.bfloat16)
    weights = weights.astype(jnp.float32)
    ids = ids_ref[...]
    tok, width = tokens_ref.shape
    coef_ref[...] = jnp.zeros_like(coef_ref)
    for slot in range(place_ref.shape[0]):
        named = jnp.where(ids == place_ref[slot], weights, 0.0)
        coef_ref[slot : slot + 1, :tok] = jnp.sum(named, axis=0, keepdims=True)
    out_ref[:, :width] = tokens_ref[...]
    out_ref[:, width:] = jnp.transpose(coef_ref[...])[:tok].astype(jnp.bfloat16)


def first(tokens, probs, ids, old_place):
    vmem = pl.BlockSpec(memory_space=pltpu.VMEM)
    return pl.pallas_call(
        first_kernel,
        in_specs=[vmem] * 3 + [pl.BlockSpec(memory_space=pltpu.SMEM)],
        out_specs=vmem,
        out_shape=jax.ShapeDtypeStruct((tokens.shape[0], tokens.shape[1] + LANES), tokens.dtype),
        scratch_shapes=[pltpu.VMEM((LANES, LANES), jnp.float32)],
        compiler_params=params(),
        cost_estimate=NOTHING,
    )(tokens, probs.T, ids.T, old_place)


def copy_kernel(plan, n_in, n_out, *refs):
    old_ref, new_ref = refs[:2]
    ins, refs = refs[2 : 2 + n_in], refs[-n_out - 3 :]
    outs, (held, in_sems, out_sems) = refs[:n_out], refs[n_out:]
    _, core, row = position()
    second = 2 * row + 1
    moved = (old_ref[second] != new_ref[second]).astype(jnp.int32)
    slots = {"mine": core, "theirs": 1 - core, "leaves": moved, "stays": 1 - moved}
    slots.update({i: i for i in range(3)})
    loads = [
        pltpu.make_async_copy(ins[i].at[slots[a]], held.at[n], in_sems.at[n])
        for n, (i, a, o, b) in enumerate(plan)
    ]
    stores = [
        pltpu.make_async_copy(held.at[n], outs[o].at[slots[b]], out_sems.at[n])
        for n, (i, a, o, b) in enumerate(plan)
    ]
    for c in loads:
        c.start()
    for n, c in enumerate(stores):
        loads[n].wait()
        c.start()
    for c in stores:
        c.wait()


def copies(plan, places, ins, counts, after=(), aliases=()):
    slot, kind = ins[0].shape[1:], ins[0].dtype
    smem, anywhere = pl.BlockSpec(memory_space=pltpu.SMEM), pl.BlockSpec(memory_space=pl.ANY)
    return pl.pallas_call(
        functools.partial(copy_kernel, plan, len(ins), len(counts)),
        in_specs=[smem] * 2 + [anywhere] * (len(ins) + len(aliases) + len(after)),
        out_specs=(anywhere,) * len(counts),
        out_shape=tuple(jax.ShapeDtypeStruct((n,) + slot, kind) for n in counts),
        input_output_aliases={2 + len(ins) + i: i for i in range(len(aliases))},
        scratch_shapes=[
            pltpu.VMEM((len(plan),) + slot, kind),
            pltpu.SemaphoreType.DMA((len(plan),)),
            pltpu.SemaphoreType.DMA((len(plan),)),
        ],
        compiler_params=params(MOST),
        cost_estimate=NOTHING,
    )(*places, *ins, *aliases, *after)


def order_kernel(mine_ref, other_ref, first_ref, second_ref, held, in_sems, out_sems):
    _, core, _ = position()
    loads = [
        pltpu.make_async_copy(mine_ref.at[core], held.at[core], in_sems.at[0]),
        pltpu.make_async_copy(other_ref.at[0], held.at[1 - core], in_sems.at[1]),
    ]
    stores = [
        pltpu.make_async_copy(held.at[n], out, out_sems.at[n])
        for n, out in enumerate((first_ref, second_ref))
    ]
    for c in loads:
        c.start()
    for c in loads:
        c.wait()
    for c in stores:
        c.start()
    for c in stores:
        c.wait()


def in_order(w_down, other):
    anywhere = pl.BlockSpec(memory_space=pl.ANY)
    slot = w_down.shape[1:]
    return pl.pallas_call(
        order_kernel,
        in_specs=[anywhere] * 2,
        out_specs=(anywhere,) * 2,
        out_shape=(jax.ShapeDtypeStruct(slot, w_down.dtype),) * 2,
        scratch_shapes=[
            pltpu.VMEM((2,) + slot, w_down.dtype),
            pltpu.SemaphoreType.DMA((2,)),
            pltpu.SemaphoreType.DMA((2,)),
        ],
        compiler_params=params(MOST),
        cost_estimate=NOTHING,
    )(w_down, other)


def join_kernel(*refs):
    pass


def joined(x, *after):
    anywhere = pl.BlockSpec(memory_space=pl.ANY)
    return pl.pallas_call(
        join_kernel,
        in_specs=[anywhere] * (1 + len(after)),
        out_specs=anywhere,
        out_shape=jax.ShapeDtypeStruct(x.shape, x.dtype),
        input_output_aliases={0: 0},
        compiler_params=params(),
        cost_estimate=NOTHING,
    )(x, *after)


def hidden_kernel(n_pieces, *refs):
    pieces, weights, (out_ref, x_ref, coef_ref) = refs[:n_pieces], refs[n_pieces:-3], refs[-3:]
    _, depth, block = weights[0].shape
    rows, width = x_ref.shape
    tall = rows // n_pieces
    pair, core, row = position()

    @pl.when(pl.program_id(0) == 0)
    def _():
        for n, p in enumerate(pieces):
            x_ref[n * tall : (n + 1) * tall] = p[:, :width]
            coef = p[:, width:].astype(jnp.float32)
            lane = lax.broadcasted_iota(jnp.int32, coef.shape, 1)
            coef = jnp.sum(jnp.where(lane == 2 * row + core, coef, 0.0), axis=1, keepdims=True)
            coef_ref[n * tall : (n + 1) * tall] = jnp.broadcast_to(coef, (tall, LANES))

    tile = min(rows, 512)
    for top in range(0, rows, tile):
        gate = jnp.zeros((tile, block), jnp.float32)
        up = jnp.zeros((tile, block), jnp.float32)
        for i, w in enumerate(weights):
            start = (2 * (pair ^ (i // 2)) + (core ^ (i % 2))) * depth
            x = x_ref[top : top + tile, pl.ds(pl.multiple_of(start, LANES), depth)]
            gate += jnp.dot(x, w[0], preferred_element_type=jnp.float32)
            up += jnp.dot(x, w[1], preferred_element_type=jnp.float32)
        coef = coef_ref[top : top + tile, :1]
        hidden = gate / (1.0 + jnp.exp(-gate)) * up * coef
        out_ref[top : top + tile] = hidden.astype(out_ref.dtype)


def hidden_of(pieces, weights):
    _, depth, ff = weights[0].shape
    block = 256
    tall, wide = pieces[0].shape
    rows = tall * len(pieces)
    return pl.pallas_call(
        functools.partial(hidden_kernel, len(pieces)),
        grid=(ff // block,),
        in_specs=[pl.BlockSpec((tall, wide), lambda f: (0, 0))] * len(pieces)
        + [pl.BlockSpec((2, depth, block), lambda f: (0, 0, f))] * len(weights),
        out_specs=pl.BlockSpec((rows, block), lambda f: (0, f)),
        out_shape=jax.ShapeDtypeStruct((rows, ff), pieces[0].dtype),
        scratch_shapes=[
            pltpu.VMEM((rows, wide - LANES), pieces[0].dtype),
            pltpu.VMEM((rows, LANES), jnp.float32),
        ],
        compiler_params=params(),
        cost_estimate=pl.CostEstimate(flops=1, bytes_accessed=1, transcendentals=0),
    )(*pieces, *weights)


def down_kernel(n_downs, hidden_ref, *refs):
    downs, (kept_ref, sent_ref) = refs[:n_downs], refs[-2:]
    depth = downs[0].shape[0]
    rows = kept_ref.shape[0]
    tile = min(rows, 512)
    contract = (((1,), (1,)), ((), ()))
    for i, w in enumerate(downs):
        for out, base in ((kept_ref, 0), (sent_ref, rows)):
            for top in range(0, rows, tile):
                part = lax.dot_general(
                    hidden_ref[base + top : base + top + tile], w[...], contract,
                    preferred_element_type=jnp.float32,
                )
                out[top : top + tile, i * depth : (i + 1) * depth] = part.astype(out.dtype)


def down_of(hidden, downs, after):
    depth, ff = downs[0].shape
    rows = hidden.shape[0] // 2
    vmem = pl.BlockSpec(memory_space=pltpu.VMEM)
    out = jax.ShapeDtypeStruct((rows, len(downs) * depth), hidden.dtype)
    return pl.pallas_call(
        functools.partial(down_kernel, len(downs)),
        in_specs=[vmem] * (1 + len(downs)) + [pl.BlockSpec(memory_space=pl.ANY)] * len(after),
        out_specs=(vmem, vmem),
        out_shape=(out, out),
        compiler_params=params(),
        cost_estimate=pl.CostEstimate(flops=1, bytes_accessed=1, transcendentals=0),
    )(hidden, *downs, *after)


def over_core(kept, sent):
    return kept.astype(jnp.float32) + swap(sent, "shard", 1).astype(jnp.float32)


def over_x(total, tok):
    total = total.reshape(-1, 2, tok, total.shape[-1])
    given = swap(total[:, 1].astype(jnp.bfloat16), "dp", 1)
    return total[:, 0] + given.astype(jnp.float32)


def over_z(total):
    while total.shape[0] > 1:
        half = total.shape[0] // 2
        given = flip_z(total[half:].astype(jnp.bfloat16), half)
        total = total[:half] + given.astype(jnp.float32)
    return total[0].astype(jnp.bfloat16)


def place_kernel(depth, *refs):
    parts, out_ref = refs[:-1], refs[-1]
    pair, _, _ = position()
    for part, blocks in zip(parts, out_blocks(depth, [p.shape[1] for p in parts])):
        for n, (j, core) in enumerate(blocks):
            start = pl.multiple_of((2 * (pair ^ j) + core) * depth, LANES)
            out_ref[:, pl.ds(start, depth)] = part[:, n * depth : (n + 1) * depth]


def out_blocks(depth, widths):
    others = range(1, widths[1] // depth + 1)
    return [[(0, 0), (0, 1)] + [(j, 0) for j in others], [(j, 1) for j in others]]


def placed(parts, depth, width):
    vmem = pl.BlockSpec(memory_space=pltpu.VMEM)
    return pl.pallas_call(
        functools.partial(place_kernel, depth),
        in_specs=[vmem] * len(parts),
        out_specs=vmem,
        out_shape=jax.ShapeDtypeStruct((parts[0].shape[0], width), parts[0].dtype),
        compiler_params=params(),
        cost_estimate=NOTHING,
    )(*parts)


def local(tokens, router_probs, expert_ids, old_place, new_place, w_gate, w_up, w_down):
    tok, width = tokens.shape
    depth = w_gate.shape[1]
    n_z = lax.axis_size("dp") // 2
    places = (old_place, new_place)

    (mine,) = copies(((0, "mine", 0, 0), (1, "mine", 0, 1)), places, (w_gate, w_up), (2,))
    theirs, theirs_down = copies(
        ((0, "theirs", 0, 0), (1, "theirs", 0, 1), (2, "theirs", 1, 0)),
        places, (w_gate, w_up, w_down), (2, 1), (mine,),
    )
    near_weights = [mine, swap(theirs, "shard", 1)]
    weights = spread(near_weights)
    downs = [spread([d]) for d in in_order(w_down, swap(theirs_down, "shard", 1))]

    own = first(tokens, router_probs, expert_ids, old_place)
    columns = [own] + [flip_z(own, j) for j in range(1, n_z)]
    across = [swap(c, "dp", 1) for c in columns]
    near = [joined(jnp.concatenate(p, axis=0), weights[2]) for p in zip(columns, across)]
    far = [swap(p, "shard", 1) for p in near]

    hidden = hidden_of(near + far, weights)
    leave, *news = copies(
        tuple((i, "leaves", 0, i) for i in range(3))
        + tuple((i, "stays", i + 1, "stays") for i in range(3)),
        places, (w_gate, w_up, w_down), (3, 2, 2, 2), near,
    )
    arrive = passed_along(leave, "dp", 1)

    leave, *news = copies(
        tuple((i, "leaves", 0, i) for i in range(3))
        + tuple((i, "stays", i + 1, "stays") for i in range(3)),
        places, (w_gate, w_up, w_down), (3, 2, 2, 2), across,
    )
    arrive = passed_along(leave, "dp", 1)
    news = copies(
        tuple((0, i, i, "leaves") for i in range(3)), places, (arrive,), (2, 2, 2), (), news
    )

    groups = [[d[0] for d in downs] + downs[0][1:], downs[1][1:]]
    kept, sent = down_of(hidden, groups[0], ())
    at_core = over_core(kept, sent)
    at_x = over_x(at_core, tok)
    kept, sent = down_of(hidden, groups[1], (news[0], at_x))
    parts = [over_z(at_x), over_z(over_x(over_core(kept, sent), tok))]
    moe_output = placed(parts, depth, width)

    return (moe_output, *news)


def solution(mesh):
    in_specs = (
        P(("dp", "shard"), None),
        P(("dp", "shard"), None),
        P(("dp", "shard"), None),
        P(),
        P(),
        P("dp", "shard", None),
        P("dp", "shard", None),
        P("dp", "shard", None),
    )
    out_specs = (
        P(("dp", "shard"), None),
        P("dp", "shard", None),
        P("dp", "shard", None),
        P("dp", "shard", None),
    )
    return jax.shard_map(local, mesh=mesh, in_specs=in_specs, out_specs=out_specs, check_vma=False)
```

```python
import functools

import jax
import jax.numpy as jnp
from jax import lax
from jax.experimental import pallas as pl
from jax.experimental.pallas import tpu as pltpu
from jax.sharding import PartitionSpec as P

LANES = 128
VMEM_BYTES = 32 * 1024 * 1024
MOST = 56 * 1024 * 1024
NOTHING = pl.CostEstimate(flops=0, bytes_accessed=0, transcendentals=0)


def swap(x, axis, bit):
    return lax.ppermute(x, axis, [(i, i ^ bit) for i in range(lax.axis_size(axis))])


def passed_along(x, axis, by):
    size = lax.axis_size(axis)
    return lax.ppermute(x, axis, [(i, (i + by) % size) for i in range(size)])


def flip_z(x, bits):
    return swap(x, "dp", 2 * bits)


def spread(pieces):
    bit = 2
    while bit < lax.axis_size("shard"):
        pieces = pieces + [swap(p, "shard", bit) for p in pieces]
        bit *= 2
    return pieces


def params(amount=VMEM_BYTES):
    return pltpu.CompilerParams(vmem_limit_bytes=amount)


def position():
    column = lax.axis_index("shard")
    return lax.div(column, 2), lax.rem(column, 2), lax.axis_index("dp")


def first_kernel(tokens_ref, probs_ref, ids_ref, place_ref, out_ref, coef_ref):
    probs = probs_ref[...]
    weights = (probs / jnp.sum(probs, axis=0, keepdims=True)).astype(jnp.bfloat16)
    weights = weights.astype(jnp.float32)
    ids = ids_ref[...]
    tok, width = tokens_ref.shape
    coef_ref[...] = jnp.zeros_like(coef_ref)
    for slot in range(place_ref.shape[0]):
        named = jnp.where(ids == place_ref[slot], weights, 0.0)
        coef_ref[slot : slot + 1, :tok] = jnp.sum(named, axis=0, keepdims=True)
    out_ref[:, :width] = tokens_ref[...]
    out_ref[:, width:] = jnp.transpose(coef_ref[...])[:tok].astype(jnp.bfloat16)


def first(tokens, probs, ids, old_place):
    vmem = pl.BlockSpec(memory_space=pltpu.VMEM)
    return pl.pallas_call(
        first_kernel,
        in_specs=[vmem] * 3 + [pl.BlockSpec(memory_space=pltpu.SMEM)],
        out_specs=vmem,
        out_shape=jax.ShapeDtypeStruct((tokens.shape[0], tokens.shape[1] + LANES), tokens.dtype),
        scratch_shapes=[pltpu.VMEM((LANES, LANES), jnp.float32)],
        compiler_params=params(),
        cost_estimate=NOTHING,
    )(tokens, probs.T, ids.T, old_place)


def copy_kernel(plan, n_in, n_out, *refs):
    old_ref, new_ref = refs[:2]
    ins, refs = refs[2 : 2 + n_in], refs[-n_out - 3 :]
    outs, (held, in_sems, out_sems) = refs[:n_out], refs[n_out:]
    _, core, row = position()
    second = 2 * row + 1
    moved = (old_ref[second] != new_ref[second]).astype(jnp.int32)
    slots = {"mine": core, "theirs": 1 - core, "leaves": moved, "stays": 1 - moved}
    slots.update({i: i for i in range(3)})
    loads = [
        pltpu.make_async_copy(ins[i].at[slots[a]], held.at[n], in_sems.at[n])
        for n, (i, a, o, b) in enumerate(plan)
    ]
    stores = [
        pltpu.make_async_copy(held.at[n], outs[o].at[slots[b]], out_sems.at[n])
        for n, (i, a, o, b) in enumerate(plan)
    ]
    for c in loads:
        c.start()
    for n, c in enumerate(stores):
        loads[n].wait()
        c.start()
    for c in stores:
        c.wait()


def copies(plan, places, ins, counts, after=(), aliases=()):
    slot, kind = ins[0].shape[1:], ins[0].dtype
    smem, anywhere = pl.BlockSpec(memory_space=pltpu.SMEM), pl.BlockSpec(memory_space=pl.ANY)
    return pl.pallas_call(
        functools.partial(copy_kernel, plan, len(ins), len(counts)),
        in_specs=[smem] * 2 + [anywhere] * (len(ins) + len(aliases) + len(after)),
        out_specs=(anywhere,) * len(counts),
        out_shape=tuple(jax.ShapeDtypeStruct((n,) + slot, kind) for n in counts),
        input_output_aliases={2 + len(ins) + i: i for i in range(len(aliases))},
        scratch_shapes=[
            pltpu.VMEM((len(plan),) + slot, kind),
            pltpu.SemaphoreType.DMA((len(plan),)),
            pltpu.SemaphoreType.DMA((len(plan),)),
        ],
        compiler_params=params(MOST),
        cost_estimate=NOTHING,
    )(*places, *ins, *aliases, *after)


def order_kernel(mine_ref, other_ref, first_ref, second_ref, held, in_sems, out_sems):
    _, core, _ = position()
    loads = [
        pltpu.make_async_copy(mine_ref.at[core], held.at[core], in_sems.at[0]),
        pltpu.make_async_copy(other_ref.at[0], held.at[1 - core], in_sems.at[1]),
    ]
    stores = [
        pltpu.make_async_copy(held.at[n], out, out_sems.at[n])
        for n, out in enumerate((first_ref, second_ref))
    ]
    for c in loads:
        c.start()
    for c in loads:
        c.wait()
    for c in stores:
        c.start()
    for c in stores:
        c.wait()


def in_order(w_down, other):
    anywhere = pl.BlockSpec(memory_space=pl.ANY)
    slot = w_down.shape[1:]
    return pl.pallas_call(
        order_kernel,
        in_specs=[anywhere] * 2,
        out_specs=(anywhere,) * 2,
        out_shape=(jax.ShapeDtypeStruct(slot, w_down.dtype),) * 2,
        scratch_shapes=[
            pltpu.VMEM((2,) + slot, w_down.dtype),
            pltpu.SemaphoreType.DMA((2,)),
            pltpu.SemaphoreType.DMA((2,)),
        ],
        compiler_params=params(MOST),
        cost_estimate=NOTHING,
    )(w_down, other)


def join_kernel(*refs):
    pass


def joined(x, *after):
    anywhere = pl.BlockSpec(memory_space=pl.ANY)
    return pl.pallas_call(
        join_kernel,
        in_specs=[anywhere] * (1 + len(after)),
        out_specs=anywhere,
        out_shape=jax.ShapeDtypeStruct(x.shape, x.dtype),
        input_output_aliases={0: 0},
        compiler_params=params(),
        cost_estimate=NOTHING,
    )(x, *after)


def hidden_kernel(n_pieces, *refs):
    pieces, weights, (out_ref, x_ref, coef_ref) = refs[:n_pieces], refs[n_pieces:-3], refs[-3:]
    _, depth, block = weights[0].shape
    rows, width = x_ref.shape
    tall = rows // n_pieces
    pair, core, row = position()

    @pl.when(pl.program_id(0) == 0)
    def _():
        for n, p in enumerate(pieces):
            x_ref[n * tall : (n + 1) * tall] = p[:, :width]
            coef = p[:, width:].astype(jnp.float32)
            lane = lax.broadcasted_iota(jnp.int32, coef.shape, 1)
            coef = jnp.sum(jnp.where(lane == 2 * row + core, coef, 0.0), axis=1, keepdims=True)
            coef_ref[n * tall : (n + 1) * tall] = jnp.broadcast_to(coef, (tall, LANES))

    tile = min(rows, 512)
    for top in range(0, rows, tile):
        gate = jnp.zeros((tile, block), jnp.float32)
        up = jnp.zeros((tile, block), jnp.float32)
        for i, w in enumerate(weights):
            start = (2 * (pair ^ (i // 2)) + (core ^ (i % 2))) * depth
            x = x_ref[top : top + tile, pl.ds(pl.multiple_of(start, LANES), depth)]
            gate += jnp.dot(x, w[0], preferred_element_type=jnp.float32)
            up += jnp.dot(x, w[1], preferred_element_type=jnp.float32)
        coef = coef_ref[top : top + tile, :1]
        hidden = gate / (1.0 + jnp.exp(-gate)) * up * coef
        out_ref[top : top + tile] = hidden.astype(out_ref.dtype)


def hidden_of(pieces, weights):
    _, depth, ff = weights[0].shape
    block = 256
    tall, wide = pieces[0].shape
    rows = tall * len(pieces)
    return pl.pallas_call(
        functools.partial(hidden_kernel, len(pieces)),
        grid=(ff // block,),
        in_specs=[pl.BlockSpec((tall, wide), lambda f: (0, 0))] * len(pieces)
        + [pl.BlockSpec((2, depth, block), lambda f: (0, 0, f))] * len(weights),
        out_specs=pl.BlockSpec((rows, block), lambda f: (0, f)),
        out_shape=jax.ShapeDtypeStruct((rows, ff), pieces[0].dtype),
        scratch_shapes=[
            pltpu.VMEM((rows, wide - LANES), pieces[0].dtype),
            pltpu.VMEM((rows, LANES), jnp.float32),
        ],
        compiler_params=params(),
        cost_estimate=pl.CostEstimate(flops=1, bytes_accessed=1, transcendentals=0),
    )(*pieces, *weights)


def down_kernel(n_downs, hidden_ref, *refs):
    downs, (kept_ref, sent_ref) = refs[:n_downs], refs[-2:]
    depth = downs[0].shape[0]
    rows = kept_ref.shape[0]
    tile = min(rows, 512)
    contract = (((1,), (1,)), ((), ()))
    for i, w in enumerate(downs):
        for out, base in ((kept_ref, 0), (sent_ref, rows)):
            for top in range(0, rows, tile):
                part = lax.dot_general(
                    hidden_ref[base + top : base + top + tile], w[...], contract,
                    preferred_element_type=jnp.float32,
                )
                out[top : top + tile, i * depth : (i + 1) * depth] = part.astype(out.dtype)


def down_of(hidden, downs, after):
    depth, ff = downs[0].shape
    rows = hidden.shape[0] // 2
    vmem = pl.BlockSpec(memory_space=pltpu.VMEM)
    out = jax.ShapeDtypeStruct((rows, len(downs) * depth), hidden.dtype)
    return pl.pallas_call(
        functools.partial(down_kernel, len(downs)),
        in_specs=[vmem] * (1 + len(downs)) + [pl.BlockSpec(memory_space=pl.ANY)] * len(after),
        out_specs=(vmem, vmem),
        out_shape=(out, out),
        compiler_params=params(),
        cost_estimate=pl.CostEstimate(flops=1, bytes_accessed=1, transcendentals=0),
    )(hidden, *downs, *after)


def over_core(kept, sent):
    return kept.astype(jnp.float32) + swap(sent, "shard", 1).astype(jnp.float32)


def over_x(total, tok):
    total = total.reshape(-1, 2, tok, total.shape[-1])
    given = swap(total[:, 1].astype(jnp.bfloat16), "dp", 1)
    return total[:, 0] + given.astype(jnp.float32)


def over_z(total):
    while total.shape[0] > 1:
        half = total.shape[0] // 2
        given = flip_z(total[half:].astype(jnp.bfloat16), half)
        total = total[:half] + given.astype(jnp.float32)
    return total[0].astype(jnp.bfloat16)


def place_kernel(depth, *refs):
    parts, out_ref = refs[:-1], refs[-1]
    pair, _, _ = position()
    for part, blocks in zip(parts, out_blocks(depth, [p.shape[1] for p in parts])):
        for n, (j, core) in enumerate(blocks):
            start = pl.multiple_of((2 * (pair ^ j) + core) * depth, LANES)
            out_ref[:, pl.ds(start, depth)] = part[:, n * depth : (n + 1) * depth]


def out_blocks(depth, widths):
    others = range(1, widths[1] // depth + 1)
    return [[(0, 0), (0, 1)] + [(j, 0) for j in others], [(j, 1) for j in others]]


def placed(parts, depth, width):
    vmem = pl.BlockSpec(memory_space=pltpu.VMEM)
    return pl.pallas_call(
        functools.partial(place_kernel, depth),
        in_specs=[vmem] * len(parts),
        out_specs=vmem,
        out_shape=jax.ShapeDtypeStruct((parts[0].shape[0], width), parts[0].dtype),
        compiler_params=params(),
        cost_estimate=NOTHING,
    )(*parts)


def local(tokens, router_probs, expert_ids, old_place, new_place, w_gate, w_up, w_down):
    tok, width = tokens.shape
    depth = w_gate.shape[1]
    n_z = lax.axis_size("dp") // 2
    places = (old_place, new_place)

    (mine,) = copies(((0, "mine", 0, 0), (1, "mine", 0, 1)), places, (w_gate, w_up), (2,))
    theirs, theirs_down = copies(
        ((0, "theirs", 0, 0), (1, "theirs", 0, 1), (2, "theirs", 1, 0)),
        places, (w_gate, w_up, w_down), (2, 1), (mine,),
    )
    near_weights = [mine, swap(theirs, "shard", 1)]
    weights = spread(near_weights)
    downs = [spread([d]) for d in in_order(w_down, swap(theirs_down, "shard", 1))]

    own = first(tokens, router_probs, expert_ids, old_place)
    columns = [own] + [flip_z(own, j) for j in range(1, n_z)]
    across = [swap(c, "dp", 1) for c in columns]
    near = [joined(jnp.concatenate(p, axis=0), weights[2]) for p in zip(columns, across)]
    far = [swap(p, "shard", 1) for p in near]

    hidden = hidden_of(near + far, weights)
    leave, *news = copies(
        tuple((i, "leaves", 0, i) for i in range(3))
        + tuple((i, "stays", i + 1, "stays") for i in range(3)),
        places, (w_gate, w_up, w_down), (3, 2, 2, 2), near,
    )
    arrive = passed_along(leave, "dp", 1)

    leave, *news = copies(
        tuple((i, "leaves", 0, i) for i in range(3))
        + tuple((i, "stays", i + 1, "stays") for i in range(3)),
        places, (w_gate, w_up, w_down), (3, 2, 2, 2), across + [weights[2]],
    )
    arrive = passed_along(leave, "dp", 1)
    news = copies(
        tuple((0, i, i, "leaves") for i in range(3)), places, (arrive,), (2, 2, 2), (), news
    )

    groups = [[d[0] for d in downs]] + [d[1:] for d in downs]
    kept, sent = down_of(hidden, groups[0], ())
    at_core = over_core(kept, sent)
    kept, sent = down_of(hidden, groups[1], (sent,))
    at_x = over_x(at_core, tok)
    at_core = over_core(kept, sent)
    at_x2 = over_x(at_core, tok)
    kept, last = down_of(hidden, groups[2], (sent, news[0], at_x, at_x2))
    early = over_z(jnp.concatenate([at_x, at_x2], axis=-1))
    parts = [early, over_z(over_x(over_core(kept, last), tok))]
    moe_output = placed(parts, depth, width)

    return (moe_output, *news)


def solution(mesh):
    in_specs = (
        P(("dp", "shard"), None),
        P(("dp", "shard"), None),
        P(("dp", "shard"), None),
        P(),
        P(),
        P("dp", "shard", None),
        P("dp", "shard", None),
        P("dp", "shard", None),
    )
    out_specs = (
        P(("dp", "shard"), None),
        P("dp", "shard", None),
        P("dp", "shard", None),
        P("dp", "shard", None),
    )
    return jax.shard_map(local, mesh=mesh, in_specs=in_specs, out_specs=out_specs, check_vma=False)
```

```python
import functools

import jax
import jax.numpy as jnp
from jax import lax
from jax.experimental import pallas as pl
from jax.experimental.pallas import tpu as pltpu
from jax.sharding import PartitionSpec as P

LANES = 128
VMEM_BYTES = 32 * 1024 * 1024
MOST = 56 * 1024 * 1024
NOTHING = pl.CostEstimate(flops=0, bytes_accessed=0, transcendentals=0)


def swap(x, axis, bit):
    return lax.ppermute(x, axis, [(i, i ^ bit) for i in range(lax.axis_size(axis))])


def passed_along(x, axis, by):
    size = lax.axis_size(axis)
    return lax.ppermute(x, axis, [(i, (i + by) % size) for i in range(size)])


def flip_z(x, bits):
    return swap(x, "dp", 2 * bits)


def spread(pieces):
    bit = 2
    while bit < lax.axis_size("shard"):
        pieces = pieces + [swap(p, "shard", bit) for p in pieces]
        bit *= 2
    return pieces


def params(amount=VMEM_BYTES):
    return pltpu.CompilerParams(vmem_limit_bytes=amount)


def position():
    column = lax.axis_index("shard")
    return lax.div(column, 2), lax.rem(column, 2), lax.axis_index("dp")


def first_kernel(tokens_ref, probs_ref, ids_ref, place_ref, out_ref, coef_ref):
    probs = probs_ref[...]
    weights = (probs / jnp.sum(probs, axis=0, keepdims=True)).astype(jnp.bfloat16)
    weights = weights.astype(jnp.float32)
    ids = ids_ref[...]
    tok, width = tokens_ref.shape
    coef_ref[...] = jnp.zeros_like(coef_ref)
    for slot in range(place_ref.shape[0]):
        named = jnp.where(ids == place_ref[slot], weights, 0.0)
        coef_ref[slot : slot + 1, :tok] = jnp.sum(named, axis=0, keepdims=True)
    out_ref[:, :width] = tokens_ref[...]
    out_ref[:, width:] = jnp.transpose(coef_ref[...])[:tok].astype(jnp.bfloat16)


def first(tokens, probs, ids, old_place):
    vmem = pl.BlockSpec(memory_space=pltpu.VMEM)
    return pl.pallas_call(
        first_kernel,
        in_specs=[vmem] * 3 + [pl.BlockSpec(memory_space=pltpu.SMEM)],
        out_specs=vmem,
        out_shape=jax.ShapeDtypeStruct((tokens.shape[0], tokens.shape[1] + LANES), tokens.dtype),
        scratch_shapes=[pltpu.VMEM((LANES, LANES), jnp.float32)],
        compiler_params=params(),
        cost_estimate=NOTHING,
    )(tokens, probs.T, ids.T, old_place)


def copy_kernel(plan, n_in, n_out, *refs):
    old_ref, new_ref = refs[:2]
    ins, refs = refs[2 : 2 + n_in], refs[-n_out - 3 :]
    outs, (held, in_sems, out_sems) = refs[:n_out], refs[n_out:]
    _, core, row = position()
    second = 2 * row + 1
    moved = (old_ref[second] != new_ref[second]).astype(jnp.int32)
    slots = {"mine": core, "theirs": 1 - core, "leaves": moved, "stays": 1 - moved}
    slots.update({i: i for i in range(3)})
    loads = [
        pltpu.make_async_copy(ins[i].at[slots[a]], held.at[n], in_sems.at[n])
        for n, (i, a, o, b) in enumerate(plan)
    ]
    stores = [
        pltpu.make_async_copy(held.at[n], outs[o].at[slots[b]], out_sems.at[n])
        for n, (i, a, o, b) in enumerate(plan)
    ]
    for c in loads:
        c.start()
    for n, c in enumerate(stores):
        loads[n].wait()
        c.start()
    for c in stores:
        c.wait()


def copies(plan, places, ins, counts, after=(), aliases=()):
    slot, kind = ins[0].shape[1:], ins[0].dtype
    smem, anywhere = pl.BlockSpec(memory_space=pltpu.SMEM), pl.BlockSpec(memory_space=pl.ANY)
    return pl.pallas_call(
        functools.partial(copy_kernel, plan, len(ins), len(counts)),
        in_specs=[smem] * 2 + [anywhere] * (len(ins) + len(aliases) + len(after)),
        out_specs=(anywhere,) * len(counts),
        out_shape=tuple(jax.ShapeDtypeStruct((n,) + slot, kind) for n in counts),
        input_output_aliases={2 + len(ins) + i: i for i in range(len(aliases))},
        scratch_shapes=[
            pltpu.VMEM((len(plan),) + slot, kind),
            pltpu.SemaphoreType.DMA((len(plan),)),
            pltpu.SemaphoreType.DMA((len(plan),)),
        ],
        compiler_params=params(MOST),
        cost_estimate=NOTHING,
    )(*places, *ins, *aliases, *after)


def order_kernel(mine_ref, other_ref, first_ref, second_ref, held, in_sems, out_sems):
    _, core, _ = position()
    loads = [
        pltpu.make_async_copy(mine_ref.at[core], held.at[core], in_sems.at[0]),
        pltpu.make_async_copy(other_ref.at[0], held.at[1 - core], in_sems.at[1]),
    ]
    stores = [
        pltpu.make_async_copy(held.at[n], out, out_sems.at[n])
        for n, out in enumerate((first_ref, second_ref))
    ]
    for c in loads:
        c.start()
    for c in loads:
        c.wait()
    for c in stores:
        c.start()
    for c in stores:
        c.wait()


def in_order(w_down, other):
    anywhere = pl.BlockSpec(memory_space=pl.ANY)
    slot = w_down.shape[1:]
    return pl.pallas_call(
        order_kernel,
        in_specs=[anywhere] * 2,
        out_specs=(anywhere,) * 2,
        out_shape=(jax.ShapeDtypeStruct(slot, w_down.dtype),) * 2,
        scratch_shapes=[
            pltpu.VMEM((2,) + slot, w_down.dtype),
            pltpu.SemaphoreType.DMA((2,)),
            pltpu.SemaphoreType.DMA((2,)),
        ],
        compiler_params=params(MOST),
        cost_estimate=NOTHING,
    )(w_down, other)


def join_kernel(*refs):
    pass


def joined(x, *after):
    anywhere = pl.BlockSpec(memory_space=pl.ANY)
    return pl.pallas_call(
        join_kernel,
        in_specs=[anywhere] * (1 + len(after)),
        out_specs=anywhere,
        out_shape=jax.ShapeDtypeStruct(x.shape, x.dtype),
        input_output_aliases={0: 0},
        compiler_params=params(),
        cost_estimate=NOTHING,
    )(x, *after)


def hidden_kernel(n_pieces, *refs):
    pieces, weights, (out_ref, x_ref, coef_ref) = refs[:n_pieces], refs[n_pieces:-3], refs[-3:]
    _, depth, block = weights[0].shape
    rows, width = x_ref.shape
    tall = rows // n_pieces
    pair, core, row = position()

    @pl.when(pl.program_id(0) == 0)
    def _():
        for n, p in enumerate(pieces):
            x_ref[n * tall : (n + 1) * tall] = p[:, :width]
            coef = p[:, width:].astype(jnp.float32)
            lane = lax.broadcasted_iota(jnp.int32, coef.shape, 1)
            coef = jnp.sum(jnp.where(lane == 2 * row + core, coef, 0.0), axis=1, keepdims=True)
            coef_ref[n * tall : (n + 1) * tall] = jnp.broadcast_to(coef, (tall, LANES))

    tile = min(rows, 512)
    for top in range(0, rows, tile):
        gate = jnp.zeros((tile, block), jnp.float32)
        up = jnp.zeros((tile, block), jnp.float32)
        for i, w in enumerate(weights):
            start = (2 * (pair ^ (i // 2)) + (core ^ (i % 2))) * depth
            x = x_ref[top : top + tile, pl.ds(pl.multiple_of(start, LANES), depth)]
            gate += jnp.dot(x, w[0], preferred_element_type=jnp.float32)
            up += jnp.dot(x, w[1], preferred_element_type=jnp.float32)
        coef = coef_ref[top : top + tile, :1]
        hidden = gate / (1.0 + jnp.exp(-gate)) * up * coef
        out_ref[top : top + tile] = hidden.astype(out_ref.dtype)


def hidden_of(pieces, weights):
    _, depth, ff = weights[0].shape
    block = 256
    tall, wide = pieces[0].shape
    rows = tall * len(pieces)
    return pl.pallas_call(
        functools.partial(hidden_kernel, len(pieces)),
        grid=(ff // block,),
        in_specs=[pl.BlockSpec((tall, wide), lambda f: (0, 0))] * len(pieces)
        + [pl.BlockSpec((2, depth, block), lambda f: (0, 0, f))] * len(weights),
        out_specs=pl.BlockSpec((rows, block), lambda f: (0, f)),
        out_shape=jax.ShapeDtypeStruct((rows, ff), pieces[0].dtype),
        scratch_shapes=[
            pltpu.VMEM((rows, wide - LANES), pieces[0].dtype),
            pltpu.VMEM((rows, LANES), jnp.float32),
        ],
        compiler_params=params(),
        cost_estimate=pl.CostEstimate(flops=1, bytes_accessed=1, transcendentals=0),
    )(*pieces, *weights)


def down_kernel(n_downs, hidden_ref, *refs):
    downs, (kept_ref, sent_ref) = refs[:n_downs], refs[-2:]
    depth = downs[0].shape[0]
    rows = kept_ref.shape[0]
    tile = min(rows, 512)
    contract = (((1,), (1,)), ((), ()))
    for i, w in enumerate(downs):
        for out, base in ((kept_ref, 0), (sent_ref, rows)):
            for top in range(0, rows, tile):
                part = lax.dot_general(
                    hidden_ref[base + top : base + top + tile], w[...], contract,
                    preferred_element_type=jnp.float32,
                )
                out[top : top + tile, i * depth : (i + 1) * depth] = part.astype(out.dtype)


def down_of(hidden, downs, after):
    depth, ff = downs[0].shape
    rows = hidden.shape[0] // 2
    vmem = pl.BlockSpec(memory_space=pltpu.VMEM)
    out = jax.ShapeDtypeStruct((rows, len(downs) * depth), hidden.dtype)
    return pl.pallas_call(
        functools.partial(down_kernel, len(downs)),
        in_specs=[vmem] * (1 + len(downs)) + [pl.BlockSpec(memory_space=pl.ANY)] * len(after),
        out_specs=(vmem, vmem),
        out_shape=(out, out),
        compiler_params=params(),
        cost_estimate=pl.CostEstimate(flops=1, bytes_accessed=1, transcendentals=0),
    )(hidden, *downs, *after)


def over_core(kept, sent):
    return kept.astype(jnp.float32) + swap(sent, "shard", 1).astype(jnp.float32)


def over_x(total, tok):
    total = total.reshape(-1, 2, tok, total.shape[-1])
    given = swap(total[:, 1].astype(jnp.bfloat16), "dp", 1)
    return total[:, 0] + given.astype(jnp.float32)


def over_z(total):
    while total.shape[0] > 1:
        half = total.shape[0] // 2
        given = flip_z(total[half:].astype(jnp.bfloat16), half)
        total = total[:half] + given.astype(jnp.float32)
    return total[0].astype(jnp.bfloat16)


def place_kernel(depth, *refs):
    parts, out_ref = refs[:-1], refs[-1]
    pair, _, _ = position()
    for part, blocks in zip(parts, out_blocks(depth, [p.shape[1] for p in parts])):
        for n, (j, core) in enumerate(blocks):
            start = pl.multiple_of((2 * (pair ^ j) + core) * depth, LANES)
            out_ref[:, pl.ds(start, depth)] = part[:, n * depth : (n + 1) * depth]


def out_blocks(depth, widths):
    others = range(1, widths[1] // depth + 1)
    return [[(0, 0), (0, 1)] + [(j, 0) for j in others], [(j, 1) for j in others]]


def placed(parts, depth, width):
    vmem = pl.BlockSpec(memory_space=pltpu.VMEM)
    return pl.pallas_call(
        functools.partial(place_kernel, depth),
        in_specs=[vmem] * len(parts),
        out_specs=vmem,
        out_shape=jax.ShapeDtypeStruct((parts[0].shape[0], width), parts[0].dtype),
        compiler_params=params(),
        cost_estimate=NOTHING,
    )(*parts)


def local(tokens, router_probs, expert_ids, old_place, new_place, w_gate, w_up, w_down):
    tok, width = tokens.shape
    depth = w_gate.shape[1]
    n_z = lax.axis_size("dp") // 2
    places = (old_place, new_place)

    (mine,) = copies(((0, "mine", 0, 0), (1, "mine", 0, 1)), places, (w_gate, w_up), (2,))
    theirs, theirs_down = copies(
        ((0, "theirs", 0, 0), (1, "theirs", 0, 1), (2, "theirs", 1, 0)),
        places, (w_gate, w_up, w_down), (2, 1), (mine,),
    )
    near_weights = [mine, swap(theirs, "shard", 1)]
    weights = spread(near_weights)
    downs = [spread([d]) for d in in_order(w_down, swap(theirs_down, "shard", 1))]

    (leave,) = copies(
        ((0, "leaves", 0, 0),), places, (w_gate,), (1,), (mine,)
    )
    arrive = passed_along(leave, "dp", 1)

    own = first(tokens, router_probs, expert_ids, old_place)
    columns = [own] + [flip_z(own, j) for j in range(1, n_z)]
    across = [swap(joined(c, arrive), "dp", 1) for c in columns]
    near = [joined(jnp.concatenate(p, axis=0), weights[2]) for p in zip(columns, across)]
    far = [swap(p, "shard", 1) for p in near]

    hidden = hidden_of(near + far, weights)
    leave, *news = copies(
        ((1, "leaves", 0, 0), (2, "leaves", 0, 1))
        + tuple((i, "stays", i + 1, "stays") for i in range(3)),
        places, (w_gate, w_up, w_down), (2, 2, 2, 2), across + [weights[2]],
    )
    arrive_rest = passed_along(leave, "dp", 1)
    news = copies(
        ((0, 0, 0, "leaves"), (1, 0, 1, "leaves"), (1, 1, 2, "leaves")),
        places, (arrive, arrive_rest), (2, 2, 2), (), news,
    )

    groups = [[d[0] for d in downs]] + [d[1:] for d in downs]
    kept, sent = down_of(hidden, groups[0], ())
    at_core = over_core(kept, sent)
    kept, sent = down_of(hidden, groups[1], (sent, arrive_rest))
    at_x = over_x(at_core, tok)
    at_core = over_core(kept, sent)
    at_x2 = over_x(at_core, tok)
    kept, last = down_of(hidden, groups[2], (sent, news[0], at_x, at_x2))
    early = over_z(jnp.concatenate([at_x, at_x2], axis=-1))
    parts = [early, over_z(over_x(over_core(kept, last), tok))]
    moe_output = placed(parts, depth, width)

    return (moe_output, *news)


def solution(mesh):
    in_specs = (
        P(("dp", "shard"), None),
        P(("dp", "shard"), None),
        P(("dp", "shard"), None),
        P(),
        P(),
        P("dp", "shard", None),
        P("dp", "shard", None),
        P("dp", "shard", None),
    )
    out_specs = (
        P(("dp", "shard"), None),
        P("dp", "shard", None),
        P("dp", "shard", None),
        P("dp", "shard", None),
    )
    return jax.shard_map(local, mesh=mesh, in_specs=in_specs, out_specs=out_specs, check_vma=False)
```

```python
import functools

import jax
import jax.numpy as jnp
from jax import lax
from jax.experimental import pallas as pl
from jax.experimental.pallas import tpu as pltpu
from jax.sharding import PartitionSpec as P

LANES = 128
VMEM_BYTES = 32 * 1024 * 1024
MOST = 56 * 1024 * 1024
NOTHING = pl.CostEstimate(flops=0, bytes_accessed=0, transcendentals=0)


def swap(x, axis, bit):
    return lax.ppermute(x, axis, [(i, i ^ bit) for i in range(lax.axis_size(axis))])


def passed_along(x, axis, by):
    size = lax.axis_size(axis)
    return lax.ppermute(x, axis, [(i, (i + by) % size) for i in range(size)])


def flip_z(x, bits):
    return swap(x, "dp", 2 * bits)


def spread(pieces):
    bit = 2
    while bit < lax.axis_size("shard"):
        pieces = pieces + [swap(p, "shard", bit) for p in pieces]
        bit *= 2
    return pieces


def params(amount=VMEM_BYTES):
    return pltpu.CompilerParams(vmem_limit_bytes=amount)


def position():
    column = lax.axis_index("shard")
    return lax.div(column, 2), lax.rem(column, 2), lax.axis_index("dp")


def first_kernel(tokens_ref, probs_ref, ids_ref, place_ref, out_ref, coef_ref):
    probs = probs_ref[...]
    weights = (probs / jnp.sum(probs, axis=0, keepdims=True)).astype(jnp.bfloat16)
    weights = weights.astype(jnp.float32)
    ids = ids_ref[...]
    tok, width = tokens_ref.shape
    coef_ref[...] = jnp.zeros_like(coef_ref)
    for slot in range(place_ref.shape[0]):
        named = jnp.where(ids == place_ref[slot], weights, 0.0)
        coef_ref[slot : slot + 1, :tok] = jnp.sum(named, axis=0, keepdims=True)
    out_ref[:, :width] = tokens_ref[...]
    out_ref[:, width:] = jnp.transpose(coef_ref[...])[:tok].astype(jnp.bfloat16)


def first(tokens, probs, ids, old_place):
    vmem = pl.BlockSpec(memory_space=pltpu.VMEM)
    return pl.pallas_call(
        first_kernel,
        in_specs=[vmem] * 3 + [pl.BlockSpec(memory_space=pltpu.SMEM)],
        out_specs=vmem,
        out_shape=jax.ShapeDtypeStruct((tokens.shape[0], tokens.shape[1] + LANES), tokens.dtype),
        scratch_shapes=[pltpu.VMEM((LANES, LANES), jnp.float32)],
        compiler_params=params(),
        cost_estimate=NOTHING,
    )(tokens, probs.T, ids.T, old_place)


def copy_kernel(plan, n_in, n_out, *refs):
    old_ref, new_ref = refs[:2]
    ins, refs = refs[2 : 2 + n_in], refs[-n_out - 3 :]
    outs, (held, in_sems, out_sems) = refs[:n_out], refs[n_out:]
    _, core, row = position()
    second = 2 * row + 1
    moved = (old_ref[second] != new_ref[second]).astype(jnp.int32)
    slots = {"mine": core, "theirs": 1 - core, "leaves": moved, "stays": 1 - moved}
    slots.update({i: i for i in range(3)})
    loads = [
        pltpu.make_async_copy(ins[i].at[slots[a]], held.at[n], in_sems.at[n])
        for n, (i, a, o, b) in enumerate(plan)
    ]
    stores = [
        pltpu.make_async_copy(held.at[n], outs[o].at[slots[b]], out_sems.at[n])
        for n, (i, a, o, b) in enumerate(plan)
    ]
    for c in loads:
        c.start()
    for n, c in enumerate(stores):
        loads[n].wait()
        c.start()
    for c in stores:
        c.wait()


def copies(plan, places, ins, counts, after=(), aliases=()):
    slot, kind = ins[0].shape[1:], ins[0].dtype
    smem, anywhere = pl.BlockSpec(memory_space=pltpu.SMEM), pl.BlockSpec(memory_space=pl.ANY)
    return pl.pallas_call(
        functools.partial(copy_kernel, plan, len(ins), len(counts)),
        in_specs=[smem] * 2 + [anywhere] * (len(ins) + len(aliases) + len(after)),
        out_specs=(anywhere,) * len(counts),
        out_shape=tuple(jax.ShapeDtypeStruct((n,) + slot, kind) for n in counts),
        input_output_aliases={2 + len(ins) + i: i for i in range(len(aliases))},
        scratch_shapes=[
            pltpu.VMEM((len(plan),) + slot, kind),
            pltpu.SemaphoreType.DMA((len(plan),)),
            pltpu.SemaphoreType.DMA((len(plan),)),
        ],
        compiler_params=params(MOST),
        cost_estimate=NOTHING,
    )(*places, *ins, *aliases, *after)


def order_kernel(mine_ref, other_ref, first_ref, second_ref, held, in_sems, out_sems):
    _, core, _ = position()
    loads = [
        pltpu.make_async_copy(mine_ref.at[core], held.at[core], in_sems.at[0]),
        pltpu.make_async_copy(other_ref.at[0], held.at[1 - core], in_sems.at[1]),
    ]
    stores = [
        pltpu.make_async_copy(held.at[n], out, out_sems.at[n])
        for n, out in enumerate((first_ref, second_ref))
    ]
    for c in loads:
        c.start()
    for c in loads:
        c.wait()
    for c in stores:
        c.start()
    for c in stores:
        c.wait()


def in_order(w_down, other):
    anywhere = pl.BlockSpec(memory_space=pl.ANY)
    slot = w_down.shape[1:]
    return pl.pallas_call(
        order_kernel,
        in_specs=[anywhere] * 2,
        out_specs=(anywhere,) * 2,
        out_shape=(jax.ShapeDtypeStruct(slot, w_down.dtype),) * 2,
        scratch_shapes=[
            pltpu.VMEM((2,) + slot, w_down.dtype),
            pltpu.SemaphoreType.DMA((2,)),
            pltpu.SemaphoreType.DMA((2,)),
        ],
        compiler_params=params(MOST),
        cost_estimate=NOTHING,
    )(w_down, other)


def join_kernel(*refs):
    pass


def joined(x, *after):
    anywhere = pl.BlockSpec(memory_space=pl.ANY)
    return pl.pallas_call(
        join_kernel,
        in_specs=[anywhere] * (1 + len(after)),
        out_specs=anywhere,
        out_shape=jax.ShapeDtypeStruct(x.shape, x.dtype),
        input_output_aliases={0: 0},
        compiler_params=params(),
        cost_estimate=NOTHING,
    )(x, *after)


def hidden_kernel(n_pieces, *refs):
    pieces, weights, (out_ref, x_ref, coef_ref) = refs[:n_pieces], refs[n_pieces:-3], refs[-3:]
    _, depth, block = weights[0].shape
    rows, width = x_ref.shape
    tall = rows // n_pieces
    pair, core, row = position()

    @pl.when(pl.program_id(0) == 0)
    def _():
        for n, p in enumerate(pieces):
            x_ref[n * tall : (n + 1) * tall] = p[:, :width]
            coef = p[:, width:].astype(jnp.float32)
            lane = lax.broadcasted_iota(jnp.int32, coef.shape, 1)
            coef = jnp.sum(jnp.where(lane == 2 * row + core, coef, 0.0), axis=1, keepdims=True)
            coef_ref[n * tall : (n + 1) * tall] = jnp.broadcast_to(coef, (tall, LANES))

    tile = min(rows, 512)
    for top in range(0, rows, tile):
        gate = jnp.zeros((tile, block), jnp.float32)
        up = jnp.zeros((tile, block), jnp.float32)
        for i, w in enumerate(weights):
            start = (2 * (pair ^ (i // 2)) + (core ^ (i % 2))) * depth
            x = x_ref[top : top + tile, pl.ds(pl.multiple_of(start, LANES), depth)]
            gate += jnp.dot(x, w[0], preferred_element_type=jnp.float32)
            up += jnp.dot(x, w[1], preferred_element_type=jnp.float32)
        coef = coef_ref[top : top + tile, :1]
        hidden = gate / (1.0 + jnp.exp(-gate)) * up * coef
        out_ref[top : top + tile] = hidden.astype(out_ref.dtype)


def hidden_of(pieces, weights):
    _, depth, ff = weights[0].shape
    block = 256
    tall, wide = pieces[0].shape
    rows = tall * len(pieces)
    return pl.pallas_call(
        functools.partial(hidden_kernel, len(pieces)),
        grid=(ff // block,),
        in_specs=[pl.BlockSpec((tall, wide), lambda f: (0, 0))] * len(pieces)
        + [pl.BlockSpec((2, depth, block), lambda f: (0, 0, f))] * len(weights),
        out_specs=pl.BlockSpec((rows, block), lambda f: (0, f)),
        out_shape=jax.ShapeDtypeStruct((rows, ff), pieces[0].dtype),
        scratch_shapes=[
            pltpu.VMEM((rows, wide - LANES), pieces[0].dtype),
            pltpu.VMEM((rows, LANES), jnp.float32),
        ],
        compiler_params=params(),
        cost_estimate=pl.CostEstimate(flops=1, bytes_accessed=1, transcendentals=0),
    )(*pieces, *weights)


def down_kernel(n_downs, hidden_ref, *refs):
    downs, (kept_ref, sent_ref) = refs[:n_downs], refs[-2:]
    depth = downs[0].shape[0]
    rows = kept_ref.shape[0]
    tile = min(rows, 512)
    contract = (((1,), (1,)), ((), ()))
    for i, w in enumerate(downs):
        for out, base in ((kept_ref, 0), (sent_ref, rows)):
            for top in range(0, rows, tile):
                part = lax.dot_general(
                    hidden_ref[base + top : base + top + tile], w[...], contract,
                    preferred_element_type=jnp.float32,
                )
                out[top : top + tile, i * depth : (i + 1) * depth] = part.astype(out.dtype)


def down_of(hidden, downs, after):
    depth, ff = downs[0].shape
    rows = hidden.shape[0] // 2
    vmem = pl.BlockSpec(memory_space=pltpu.VMEM)
    out = jax.ShapeDtypeStruct((rows, len(downs) * depth), hidden.dtype)
    return pl.pallas_call(
        functools.partial(down_kernel, len(downs)),
        in_specs=[vmem] * (1 + len(downs)) + [pl.BlockSpec(memory_space=pl.ANY)] * len(after),
        out_specs=(vmem, vmem),
        out_shape=(out, out),
        compiler_params=params(),
        cost_estimate=pl.CostEstimate(flops=1, bytes_accessed=1, transcendentals=0),
    )(hidden, *downs, *after)


def over_core(kept, sent):
    return kept.astype(jnp.float32) + swap(sent, "shard", 1).astype(jnp.float32)


def over_x(total, tok):
    total = total.reshape(-1, 2, tok, total.shape[-1])
    given = swap(total[:, 1].astype(jnp.bfloat16), "dp", 1)
    return total[:, 0] + given.astype(jnp.float32)


def over_z(total):
    while total.shape[0] > 1:
        half = total.shape[0] // 2
        given = flip_z(total[half:].astype(jnp.bfloat16), half)
        total = total[:half] + given.astype(jnp.float32)
    return total[0].astype(jnp.bfloat16)


def place_kernel(depth, *refs):
    parts, out_ref = refs[:-1], refs[-1]
    pair, _, _ = position()
    for part, blocks in zip(parts, out_blocks(depth, [p.shape[1] for p in parts])):
        for n, (j, core) in enumerate(blocks):
            start = pl.multiple_of((2 * (pair ^ j) + core) * depth, LANES)
            out_ref[:, pl.ds(start, depth)] = part[:, n * depth : (n + 1) * depth]


def out_blocks(depth, widths):
    others = range(1, widths[1] // depth + 1)
    return [[(0, 0), (0, 1)] + [(j, 0) for j in others], [(j, 1) for j in others]]


def placed(parts, depth, width):
    vmem = pl.BlockSpec(memory_space=pltpu.VMEM)
    return pl.pallas_call(
        functools.partial(place_kernel, depth),
        in_specs=[vmem] * len(parts),
        out_specs=vmem,
        out_shape=jax.ShapeDtypeStruct((parts[0].shape[0], width), parts[0].dtype),
        compiler_params=params(),
        cost_estimate=NOTHING,
    )(*parts)


def local(tokens, router_probs, expert_ids, old_place, new_place, w_gate, w_up, w_down):
    tok, width = tokens.shape
    depth = w_gate.shape[1]
    n_z = lax.axis_size("dp") // 2
    places = (old_place, new_place)

    (mine,) = copies(((0, "mine", 0, 0), (1, "mine", 0, 1)), places, (w_gate, w_up), (2,))
    theirs, theirs_down = copies(
        ((0, "theirs", 0, 0), (1, "theirs", 0, 1), (2, "theirs", 1, 0)),
        places, (w_gate, w_up, w_down), (2, 1),
    )
    near_weights = [mine, swap(theirs, "shard", 1)]
    weights = spread(near_weights)
    downs = [spread([d]) for d in in_order(w_down, swap(theirs_down, "shard", 1))]

    own = first(tokens, router_probs, expert_ids, old_place)
    columns = [own] + [flip_z(own, j) for j in range(1, n_z)]
    across = [swap(c, "dp", 1) for c in columns]
    near = [joined(jnp.concatenate(p, axis=0), weights[2]) for p in zip(columns, across)]
    far = [swap(p, "shard", 1) for p in near]

    hidden = hidden_of(near + far, weights)
    (leave,) = copies(
        tuple((i, "leaves", 0, i) for i in range(3)), places, (w_gate, w_up, w_down), (3,), across
    )
    arrive = passed_along(leave, "dp", 1)
    news = copies(
        tuple((0, i, i, "leaves") for i in range(3))
        + tuple((i + 1, "stays", i, "stays") for i in range(3)),
        places, (arrive, w_gate, w_up, w_down), (2, 2, 2),
    )

    groups = [[d[0] for d in downs]] + [d[1:] for d in downs]
    kept, sent = down_of(hidden, groups[0], ())
    at_core = over_core(kept, sent)
    kept, sent = down_of(hidden, groups[1], (sent,))
    at_x = over_x(at_core, tok)
    at_core = over_core(kept, sent)
    at_x2 = over_x(at_core, tok)
    kept, last = down_of(hidden, groups[2], (sent, news[0], at_x, at_x2))
    early = over_z(jnp.concatenate([at_x, at_x2], axis=-1))
    parts = [early, over_z(over_x(over_core(kept, last), tok))]
    moe_output = placed(parts, depth, width)

    return (moe_output, *news)


def solution(mesh):
    in_specs = (
        P(("dp", "shard"), None),
        P(("dp", "shard"), None),
        P(("dp", "shard"), None),
        P(),
        P(),
        P("dp", "shard", None),
        P("dp", "shard", None),
        P("dp", "shard", None),
    )
    out_specs = (
        P(("dp", "shard"), None),
        P("dp", "shard", None),
        P("dp", "shard", None),
        P("dp", "shard", None),
    )
    return jax.shard_map(local, mesh=mesh, in_specs=in_specs, out_specs=out_specs, check_vma=False)
```

```python
import functools

import jax
import jax.numpy as jnp
from jax import lax
from jax.experimental import pallas as pl
from jax.experimental.pallas import tpu as pltpu
from jax.sharding import PartitionSpec as P

LANES = 128
VMEM_BYTES = 32 * 1024 * 1024
MOST = 56 * 1024 * 1024
NOTHING = pl.CostEstimate(flops=0, bytes_accessed=0, transcendentals=0)


def swap(x, axis, bit):
    return lax.ppermute(x, axis, [(i, i ^ bit) for i in range(lax.axis_size(axis))])


def passed_along(x, axis, by):
    size = lax.axis_size(axis)
    return lax.ppermute(x, axis, [(i, (i + by) % size) for i in range(size)])


def flip_z(x, bits):
    return swap(x, "dp", 2 * bits)


def spread(pieces):
    bit = 2
    while bit < lax.axis_size("shard"):
        pieces = pieces + [swap(p, "shard", bit) for p in pieces]
        bit *= 2
    return pieces


def params(amount=VMEM_BYTES):
    return pltpu.CompilerParams(vmem_limit_bytes=amount)


def position():
    column = lax.axis_index("shard")
    return lax.div(column, 2), lax.rem(column, 2), lax.axis_index("dp")


def first_kernel(tokens_ref, probs_ref, ids_ref, place_ref, out_ref, coef_ref):
    probs = probs_ref[...]
    weights = (probs / jnp.sum(probs, axis=0, keepdims=True)).astype(jnp.bfloat16)
    weights = weights.astype(jnp.float32)
    ids = ids_ref[...]
    tok, width = tokens_ref.shape
    coef_ref[...] = jnp.zeros_like(coef_ref)
    for slot in range(place_ref.shape[0]):
        named = jnp.where(ids == place_ref[slot], weights, 0.0)
        coef_ref[slot : slot + 1, :tok] = jnp.sum(named, axis=0, keepdims=True)
    out_ref[:, :width] = tokens_ref[...]
    out_ref[:, width:] = jnp.transpose(coef_ref[...])[:tok].astype(jnp.bfloat16)


def first(tokens, probs, ids, old_place):
    vmem = pl.BlockSpec(memory_space=pltpu.VMEM)
    return pl.pallas_call(
        first_kernel,
        in_specs=[vmem] * 3 + [pl.BlockSpec(memory_space=pltpu.SMEM)],
        out_specs=vmem,
        out_shape=jax.ShapeDtypeStruct((tokens.shape[0], tokens.shape[1] + LANES), tokens.dtype),
        scratch_shapes=[pltpu.VMEM((LANES, LANES), jnp.float32)],
        compiler_params=params(),
        cost_estimate=NOTHING,
    )(tokens, probs.T, ids.T, old_place)


def copy_kernel(plan, n_in, n_out, *refs):
    old_ref, new_ref = refs[:2]
    ins, refs = refs[2 : 2 + n_in], refs[-n_out - 3 :]
    outs, (held, in_sems, out_sems) = refs[:n_out], refs[n_out:]
    _, core, row = position()
    second = 2 * row + 1
    moved = (old_ref[second] != new_ref[second]).astype(jnp.int32)
    slots = {"mine": core, "theirs": 1 - core, "leaves": moved, "stays": 1 - moved}
    slots.update({i: i for i in range(3)})
    loads = [
        pltpu.make_async_copy(ins[i].at[slots[a]], held.at[n], in_sems.at[n])
        for n, (i, a, o, b) in enumerate(plan)
    ]
    stores = [
        pltpu.make_async_copy(held.at[n], outs[o].at[slots[b]], out_sems.at[n])
        for n, (i, a, o, b) in enumerate(plan)
    ]
    for c in loads:
        c.start()
    for n, c in enumerate(stores):
        loads[n].wait()
        c.start()
    for c in stores:
        c.wait()


def copies(plan, places, ins, counts, after=(), aliases=()):
    slot, kind = ins[0].shape[1:], ins[0].dtype
    smem, anywhere = pl.BlockSpec(memory_space=pltpu.SMEM), pl.BlockSpec(memory_space=pl.ANY)
    return pl.pallas_call(
        functools.partial(copy_kernel, plan, len(ins), len(counts)),
        in_specs=[smem] * 2 + [anywhere] * (len(ins) + len(aliases) + len(after)),
        out_specs=(anywhere,) * len(counts),
        out_shape=tuple(jax.ShapeDtypeStruct((n,) + slot, kind) for n in counts),
        input_output_aliases={2 + len(ins) + i: i for i in range(len(aliases))},
        scratch_shapes=[
            pltpu.VMEM((len(plan),) + slot, kind),
            pltpu.SemaphoreType.DMA((len(plan),)),
            pltpu.SemaphoreType.DMA((len(plan),)),
        ],
        compiler_params=params(MOST),
        cost_estimate=NOTHING,
    )(*places, *ins, *aliases, *after)


def order_kernel(mine_ref, other_ref, first_ref, second_ref, held, in_sems, out_sems):
    _, core, _ = position()
    loads = [
        pltpu.make_async_copy(mine_ref.at[core], held.at[core], in_sems.at[0]),
        pltpu.make_async_copy(other_ref.at[0], held.at[1 - core], in_sems.at[1]),
    ]
    stores = [
        pltpu.make_async_copy(held.at[n], out, out_sems.at[n])
        for n, out in enumerate((first_ref, second_ref))
    ]
    for c in loads:
        c.start()
    for c in loads:
        c.wait()
    for c in stores:
        c.start()
    for c in stores:
        c.wait()


def in_order(w_down, other):
    anywhere = pl.BlockSpec(memory_space=pl.ANY)
    slot = w_down.shape[1:]
    return pl.pallas_call(
        order_kernel,
        in_specs=[anywhere] * 2,
        out_specs=(anywhere,) * 2,
        out_shape=(jax.ShapeDtypeStruct(slot, w_down.dtype),) * 2,
        scratch_shapes=[
            pltpu.VMEM((2,) + slot, w_down.dtype),
            pltpu.SemaphoreType.DMA((2,)),
            pltpu.SemaphoreType.DMA((2,)),
        ],
        compiler_params=params(MOST),
        cost_estimate=NOTHING,
    )(w_down, other)


def join_kernel(*refs):
    pass


def joined(x, *after):
    anywhere = pl.BlockSpec(memory_space=pl.ANY)
    return pl.pallas_call(
        join_kernel,
        in_specs=[anywhere] * (1 + len(after)),
        out_specs=anywhere,
        out_shape=jax.ShapeDtypeStruct(x.shape, x.dtype),
        input_output_aliases={0: 0},
        compiler_params=params(),
        cost_estimate=NOTHING,
    )(x, *after)


def hidden_kernel(n_pieces, *refs):
    pieces, weights, (out_ref, x_ref, coef_ref) = refs[:n_pieces], refs[n_pieces:-3], refs[-3:]
    _, depth, block = weights[0].shape
    rows, width = x_ref.shape
    tall = rows // n_pieces
    pair, core, row = position()

    @pl.when(pl.program_id(0) == 0)
    def _():
        for n, p in enumerate(pieces):
            x_ref[n * tall : (n + 1) * tall] = p[:, :width]
            coef = p[:, width:].astype(jnp.float32)
            lane = lax.broadcasted_iota(jnp.int32, coef.shape, 1)
            coef = jnp.sum(jnp.where(lane == 2 * row + core, coef, 0.0), axis=1, keepdims=True)
            coef_ref[n * tall : (n + 1) * tall] = jnp.broadcast_to(coef, (tall, LANES))

    tile = min(rows, 512)
    for top in range(0, rows, tile):
        gate = jnp.zeros((tile, block), jnp.float32)
        up = jnp.zeros((tile, block), jnp.float32)
        for i, w in enumerate(weights):
            start = (2 * (pair ^ (i // 2)) + (core ^ (i % 2))) * depth
            x = x_ref[top : top + tile, pl.ds(pl.multiple_of(start, LANES), depth)]
            gate += jnp.dot(x, w[0], preferred_element_type=jnp.float32)
            up += jnp.dot(x, w[1], preferred_element_type=jnp.float32)
        coef = coef_ref[top : top + tile, :1]
        hidden = gate / (1.0 + jnp.exp(-gate)) * up * coef
        out_ref[top : top + tile] = hidden.astype(out_ref.dtype)


def hidden_of(pieces, weights):
    _, depth, ff = weights[0].shape
    block = 256
    tall, wide = pieces[0].shape
    rows = tall * len(pieces)
    return pl.pallas_call(
        functools.partial(hidden_kernel, len(pieces)),
        grid=(ff // block,),
        in_specs=[pl.BlockSpec((tall, wide), lambda f: (0, 0))] * len(pieces)
        + [pl.BlockSpec((2, depth, block), lambda f: (0, 0, f))] * len(weights),
        out_specs=pl.BlockSpec((rows, block), lambda f: (0, f)),
        out_shape=jax.ShapeDtypeStruct((rows, ff), pieces[0].dtype),
        scratch_shapes=[
            pltpu.VMEM((rows, wide - LANES), pieces[0].dtype),
            pltpu.VMEM((rows, LANES), jnp.float32),
        ],
        compiler_params=params(),
        cost_estimate=pl.CostEstimate(flops=1, bytes_accessed=1, transcendentals=0),
    )(*pieces, *weights)


def down_kernel(n_downs, hidden_ref, *refs):
    downs, (kept_ref, sent_ref) = refs[:n_downs], refs[-2:]
    depth = downs[0].shape[0]
    rows = kept_ref.shape[0]
    tile = min(rows, 512)
    contract = (((1,), (1,)), ((), ()))
    for i, w in enumerate(downs):
        for out, base in ((kept_ref, 0), (sent_ref, rows)):
            for top in range(0, rows, tile):
                part = lax.dot_general(
                    hidden_ref[base + top : base + top + tile], w[...], contract,
                    preferred_element_type=jnp.float32,
                )
                out[top : top + tile, i * depth : (i + 1) * depth] = part.astype(out.dtype)


def down_of(hidden, downs, after):
    depth, ff = downs[0].shape
    rows = hidden.shape[0] // 2
    vmem = pl.BlockSpec(memory_space=pltpu.VMEM)
    out = jax.ShapeDtypeStruct((rows, len(downs) * depth), hidden.dtype)
    return pl.pallas_call(
        functools.partial(down_kernel, len(downs)),
        in_specs=[vmem] * (1 + len(downs)) + [pl.BlockSpec(memory_space=pl.ANY)] * len(after),
        out_specs=(vmem, vmem),
        out_shape=(out, out),
        compiler_params=params(),
        cost_estimate=pl.CostEstimate(flops=1, bytes_accessed=1, transcendentals=0),
    )(hidden, *downs, *after)


def over_core(kept, sent):
    return kept.astype(jnp.float32) + swap(sent, "shard", 1).astype(jnp.float32)


def over_x(total, tok):
    total = total.reshape(-1, 2, tok, total.shape[-1])
    given = swap(total[:, 1].astype(jnp.bfloat16), "dp", 1)
    return total[:, 0] + given.astype(jnp.float32)


def over_z(total):
    while total.shape[0] > 1:
        half = total.shape[0] // 2
        given = flip_z(total[half:].astype(jnp.bfloat16), half)
        total = total[:half] + given.astype(jnp.float32)
    return total[0].astype(jnp.bfloat16)


def place_kernel(depth, *refs):
    parts, out_ref = refs[:-1], refs[-1]
    pair, _, _ = position()
    for part, blocks in zip(parts, out_blocks(depth, [p.shape[1] for p in parts])):
        for n, (j, core) in enumerate(blocks):
            start = pl.multiple_of((2 * (pair ^ j) + core) * depth, LANES)
            out_ref[:, pl.ds(start, depth)] = part[:, n * depth : (n + 1) * depth]


def out_blocks(depth, widths):
    others = range(1, widths[1] // depth + 1)
    return [[(0, 0), (0, 1)] + [(j, 0) for j in others], [(j, 1) for j in others]]


def placed(parts, depth, width):
    vmem = pl.BlockSpec(memory_space=pltpu.VMEM)
    return pl.pallas_call(
        functools.partial(place_kernel, depth),
        in_specs=[vmem] * len(parts),
        out_specs=vmem,
        out_shape=jax.ShapeDtypeStruct((parts[0].shape[0], width), parts[0].dtype),
        compiler_params=params(),
        cost_estimate=NOTHING,
    )(*parts)


def local(tokens, router_probs, expert_ids, old_place, new_place, w_gate, w_up, w_down):
    tok, width = tokens.shape
    depth = w_gate.shape[1]
    n_z = lax.axis_size("dp") // 2
    places = (old_place, new_place)

    (mine,) = copies(((0, "mine", 0, 0), (1, "mine", 0, 1)), places, (w_gate, w_up), (2,))
    theirs, theirs_down = copies(
        ((0, "theirs", 0, 0), (1, "theirs", 0, 1), (2, "theirs", 1, 0)),
        places, (w_gate, w_up, w_down), (2, 1),
    )
    near_weights = [mine, swap(theirs, "shard", 1)]
    weights = spread(near_weights)
    downs = [spread([d]) for d in in_order(w_down, swap(theirs_down, "shard", 1))]

    own = first(tokens, router_probs, expert_ids, old_place)
    columns = [own] + [flip_z(own, j) for j in range(1, n_z)]
    across = [swap(own, "dp", 1)]
    for c in columns[1:]:
        across.append(swap(joined(c, across[-1]), "dp", 1))
    near = [joined(jnp.concatenate(p, axis=0), weights[2]) for p in zip(columns, across)]
    far = [swap(p, "shard", 1) for p in near]

    hidden = hidden_of(near + far, weights)
    (leave,) = copies(
        tuple((i, "leaves", 0, i) for i in range(3)), places, (w_gate, w_up, w_down), (3,), across
    )
    arrive = passed_along(leave, "dp", 1)
    news = copies(
        tuple((0, i, i, "leaves") for i in range(3))
        + tuple((i + 1, "stays", i, "stays") for i in range(3)),
        places, (arrive, w_gate, w_up, w_down), (2, 2, 2),
    )

    groups = [[d[0] for d in downs]] + [d[1:] for d in downs]
    kept, sent = down_of(hidden, groups[0], ())
    at_core = over_core(kept, sent)
    kept, sent = down_of(hidden, groups[1], (sent,))
    at_x = over_x(at_core, tok)
    at_core = over_core(kept, sent)
    at_x2 = over_x(at_core, tok)
    kept, last = down_of(hidden, groups[2], (sent, news[0], at_x, at_x2))
    early = over_z(jnp.concatenate([at_x, at_x2], axis=-1))
    parts = [early, over_z(over_x(over_core(kept, last), tok))]
    moe_output = placed(parts, depth, width)

    return (moe_output, *news)


def solution(mesh):
    in_specs = (
        P(("dp", "shard"), None),
        P(("dp", "shard"), None),
        P(("dp", "shard"), None),
        P(),
        P(),
        P("dp", "shard", None),
        P("dp", "shard", None),
        P("dp", "shard", None),
    )
    out_specs = (
        P(("dp", "shard"), None),
        P("dp", "shard", None),
        P("dp", "shard", None),
        P("dp", "shard", None),
    )
    return jax.shard_map(local, mesh=mesh, in_specs=in_specs, out_specs=out_specs, check_vma=False)
```

```python
import functools

import jax
import jax.numpy as jnp
from jax import lax
from jax.experimental import pallas as pl
from jax.experimental.pallas import tpu as pltpu
from jax.sharding import PartitionSpec as P

LANES = 128
VMEM_BYTES = 32 * 1024 * 1024
MOST = 56 * 1024 * 1024
NOTHING = pl.CostEstimate(flops=0, bytes_accessed=0, transcendentals=0)


def swap(x, axis, bit):
    return lax.ppermute(x, axis, [(i, i ^ bit) for i in range(lax.axis_size(axis))])


def passed_along(x, axis, by):
    size = lax.axis_size(axis)
    return lax.ppermute(x, axis, [(i, (i + by) % size) for i in range(size)])


def flip_z(x, bits):
    return swap(x, "dp", 2 * bits)


def spread(pieces):
    bit = 2
    while bit < lax.axis_size("shard"):
        pieces = pieces + [swap(p, "shard", bit) for p in pieces]
        bit *= 2
    return pieces


def params(amount=VMEM_BYTES):
    return pltpu.CompilerParams(vmem_limit_bytes=amount)


def position():
    column = lax.axis_index("shard")
    return lax.div(column, 2), lax.rem(column, 2), lax.axis_index("dp")


def first_kernel(tokens_ref, probs_ref, ids_ref, place_ref, out_ref, coef_ref):
    probs = probs_ref[...]
    weights = (probs / jnp.sum(probs, axis=0, keepdims=True)).astype(jnp.bfloat16)
    weights = weights.astype(jnp.float32)
    ids = ids_ref[...]
    tok, width = tokens_ref.shape
    coef_ref[...] = jnp.zeros_like(coef_ref)
    for slot in range(place_ref.shape[0]):
        named = jnp.where(ids == place_ref[slot], weights, 0.0)
        coef_ref[slot : slot + 1, :tok] = jnp.sum(named, axis=0, keepdims=True)
    out_ref[:, :width] = tokens_ref[...]
    out_ref[:, width:] = jnp.transpose(coef_ref[...])[:tok].astype(jnp.bfloat16)


def first(tokens, probs, ids, old_place):
    vmem = pl.BlockSpec(memory_space=pltpu.VMEM)
    return pl.pallas_call(
        first_kernel,
        in_specs=[vmem] * 3 + [pl.BlockSpec(memory_space=pltpu.SMEM)],
        out_specs=vmem,
        out_shape=jax.ShapeDtypeStruct((tokens.shape[0], tokens.shape[1] + LANES), tokens.dtype),
        scratch_shapes=[pltpu.VMEM((LANES, LANES), jnp.float32)],
        compiler_params=params(),
        cost_estimate=NOTHING,
    )(tokens, probs.T, ids.T, old_place)


def copy_kernel(plan, n_in, n_out, *refs):
    old_ref, new_ref = refs[:2]
    ins, refs = refs[2 : 2 + n_in], refs[-n_out - 3 :]
    outs, (held, in_sems, out_sems) = refs[:n_out], refs[n_out:]
    _, core, row = position()
    second = 2 * row + 1
    moved = (old_ref[second] != new_ref[second]).astype(jnp.int32)
    slots = {"mine": core, "theirs": 1 - core, "leaves": moved, "stays": 1 - moved}
    slots.update({i: i for i in range(3)})
    loads = [
        pltpu.make_async_copy(ins[i].at[slots[a]], held.at[n], in_sems.at[n])
        for n, (i, a, o, b) in enumerate(plan)
    ]
    stores = [
        pltpu.make_async_copy(held.at[n], outs[o].at[slots[b]], out_sems.at[n])
        for n, (i, a, o, b) in enumerate(plan)
    ]
    for c in loads:
        c.start()
    for n, c in enumerate(stores):
        loads[n].wait()
        c.start()
    for c in stores:
        c.wait()


def copies(plan, places, ins, counts, after=(), aliases=()):
    slot, kind = ins[0].shape[1:], ins[0].dtype
    smem, anywhere = pl.BlockSpec(memory_space=pltpu.SMEM), pl.BlockSpec(memory_space=pl.ANY)
    return pl.pallas_call(
        functools.partial(copy_kernel, plan, len(ins), len(counts)),
        in_specs=[smem] * 2 + [anywhere] * (len(ins) + len(aliases) + len(after)),
        out_specs=(anywhere,) * len(counts),
        out_shape=tuple(jax.ShapeDtypeStruct((n,) + slot, kind) for n in counts),
        input_output_aliases={2 + len(ins) + i: i for i in range(len(aliases))},
        scratch_shapes=[
            pltpu.VMEM((len(plan),) + slot, kind),
            pltpu.SemaphoreType.DMA((len(plan),)),
            pltpu.SemaphoreType.DMA((len(plan),)),
        ],
        compiler_params=params(MOST),
        cost_estimate=NOTHING,
    )(*places, *ins, *aliases, *after)


def order_kernel(mine_ref, other_ref, first_ref, second_ref, held, in_sems, out_sems):
    _, core, _ = position()
    loads = [
        pltpu.make_async_copy(mine_ref.at[core], held.at[core], in_sems.at[0]),
        pltpu.make_async_copy(other_ref.at[0], held.at[1 - core], in_sems.at[1]),
    ]
    stores = [
        pltpu.make_async_copy(held.at[n], out, out_sems.at[n])
        for n, out in enumerate((first_ref, second_ref))
    ]
    for c in loads:
        c.start()
    for c in loads:
        c.wait()
    for c in stores:
        c.start()
    for c in stores:
        c.wait()


def in_order(w_down, other):
    anywhere = pl.BlockSpec(memory_space=pl.ANY)
    slot = w_down.shape[1:]
    return pl.pallas_call(
        order_kernel,
        in_specs=[anywhere] * 2,
        out_specs=(anywhere,) * 2,
        out_shape=(jax.ShapeDtypeStruct(slot, w_down.dtype),) * 2,
        scratch_shapes=[
            pltpu.VMEM((2,) + slot, w_down.dtype),
            pltpu.SemaphoreType.DMA((2,)),
            pltpu.SemaphoreType.DMA((2,)),
        ],
        compiler_params=params(MOST),
        cost_estimate=NOTHING,
    )(w_down, other)


def join_kernel(*refs):
    pass


def joined(x, *after):
    anywhere = pl.BlockSpec(memory_space=pl.ANY)
    return pl.pallas_call(
        join_kernel,
        in_specs=[anywhere] * (1 + len(after)),
        out_specs=anywhere,
        out_shape=jax.ShapeDtypeStruct(x.shape, x.dtype),
        input_output_aliases={0: 0},
        compiler_params=params(),
        cost_estimate=NOTHING,
    )(x, *after)


def hidden_kernel(n_pieces, *refs):
    pieces, weights, (out_ref, x_ref, coef_ref) = refs[:n_pieces], refs[n_pieces:-3], refs[-3:]
    _, depth, block = weights[0].shape
    rows, width = x_ref.shape
    tall = rows // n_pieces
    pair, core, row = position()

    @pl.when(pl.program_id(0) == 0)
    def _():
        for n, p in enumerate(pieces):
            x_ref[n * tall : (n + 1) * tall] = p[:, :width]
            coef = p[:, width:].astype(jnp.float32)
            lane = lax.broadcasted_iota(jnp.int32, coef.shape, 1)
            coef = jnp.sum(jnp.where(lane == 2 * row + core, coef, 0.0), axis=1, keepdims=True)
            coef_ref[n * tall : (n + 1) * tall] = jnp.broadcast_to(coef, (tall, LANES))

    tile = min(rows, 512)
    for top in range(0, rows, tile):
        gate = jnp.zeros((tile, block), jnp.float32)
        up = jnp.zeros((tile, block), jnp.float32)
        for i, w in enumerate(weights):
            start = (2 * (pair ^ (i // 2)) + (core ^ (i % 2))) * depth
            x = x_ref[top : top + tile, pl.ds(pl.multiple_of(start, LANES), depth)]
            gate += jnp.dot(x, w[0], preferred_element_type=jnp.float32)
            up += jnp.dot(x, w[1], preferred_element_type=jnp.float32)
        coef = coef_ref[top : top + tile, :1]
        hidden = gate / (1.0 + jnp.exp(-gate)) * up * coef
        out_ref[top : top + tile] = hidden.astype(out_ref.dtype)


def hidden_of(pieces, weights):
    _, depth, ff = weights[0].shape
    block = 256
    tall, wide = pieces[0].shape
    rows = tall * len(pieces)
    return pl.pallas_call(
        functools.partial(hidden_kernel, len(pieces)),
        grid=(ff // block,),
        in_specs=[pl.BlockSpec((tall, wide), lambda f: (0, 0))] * len(pieces)
        + [pl.BlockSpec((2, depth, block), lambda f: (0, 0, f))] * len(weights),
        out_specs=pl.BlockSpec((rows, block), lambda f: (0, f)),
        out_shape=jax.ShapeDtypeStruct((rows, ff), pieces[0].dtype),
        scratch_shapes=[
            pltpu.VMEM((rows, wide - LANES), pieces[0].dtype),
            pltpu.VMEM((rows, LANES), jnp.float32),
        ],
        compiler_params=params(),
        cost_estimate=pl.CostEstimate(flops=1, bytes_accessed=1, transcendentals=0),
    )(*pieces, *weights)


def down_kernel(n_downs, hidden_ref, *refs):
    downs, (kept_ref, sent_ref) = refs[:n_downs], refs[-2:]
    depth = downs[0].shape[0]
    rows = kept_ref.shape[0]
    tile = min(rows, 512)
    contract = (((1,), (1,)), ((), ()))
    for i, w in enumerate(downs):
        for out, base in ((kept_ref, 0), (sent_ref, rows)):
            for top in range(0, rows, tile):
                part = lax.dot_general(
                    hidden_ref[base + top : base + top + tile], w[...], contract,
                    preferred_element_type=jnp.float32,
                )
                out[top : top + tile, i * depth : (i + 1) * depth] = part.astype(out.dtype)


def down_of(hidden, downs, after):
    depth, ff = downs[0].shape
    rows = hidden.shape[0] // 2
    vmem = pl.BlockSpec(memory_space=pltpu.VMEM)
    out = jax.ShapeDtypeStruct((rows, len(downs) * depth), hidden.dtype)
    return pl.pallas_call(
        functools.partial(down_kernel, len(downs)),
        in_specs=[vmem] * (1 + len(downs)) + [pl.BlockSpec(memory_space=pl.ANY)] * len(after),
        out_specs=(vmem, vmem),
        out_shape=(out, out),
        compiler_params=params(),
        cost_estimate=pl.CostEstimate(flops=1, bytes_accessed=1, transcendentals=0),
    )(hidden, *downs, *after)


def over_core(kept, sent):
    return kept.astype(jnp.float32) + swap(sent, "shard", 1).astype(jnp.float32)


def over_x(total, tok):
    total = total.reshape(-1, 2, tok, total.shape[-1])
    given = swap(total[:, 1].astype(jnp.bfloat16), "dp", 1)
    return total[:, 0] + given.astype(jnp.float32)


def over_z(total):
    bit = 1
    while total.shape[0] > 1:
        pairs = total.reshape((-1, 2) + total.shape[1:])
        given = flip_z(pairs[:, 1].astype(jnp.bfloat16), bit)
        total = pairs[:, 0] + given.astype(jnp.float32)
        bit *= 2
    return total[0].astype(jnp.bfloat16)


def place_kernel(depth, *refs):
    parts, out_ref = refs[:-1], refs[-1]
    pair, _, _ = position()
    for part, blocks in zip(parts, out_blocks(depth, [p.shape[1] for p in parts])):
        for n, (j, core) in enumerate(blocks):
            start = pl.multiple_of((2 * (pair ^ j) + core) * depth, LANES)
            out_ref[:, pl.ds(start, depth)] = part[:, n * depth : (n + 1) * depth]


def out_blocks(depth, widths):
    others = range(1, widths[1] // depth + 1)
    return [[(0, 0), (0, 1)] + [(j, 0) for j in others], [(j, 1) for j in others]]


def placed(parts, depth, width):
    vmem = pl.BlockSpec(memory_space=pltpu.VMEM)
    return pl.pallas_call(
        functools.partial(place_kernel, depth),
        in_specs=[vmem] * len(parts),
        out_specs=vmem,
        out_shape=jax.ShapeDtypeStruct((parts[0].shape[0], width), parts[0].dtype),
        compiler_params=params(),
        cost_estimate=NOTHING,
    )(*parts)


def local(tokens, router_probs, expert_ids, old_place, new_place, w_gate, w_up, w_down):
    tok, width = tokens.shape
    depth = w_gate.shape[1]
    n_z = lax.axis_size("dp") // 2
    places = (old_place, new_place)

    mine, theirs, theirs_down = copies(
        ((0, "mine", 0, 0), (1, "mine", 0, 1))
        + ((0, "theirs", 1, 0), (1, "theirs", 1, 1), (2, "theirs", 2, 0)),
        places, (w_gate, w_up, w_down), (2, 2, 1),
    )
    near_weights = [mine, swap(theirs, "shard", 1)]
    weights = spread(near_weights)
    downs = [spread([d]) for d in in_order(w_down, swap(theirs_down, "shard", 1))]

    own = first(tokens, router_probs, expert_ids, old_place)
    columns = [own] + [flip_z(own, j) for j in range(1, n_z)]
    across = [swap(own, "dp", 1)]
    for c in columns[1:]:
        across.append(swap(joined(c, across[-1]), "dp", 1))
    near = [joined(jnp.concatenate(p, axis=0), weights[2]) for p in zip(columns, across)]
    far = [swap(p, "shard", 1) for p in near]

    hidden = hidden_of(near + far, weights)
    (leave,) = copies(
        tuple((i, "leaves", 0, i) for i in range(3)), places, (w_gate, w_up, w_down), (3,), across
    )
    arrive = passed_along(leave, "dp", 1)
    news = copies(
        tuple((0, i, i, "leaves") for i in range(3))
        + tuple((i + 1, "stays", i, "stays") for i in range(3)),
        places, (arrive, w_gate, w_up, w_down), (2, 2, 2),
    )

    groups = [[d[0] for d in downs]] + [d[1:] for d in downs]
    kept, sent = down_of(hidden, groups[0], ())
    at_core = over_core(kept, sent)
    kept, sent = down_of(hidden, groups[1], (sent,))
    at_x = over_x(at_core, tok)
    at_core = over_core(kept, sent)
    at_x2 = over_x(at_core, tok)
    kept, last = down_of(hidden, groups[2], (sent, news[0], at_x, at_x2))
    early = over_z(jnp.concatenate([at_x, at_x2], axis=-1))
    parts = [early, over_z(over_x(over_core(kept, last), tok))]
    moe_output = placed(parts, depth, width)

    return (moe_output, *news)


def solution(mesh):
    in_specs = (
        P(("dp", "shard"), None),
        P(("dp", "shard"), None),
        P(("dp", "shard"), None),
        P(),
        P(),
        P("dp", "shard", None),
        P("dp", "shard", None),
        P("dp", "shard", None),
    )
    out_specs = (
        P(("dp", "shard"), None),
        P("dp", "shard", None),
        P("dp", "shard", None),
        P("dp", "shard", None),
    )
    return jax.shard_map(local, mesh=mesh, in_specs=in_specs, out_specs=out_specs, check_vma=False)
```

```python
import functools

import jax
import jax.numpy as jnp
from jax import lax
from jax.experimental import pallas as pl
from jax.experimental.pallas import tpu as pltpu
from jax.sharding import PartitionSpec as P

LANES = 128
VMEM_BYTES = 32 * 1024 * 1024
MOST = 56 * 1024 * 1024
NOTHING = pl.CostEstimate(flops=0, bytes_accessed=0, transcendentals=0)


def swap(x, axis, bit):
    return lax.ppermute(x, axis, [(i, i ^ bit) for i in range(lax.axis_size(axis))])


def passed_along(x, axis, by):
    size = lax.axis_size(axis)
    return lax.ppermute(x, axis, [(i, (i + by) % size) for i in range(size)])


def flip_z(x, bits):
    return swap(x, "dp", 2 * bits)


def spread(pieces):
    bit = 2
    while bit < lax.axis_size("shard"):
        pieces = pieces + [swap(p, "shard", bit) for p in pieces]
        bit *= 2
    return pieces


def params(amount=VMEM_BYTES):
    return pltpu.CompilerParams(vmem_limit_bytes=amount)


def position():
    column = lax.axis_index("shard")
    return lax.div(column, 2), lax.rem(column, 2), lax.axis_index("dp")


def first_kernel(tokens_ref, probs_ref, ids_ref, place_ref, out_ref, coef_ref):
    probs = probs_ref[...]
    weights = (probs / jnp.sum(probs, axis=0, keepdims=True)).astype(jnp.bfloat16)
    weights = weights.astype(jnp.float32)
    ids = ids_ref[...]
    tok, width = tokens_ref.shape
    coef_ref[...] = jnp.zeros_like(coef_ref)
    for slot in range(place_ref.shape[0]):
        named = jnp.where(ids == place_ref[slot], weights, 0.0)
        coef_ref[slot : slot + 1, :tok] = jnp.sum(named, axis=0, keepdims=True)
    out_ref[:, :width] = tokens_ref[...]
    out_ref[:, width:] = jnp.transpose(coef_ref[...])[:tok].astype(jnp.bfloat16)


def first(tokens, probs, ids, old_place):
    vmem = pl.BlockSpec(memory_space=pltpu.VMEM)
    return pl.pallas_call(
        first_kernel,
        in_specs=[vmem] * 3 + [pl.BlockSpec(memory_space=pltpu.SMEM)],
        out_specs=vmem,
        out_shape=jax.ShapeDtypeStruct((tokens.shape[0], tokens.shape[1] + LANES), tokens.dtype),
        scratch_shapes=[pltpu.VMEM((LANES, LANES), jnp.float32)],
        compiler_params=params(),
        cost_estimate=NOTHING,
    )(tokens, probs.T, ids.T, old_place)


def copy_kernel(plan, n_in, n_out, *refs):
    old_ref, new_ref = refs[:2]
    ins, refs = refs[2 : 2 + n_in], refs[-n_out - 3 :]
    outs, (held, in_sems, out_sems) = refs[:n_out], refs[n_out:]
    _, core, row = position()
    second = 2 * row + 1
    moved = (old_ref[second] != new_ref[second]).astype(jnp.int32)
    slots = {"mine": core, "theirs": 1 - core, "leaves": moved, "stays": 1 - moved}
    slots.update({i: i for i in range(3)})
    loads = [
        pltpu.make_async_copy(ins[i].at[slots[a]], held.at[n], in_sems.at[n])
        for n, (i, a, o, b) in enumerate(plan)
    ]
    stores = [
        pltpu.make_async_copy(held.at[n], outs[o].at[slots[b]], out_sems.at[n])
        for n, (i, a, o, b) in enumerate(plan)
    ]
    for c in loads:
        c.start()
    for n, c in enumerate(stores):
        loads[n].wait()
        c.start()
    for c in stores:
        c.wait()


def copies(plan, places, ins, counts, after=(), aliases=()):
    slot, kind = ins[0].shape[1:], ins[0].dtype
    smem, anywhere = pl.BlockSpec(memory_space=pltpu.SMEM), pl.BlockSpec(memory_space=pl.ANY)
    return pl.pallas_call(
        functools.partial(copy_kernel, plan, len(ins), len(counts)),
        in_specs=[smem] * 2 + [anywhere] * (len(ins) + len(aliases) + len(after)),
        out_specs=(anywhere,) * len(counts),
        out_shape=tuple(jax.ShapeDtypeStruct((n,) + slot, kind) for n in counts),
        input_output_aliases={2 + len(ins) + i: i for i in range(len(aliases))},
        scratch_shapes=[
            pltpu.VMEM((len(plan),) + slot, kind),
            pltpu.SemaphoreType.DMA((len(plan),)),
            pltpu.SemaphoreType.DMA((len(plan),)),
        ],
        compiler_params=params(MOST),
        cost_estimate=NOTHING,
    )(*places, *ins, *aliases, *after)


def order_kernel(mine_ref, other_ref, first_ref, second_ref, held, in_sems, out_sems):
    _, core, _ = position()
    loads = [
        pltpu.make_async_copy(mine_ref.at[core], held.at[core], in_sems.at[0]),
        pltpu.make_async_copy(other_ref.at[0], held.at[1 - core], in_sems.at[1]),
    ]
    stores = [
        pltpu.make_async_copy(held.at[n], out, out_sems.at[n])
        for n, out in enumerate((first_ref, second_ref))
    ]
    for c in loads:
        c.start()
    for c in loads:
        c.wait()
    for c in stores:
        c.start()
    for c in stores:
        c.wait()


def in_order(w_down, other):
    anywhere = pl.BlockSpec(memory_space=pl.ANY)
    slot = w_down.shape[1:]
    return pl.pallas_call(
        order_kernel,
        in_specs=[anywhere] * 2,
        out_specs=(anywhere,) * 2,
        out_shape=(jax.ShapeDtypeStruct(slot, w_down.dtype),) * 2,
        scratch_shapes=[
            pltpu.VMEM((2,) + slot, w_down.dtype),
            pltpu.SemaphoreType.DMA((2,)),
            pltpu.SemaphoreType.DMA((2,)),
        ],
        compiler_params=params(MOST),
        cost_estimate=NOTHING,
    )(w_down, other)


def join_kernel(*refs):
    pass


def joined(x, *after):
    anywhere = pl.BlockSpec(memory_space=pl.ANY)
    return pl.pallas_call(
        join_kernel,
        in_specs=[anywhere] * (1 + len(after)),
        out_specs=anywhere,
        out_shape=jax.ShapeDtypeStruct(x.shape, x.dtype),
        input_output_aliases={0: 0},
        compiler_params=params(),
        cost_estimate=NOTHING,
    )(x, *after)


def hidden_kernel(n_pieces, *refs):
    pieces, weights, (out_ref, x_ref, coef_ref) = refs[:n_pieces], refs[n_pieces:-3], refs[-3:]
    _, depth, block = weights[0].shape
    rows, width = x_ref.shape
    tall = rows // n_pieces
    pair, core, row = position()

    @pl.when(pl.program_id(0) == 0)
    def _():
        for n, p in enumerate(pieces):
            x_ref[n * tall : (n + 1) * tall] = p[:, :width]
            coef = p[:, width:].astype(jnp.float32)
            lane = lax.broadcasted_iota(jnp.int32, coef.shape, 1)
            coef = jnp.sum(jnp.where(lane == 2 * row + core, coef, 0.0), axis=1, keepdims=True)
            coef_ref[n * tall : (n + 1) * tall] = jnp.broadcast_to(coef, (tall, LANES))

    tile = min(rows, 512)
    for top in range(0, rows, tile):
        gate = jnp.zeros((tile, block), jnp.float32)
        up = jnp.zeros((tile, block), jnp.float32)
        for i, w in enumerate(weights):
            start = (2 * (pair ^ (i // 2)) + (core ^ (i % 2))) * depth
            x = x_ref[top : top + tile, pl.ds(pl.multiple_of(start, LANES), depth)]
            gate += jnp.dot(x, w[0], preferred_element_type=jnp.float32)
            up += jnp.dot(x, w[1], preferred_element_type=jnp.float32)
        coef = coef_ref[top : top + tile, :1]
        hidden = gate / (1.0 + jnp.exp(-gate)) * up * coef
        out_ref[top : top + tile] = hidden.astype(out_ref.dtype)


def hidden_of(pieces, weights):
    _, depth, ff = weights[0].shape
    block = 256
    tall, wide = pieces[0].shape
    rows = tall * len(pieces)
    return pl.pallas_call(
        functools.partial(hidden_kernel, len(pieces)),
        grid=(ff // block,),
        in_specs=[pl.BlockSpec((tall, wide), lambda f: (0, 0))] * len(pieces)
        + [pl.BlockSpec((2, depth, block), lambda f: (0, 0, f))] * len(weights),
        out_specs=pl.BlockSpec((rows, block), lambda f: (0, f)),
        out_shape=jax.ShapeDtypeStruct((rows, ff), pieces[0].dtype),
        scratch_shapes=[
            pltpu.VMEM((rows, wide - LANES), pieces[0].dtype),
            pltpu.VMEM((rows, LANES), jnp.float32),
        ],
        compiler_params=params(),
        cost_estimate=pl.CostEstimate(flops=1, bytes_accessed=1, transcendentals=0),
    )(*pieces, *weights)


def down_kernel(n_downs, hidden_ref, *refs):
    downs, (kept_ref, sent_ref) = refs[:n_downs], refs[-2:]
    depth = downs[0].shape[0]
    rows = kept_ref.shape[0]
    tile = min(rows, 512)
    contract = (((1,), (1,)), ((), ()))
    for i, w in enumerate(downs):
        for out, base in ((kept_ref, 0), (sent_ref, rows)):
            for top in range(0, rows, tile):
                part = lax.dot_general(
                    hidden_ref[base + top : base + top + tile], w[...], contract,
                    preferred_element_type=jnp.float32,
                )
                out[top : top + tile, i * depth : (i + 1) * depth] = part.astype(out.dtype)


def down_of(hidden, downs, after):
    depth, ff = downs[0].shape
    rows = hidden.shape[0] // 2
    vmem = pl.BlockSpec(memory_space=pltpu.VMEM)
    out = jax.ShapeDtypeStruct((rows, len(downs) * depth), hidden.dtype)
    return pl.pallas_call(
        functools.partial(down_kernel, len(downs)),
        in_specs=[vmem] * (1 + len(downs)) + [pl.BlockSpec(memory_space=pl.ANY)] * len(after),
        out_specs=(vmem, vmem),
        out_shape=(out, out),
        compiler_params=params(),
        cost_estimate=pl.CostEstimate(flops=1, bytes_accessed=1, transcendentals=0),
    )(hidden, *downs, *after)


def over_core(kept, sent, tok):
    total = kept.astype(jnp.float32) + swap(sent, "shard", 1).astype(jnp.float32)
    return total.reshape(-1, 2 * tok, total.shape[-1])


def step_z(total, bit):
    pairs = total.reshape((-1, 2) + total.shape[1:])
    return pairs[:, 0] + flip_z(pairs[:, 1].astype(jnp.bfloat16), bit).astype(jnp.float32)


def over_x(total):
    halves = total.reshape(total.shape[0], 2, -1, total.shape[-1])
    return halves[:, 0] + swap(halves[:, 1].astype(jnp.bfloat16), "dp", 1).astype(jnp.float32)


def over_z(total, bit):
    while total.shape[0] > 1:
        total = step_z(total, bit)
        bit *= 2
    return total[0].astype(jnp.bfloat16)


def place_kernel(depth, *refs):
    parts, out_ref = refs[:-1], refs[-1]
    pair, _, _ = position()
    for part, blocks in zip(parts, out_blocks(depth, [p.shape[1] for p in parts])):
        for n, (j, core) in enumerate(blocks):
            start = pl.multiple_of((2 * (pair ^ j) + core) * depth, LANES)
            out_ref[:, pl.ds(start, depth)] = part[:, n * depth : (n + 1) * depth]


def out_blocks(depth, widths):
    others = range(1, widths[1] // depth + 1)
    return [[(0, 0), (0, 1)] + [(j, 0) for j in others], [(j, 1) for j in others]]


def placed(parts, depth, width):
    vmem = pl.BlockSpec(memory_space=pltpu.VMEM)
    return pl.pallas_call(
        functools.partial(place_kernel, depth),
        in_specs=[vmem] * len(parts),
        out_specs=vmem,
        out_shape=jax.ShapeDtypeStruct((parts[0].shape[0], width), parts[0].dtype),
        compiler_params=params(),
        cost_estimate=NOTHING,
    )(*parts)


def local(tokens, router_probs, expert_ids, old_place, new_place, w_gate, w_up, w_down):
    tok, width = tokens.shape
    depth = w_gate.shape[1]
    n_z = lax.axis_size("dp") // 2
    places = (old_place, new_place)

    mine, theirs, theirs_down = copies(
        ((0, "mine", 0, 0), (1, "mine", 0, 1))
        + ((0, "theirs", 1, 0), (1, "theirs", 1, 1), (2, "theirs", 2, 0)),
        places, (w_gate, w_up, w_down), (2, 2, 1),
    )
    near_weights = [mine, swap(theirs, "shard", 1)]
    weights = spread(near_weights)
    downs = [spread([d]) for d in in_order(w_down, swap(theirs_down, "shard", 1))]

    own = first(tokens, router_probs, expert_ids, old_place)
    columns = [own] + [flip_z(own, j) for j in range(1, n_z)]
    across = [swap(own, "dp", 1)]
    for c in columns[1:]:
        across.append(swap(joined(c, across[-1]), "dp", 1))
    near = [joined(jnp.concatenate(p, axis=0), weights[2]) for p in zip(columns, across)]
    far = [swap(p, "shard", 1) for p in near]

    hidden = hidden_of(near + far, weights)
    (leave,) = copies(
        tuple((i, "leaves", 0, i) for i in range(3)), places, (w_gate, w_up, w_down), (3,), across
    )
    arrive = passed_along(leave, "dp", 1)
    news = copies(
        tuple((0, i, i, "leaves") for i in range(3))
        + tuple((i + 1, "stays", i, "stays") for i in range(3)),
        places, (arrive, w_gate, w_up, w_down), (2, 2, 2),
    )

    groups = [[d[0] for d in downs]] + [d[1:] for d in downs]
    kept, sent = down_of(hidden, groups[0], ())
    own_rows = step_z(over_core(kept, sent, tok), 1)
    kept, sent = down_of(hidden, groups[1], (sent,))
    first_rows = step_z(over_core(kept, sent, tok), 1)
    kept, sent = down_of(hidden, groups[2], (sent, news[0], own_rows, first_rows))
    early = over_x(jnp.concatenate([own_rows, first_rows], axis=-1))
    late = over_x(step_z(over_core(kept, sent, tok), 1))
    parts = [over_z(early, 2), over_z(late, 2)]
    moe_output = placed(parts, depth, width)

    return (moe_output, *news)


def solution(mesh):
    in_specs = (
        P(("dp", "shard"), None),
        P(("dp", "shard"), None),
        P(("dp", "shard"), None),
        P(),
        P(),
        P("dp", "shard", None),
        P("dp", "shard", None),
        P("dp", "shard", None),
    )
    out_specs = (
        P(("dp", "shard"), None),
        P("dp", "shard", None),
        P("dp", "shard", None),
        P("dp", "shard", None),
    )
    return jax.shard_map(local, mesh=mesh, in_specs=in_specs, out_specs=out_specs, check_vma=False)
```

```python
import functools

import jax
import jax.numpy as jnp
from jax import lax
from jax.experimental import pallas as pl
from jax.experimental.pallas import tpu as pltpu
from jax.sharding import PartitionSpec as P

LANES = 128
VMEM_BYTES = 32 * 1024 * 1024
MOST = 56 * 1024 * 1024
NOTHING = pl.CostEstimate(flops=0, bytes_accessed=0, transcendentals=0)


def swap(x, axis, bit):
    return lax.ppermute(x, axis, [(i, i ^ bit) for i in range(lax.axis_size(axis))])


def passed_along(x, axis, by):
    size = lax.axis_size(axis)
    return lax.ppermute(x, axis, [(i, (i + by) % size) for i in range(size)])


def flip_z(x, bits):
    return swap(x, "dp", 2 * bits)


def spread(pieces):
    bit = 2
    while bit < lax.axis_size("shard"):
        pieces = pieces + [swap(p, "shard", bit) for p in pieces]
        bit *= 2
    return pieces


def params(amount=VMEM_BYTES):
    return pltpu.CompilerParams(vmem_limit_bytes=amount)


def position():
    column = lax.axis_index("shard")
    return lax.div(column, 2), lax.rem(column, 2), lax.axis_index("dp")


def first_kernel(tokens_ref, probs_ref, ids_ref, place_ref, out_ref, coef_ref):
    probs = probs_ref[...]
    weights = (probs / jnp.sum(probs, axis=0, keepdims=True)).astype(jnp.bfloat16)
    weights = weights.astype(jnp.float32)
    ids = ids_ref[...]
    tok, width = tokens_ref.shape
    coef_ref[...] = jnp.zeros_like(coef_ref)
    for slot in range(place_ref.shape[0]):
        named = jnp.where(ids == place_ref[slot], weights, 0.0)
        coef_ref[slot : slot + 1, :tok] = jnp.sum(named, axis=0, keepdims=True)
    out_ref[:, :width] = tokens_ref[...]
    out_ref[:, width:] = jnp.transpose(coef_ref[...])[:tok].astype(jnp.bfloat16)


def first(tokens, probs, ids, old_place):
    vmem = pl.BlockSpec(memory_space=pltpu.VMEM)
    return pl.pallas_call(
        first_kernel,
        in_specs=[vmem] * 3 + [pl.BlockSpec(memory_space=pltpu.SMEM)],
        out_specs=vmem,
        out_shape=jax.ShapeDtypeStruct((tokens.shape[0], tokens.shape[1] + LANES), tokens.dtype),
        scratch_shapes=[pltpu.VMEM((LANES, LANES), jnp.float32)],
        compiler_params=params(),
        cost_estimate=NOTHING,
    )(tokens, probs.T, ids.T, old_place)


def copy_kernel(plan, n_in, n_out, *refs):
    old_ref, new_ref = refs[:2]
    ins, refs = refs[2 : 2 + n_in], refs[-n_out - 3 :]
    outs, (held, in_sems, out_sems) = refs[:n_out], refs[n_out:]
    _, core, row = position()
    second = 2 * row + 1
    moved = (old_ref[second] != new_ref[second]).astype(jnp.int32)
    slots = {"mine": core, "theirs": 1 - core, "leaves": moved, "stays": 1 - moved}
    slots.update({i: i for i in range(3)})
    loads = [
        pltpu.make_async_copy(ins[i].at[slots[a]], held.at[n], in_sems.at[n])
        for n, (i, a, o, b) in enumerate(plan)
    ]
    stores = [
        pltpu.make_async_copy(held.at[n], outs[o].at[slots[b]], out_sems.at[n])
        for n, (i, a, o, b) in enumerate(plan)
    ]
    for c in loads:
        c.start()
    for n, c in enumerate(stores):
        loads[n].wait()
        c.start()
    for c in stores:
        c.wait()


def copies(plan, places, ins, counts, after=(), aliases=()):
    slot, kind = ins[0].shape[1:], ins[0].dtype
    smem, anywhere = pl.BlockSpec(memory_space=pltpu.SMEM), pl.BlockSpec(memory_space=pl.ANY)
    return pl.pallas_call(
        functools.partial(copy_kernel, plan, len(ins), len(counts)),
        in_specs=[smem] * 2 + [anywhere] * (len(ins) + len(aliases) + len(after)),
        out_specs=(anywhere,) * len(counts),
        out_shape=tuple(jax.ShapeDtypeStruct((n,) + slot, kind) for n in counts),
        input_output_aliases={2 + len(ins) + i: i for i in range(len(aliases))},
        scratch_shapes=[
            pltpu.VMEM((len(plan),) + slot, kind),
            pltpu.SemaphoreType.DMA((len(plan),)),
            pltpu.SemaphoreType.DMA((len(plan),)),
        ],
        compiler_params=params(MOST),
        cost_estimate=NOTHING,
    )(*places, *ins, *aliases, *after)


def order_kernel(mine_ref, other_ref, first_ref, second_ref, held, in_sems, out_sems):
    _, core, _ = position()
    loads = [
        pltpu.make_async_copy(mine_ref.at[core], held.at[core], in_sems.at[0]),
        pltpu.make_async_copy(other_ref.at[0], held.at[1 - core], in_sems.at[1]),
    ]
    stores = [
        pltpu.make_async_copy(held.at[n], out, out_sems.at[n])
        for n, out in enumerate((first_ref, second_ref))
    ]
    for c in loads:
        c.start()
    for c in loads:
        c.wait()
    for c in stores:
        c.start()
    for c in stores:
        c.wait()


def in_order(w_down, other):
    anywhere = pl.BlockSpec(memory_space=pl.ANY)
    slot = w_down.shape[1:]
    return pl.pallas_call(
        order_kernel,
        in_specs=[anywhere] * 2,
        out_specs=(anywhere,) * 2,
        out_shape=(jax.ShapeDtypeStruct(slot, w_down.dtype),) * 2,
        scratch_shapes=[
            pltpu.VMEM((2,) + slot, w_down.dtype),
            pltpu.SemaphoreType.DMA((2,)),
            pltpu.SemaphoreType.DMA((2,)),
        ],
        compiler_params=params(MOST),
        cost_estimate=NOTHING,
    )(w_down, other)


def join_kernel(*refs):
    pass


def joined(x, *after):
    anywhere = pl.BlockSpec(memory_space=pl.ANY)
    return pl.pallas_call(
        join_kernel,
        in_specs=[anywhere] * (1 + len(after)),
        out_specs=anywhere,
        out_shape=jax.ShapeDtypeStruct(x.shape, x.dtype),
        input_output_aliases={0: 0},
        compiler_params=params(),
        cost_estimate=NOTHING,
    )(x, *after)


def hidden_kernel(n_pieces, *refs):
    pieces, weights, (out_ref, x_ref, coef_ref) = refs[:n_pieces], refs[n_pieces:-3], refs[-3:]
    _, depth, block = weights[0].shape
    rows, width = x_ref.shape
    tall = rows // n_pieces
    pair, core, row = position()

    @pl.when(pl.program_id(0) == 0)
    def _():
        for n, p in enumerate(pieces):
            x_ref[n * tall : (n + 1) * tall] = p[:, :width]
            coef = p[:, width:].astype(jnp.float32)
            lane = lax.broadcasted_iota(jnp.int32, coef.shape, 1)
            coef = jnp.sum(jnp.where(lane == 2 * row + core, coef, 0.0), axis=1, keepdims=True)
            coef_ref[n * tall : (n + 1) * tall] = jnp.broadcast_to(coef, (tall, LANES))

    tile = min(rows, 512)
    for top in range(0, rows, tile):
        gate = jnp.zeros((tile, block), jnp.float32)
        up = jnp.zeros((tile, block), jnp.float32)
        for i, w in enumerate(weights):
            start = (2 * (pair ^ (i // 2)) + (core ^ (i % 2))) * depth
            x = x_ref[top : top + tile, pl.ds(pl.multiple_of(start, LANES), depth)]
            gate += jnp.dot(x, w[0], preferred_element_type=jnp.float32)
            up += jnp.dot(x, w[1], preferred_element_type=jnp.float32)
        coef = coef_ref[top : top + tile, :1]
        hidden = gate / (1.0 + jnp.exp(-gate)) * up * coef
        out_ref[top : top + tile] = hidden.astype(out_ref.dtype)


def hidden_of(pieces, weights):
    _, depth, ff = weights[0].shape
    block = 256
    tall, wide = pieces[0].shape
    rows = tall * len(pieces)
    return pl.pallas_call(
        functools.partial(hidden_kernel, len(pieces)),
        grid=(ff // block,),
        in_specs=[pl.BlockSpec((tall, wide), lambda f: (0, 0))] * len(pieces)
        + [pl.BlockSpec((2, depth, block), lambda f: (0, 0, f))] * len(weights),
        out_specs=pl.BlockSpec((rows, block), lambda f: (0, f)),
        out_shape=jax.ShapeDtypeStruct((rows, ff), pieces[0].dtype),
        scratch_shapes=[
            pltpu.VMEM((rows, wide - LANES), pieces[0].dtype),
            pltpu.VMEM((rows, LANES), jnp.float32),
        ],
        compiler_params=params(),
        cost_estimate=pl.CostEstimate(flops=1, bytes_accessed=1, transcendentals=0),
    )(*pieces, *weights)


def down_kernel(n_downs, hidden_ref, *refs):
    downs, (kept_ref, sent_ref) = refs[:n_downs], refs[-2:]
    depth = downs[0].shape[0]
    rows = kept_ref.shape[0]
    tile = min(rows, 512)
    contract = (((1,), (1,)), ((), ()))
    for i, w in enumerate(downs):
        for out, base in ((kept_ref, 0), (sent_ref, rows)):
            for top in range(0, rows, tile):
                part = lax.dot_general(
                    hidden_ref[base + top : base + top + tile], w[...], contract,
                    preferred_element_type=jnp.float32,
                )
                out[top : top + tile, i * depth : (i + 1) * depth] = part.astype(out.dtype)


def down_of(hidden, downs, after):
    depth, ff = downs[0].shape
    rows = hidden.shape[0] // 2
    vmem = pl.BlockSpec(memory_space=pltpu.VMEM)
    out = jax.ShapeDtypeStruct((rows, len(downs) * depth), hidden.dtype)
    return pl.pallas_call(
        functools.partial(down_kernel, len(downs)),
        in_specs=[vmem] * (1 + len(downs)) + [pl.BlockSpec(memory_space=pl.ANY)] * len(after),
        out_specs=(vmem, vmem),
        out_shape=(out, out),
        compiler_params=params(),
        cost_estimate=pl.CostEstimate(flops=1, bytes_accessed=1, transcendentals=0),
    )(hidden, *downs, *after)


def over_core(kept, sent, tok):
    total = kept.astype(jnp.float32) + swap(sent, "shard", 1).astype(jnp.float32)
    return total.reshape(-1, 2 * tok, total.shape[-1])


def step_z(total, bit):
    pairs = total.reshape((-1, 2) + total.shape[1:])
    return pairs[:, 0] + flip_z(pairs[:, 1].astype(jnp.bfloat16), bit).astype(jnp.float32)


def over_x(total):
    halves = total.reshape(total.shape[0], 2, -1, total.shape[-1])
    return halves[:, 0] + swap(halves[:, 1].astype(jnp.bfloat16), "dp", 1).astype(jnp.float32)


def over_z(total, bit):
    while total.shape[0] > 1:
        total = step_z(total, bit)
        bit *= 2
    return total[0].astype(jnp.bfloat16)


def place_kernel(depth, *refs):
    parts, out_ref = refs[:-1], refs[-1]
    pair, _, _ = position()
    for part, blocks in zip(parts, out_blocks(depth, [p.shape[1] for p in parts])):
        for n, (j, core) in enumerate(blocks):
            start = pl.multiple_of((2 * (pair ^ j) + core) * depth, LANES)
            out_ref[:, pl.ds(start, depth)] = part[:, n * depth : (n + 1) * depth]


def out_blocks(depth, widths):
    others = range(1, widths[1] // depth + 1)
    return [[(0, 0), (0, 1)] + [(j, 0) for j in others], [(j, 1) for j in others]]


def placed(parts, depth, width):
    vmem = pl.BlockSpec(memory_space=pltpu.VMEM)
    return pl.pallas_call(
        functools.partial(place_kernel, depth),
        in_specs=[vmem] * len(parts),
        out_specs=vmem,
        out_shape=jax.ShapeDtypeStruct((parts[0].shape[0], width), parts[0].dtype),
        compiler_params=params(),
        cost_estimate=NOTHING,
    )(*parts)


def local(tokens, router_probs, expert_ids, old_place, new_place, w_gate, w_up, w_down):
    tok, width = tokens.shape
    depth = w_gate.shape[1]
    n_z = lax.axis_size("dp") // 2
    places = (old_place, new_place)

    mine, theirs = copies(
        ((0, "mine", 0, 0), (1, "mine", 0, 1), (0, "theirs", 1, 0), (1, "theirs", 1, 1)),
        places, (w_gate, w_up), (2, 2),
    )
    (theirs_down,) = copies(((0, "theirs", 0, 0),), places, (w_down,), (1,), (mine,))
    near_weights = [mine, swap(theirs, "shard", 1)]
    weights = spread(near_weights)
    downs = [spread([d]) for d in in_order(w_down, swap(theirs_down, "shard", 1))]

    own = first(tokens, router_probs, expert_ids, old_place)
    columns = [own] + [flip_z(own, j) for j in range(1, n_z)]
    across = [swap(own, "dp", 1)]
    for c in columns[1:]:
        across.append(swap(joined(c, across[-1]), "dp", 1))
    near = [joined(jnp.concatenate(p, axis=0), weights[2]) for p in zip(columns, across)]
    far = [swap(p, "shard", 1) for p in near]

    hidden = hidden_of(near + far, weights)
    (leave,) = copies(
        tuple((i, "leaves", 0, i) for i in range(3)), places, (w_gate, w_up, w_down), (3,), across
    )
    arrive = passed_along(leave, "dp", 1)
    news = copies(
        tuple((0, i, i, "leaves") for i in range(3))
        + tuple((i + 1, "stays", i, "stays") for i in range(3)),
        places, (arrive, w_gate, w_up, w_down), (2, 2, 2),
    )

    groups = [[d[0] for d in downs]] + [d[1:] for d in downs]
    kept, sent = down_of(hidden, groups[0], ())
    own_rows = step_z(over_core(kept, sent, tok), 1)
    kept, sent = down_of(hidden, groups[1], (sent,))
    first_rows = step_z(over_core(kept, sent, tok), 1)
    kept, sent = down_of(hidden, groups[2], (sent, news[0], own_rows, first_rows))
    early = over_x(jnp.concatenate([own_rows, first_rows], axis=-1))
    late = over_x(step_z(over_core(kept, sent, tok), 1))
    parts = [over_z(early, 2), over_z(late, 2)]
    moe_output = placed(parts, depth, width)

    return (moe_output, *news)


def solution(mesh):
    in_specs = (
        P(("dp", "shard"), None),
        P(("dp", "shard"), None),
        P(("dp", "shard"), None),
        P(),
        P(),
        P("dp", "shard", None),
        P("dp", "shard", None),
        P("dp", "shard", None),
    )
    out_specs = (
        P(("dp", "shard"), None),
        P("dp", "shard", None),
        P("dp", "shard", None),
        P("dp", "shard", None),
    )
    return jax.shard_map(local, mesh=mesh, in_specs=in_specs, out_specs=out_specs, check_vma=False)
```

```python
import functools

import jax
import jax.numpy as jnp
from jax import lax
from jax.experimental import pallas as pl
from jax.experimental.pallas import tpu as pltpu
from jax.sharding import PartitionSpec as P

LANES = 128
VMEM_BYTES = 32 * 1024 * 1024
MOST = 56 * 1024 * 1024
NOTHING = pl.CostEstimate(flops=0, bytes_accessed=0, transcendentals=0)


def swap(x, axis, bit):
    return lax.ppermute(x, axis, [(i, i ^ bit) for i in range(lax.axis_size(axis))])


def passed_along(x, axis, by):
    size = lax.axis_size(axis)
    return lax.ppermute(x, axis, [(i, (i + by) % size) for i in range(size)])


def flip_z(x, bits):
    return swap(x, "dp", 2 * bits)


def spread(pieces):
    bit = 2
    while bit < lax.axis_size("shard"):
        pieces = pieces + [swap(p, "shard", bit) for p in pieces]
        bit *= 2
    return pieces


def params(amount=VMEM_BYTES):
    return pltpu.CompilerParams(vmem_limit_bytes=amount)


def position():
    column = lax.axis_index("shard")
    return lax.div(column, 2), lax.rem(column, 2), lax.axis_index("dp")


def first_kernel(tokens_ref, probs_ref, ids_ref, place_ref, out_ref, coef_ref):
    probs = probs_ref[...]
    weights = (probs / jnp.sum(probs, axis=0, keepdims=True)).astype(jnp.bfloat16)
    weights = weights.astype(jnp.float32)
    ids = ids_ref[...]
    tok, width = tokens_ref.shape
    coef_ref[...] = jnp.zeros_like(coef_ref)
    for slot in range(place_ref.shape[0]):
        named = jnp.where(ids == place_ref[slot], weights, 0.0)
        coef_ref[slot : slot + 1, :tok] = jnp.sum(named, axis=0, keepdims=True)
    out_ref[:, :width] = tokens_ref[...]
    out_ref[:, width:] = jnp.transpose(coef_ref[...])[:tok].astype(jnp.bfloat16)


def first(tokens, probs, ids, old_place):
    vmem = pl.BlockSpec(memory_space=pltpu.VMEM)
    return pl.pallas_call(
        first_kernel,
        in_specs=[vmem] * 3 + [pl.BlockSpec(memory_space=pltpu.SMEM)],
        out_specs=vmem,
        out_shape=jax.ShapeDtypeStruct((tokens.shape[0], tokens.shape[1] + LANES), tokens.dtype),
        scratch_shapes=[pltpu.VMEM((LANES, LANES), jnp.float32)],
        compiler_params=params(),
        cost_estimate=NOTHING,
    )(tokens, probs.T, ids.T, old_place)


def copy_kernel(plan, n_in, n_out, *refs):
    old_ref, new_ref = refs[:2]
    ins, refs = refs[2 : 2 + n_in], refs[-n_out - 3 :]
    outs, (held, in_sems, out_sems) = refs[:n_out], refs[n_out:]
    _, core, row = position()
    second = 2 * row + 1
    moved = (old_ref[second] != new_ref[second]).astype(jnp.int32)
    slots = {"mine": core, "theirs": 1 - core, "leaves": moved, "stays": 1 - moved}
    slots.update({i: i for i in range(3)})
    loads = [
        pltpu.make_async_copy(ins[i].at[slots[a]], held.at[n], in_sems.at[n])
        for n, (i, a, o, b) in enumerate(plan)
    ]
    stores = [
        pltpu.make_async_copy(held.at[n], outs[o].at[slots[b]], out_sems.at[n])
        for n, (i, a, o, b) in enumerate(plan)
    ]
    for c in loads:
        c.start()
    for n, c in enumerate(stores):
        loads[n].wait()
        c.start()
    for c in stores:
        c.wait()


def copies(plan, places, ins, counts, after=(), aliases=()):
    slot, kind = ins[0].shape[1:], ins[0].dtype
    smem, anywhere = pl.BlockSpec(memory_space=pltpu.SMEM), pl.BlockSpec(memory_space=pl.ANY)
    return pl.pallas_call(
        functools.partial(copy_kernel, plan, len(ins), len(counts)),
        in_specs=[smem] * 2 + [anywhere] * (len(ins) + len(aliases) + len(after)),
        out_specs=(anywhere,) * len(counts),
        out_shape=tuple(jax.ShapeDtypeStruct((n,) + slot, kind) for n in counts),
        input_output_aliases={2 + len(ins) + i: i for i in range(len(aliases))},
        scratch_shapes=[
            pltpu.VMEM((len(plan),) + slot, kind),
            pltpu.SemaphoreType.DMA((len(plan),)),
            pltpu.SemaphoreType.DMA((len(plan),)),
        ],
        compiler_params=params(MOST),
        cost_estimate=NOTHING,
    )(*places, *ins, *aliases, *after)


def order_kernel(mine_ref, other_ref, first_ref, second_ref, held, in_sems, out_sems):
    _, core, _ = position()
    depth, cut = mine_ref.shape[1], first_ref.shape[0]

    def rows(n):
        return held.at[pl.ds(pl.multiple_of(n * depth, LANES), depth)]

    loads = [
        pltpu.make_async_copy(mine_ref.at[core], rows(core), in_sems.at[0]),
        pltpu.make_async_copy(other_ref.at[0], rows(1 - core), in_sems.at[1]),
    ]
    stores = [
        pltpu.make_async_copy(held.at[pl.ds(0, cut)], first_ref, out_sems.at[0]),
        pltpu.make_async_copy(held.at[pl.ds(cut, 2 * depth - cut)], second_ref, out_sems.at[1]),
    ]
    for c in loads:
        c.start()
    for c in loads:
        c.wait()
    for c in stores:
        c.start()
    for c in stores:
        c.wait()


def cut_of(depth):
    return max(LANES, 3 * depth // 4)


def in_order(w_down, other):
    anywhere = pl.BlockSpec(memory_space=pl.ANY)
    depth, ff = w_down.shape[1:]
    cut = cut_of(depth)
    return pl.pallas_call(
        order_kernel,
        in_specs=[anywhere] * 2,
        out_specs=(anywhere,) * 2,
        out_shape=tuple(
            jax.ShapeDtypeStruct((n, ff), w_down.dtype) for n in (cut, 2 * depth - cut)
        ),
        scratch_shapes=[
            pltpu.VMEM((2 * depth, ff), w_down.dtype),
            pltpu.SemaphoreType.DMA((2,)),
            pltpu.SemaphoreType.DMA((2,)),
        ],
        compiler_params=params(MOST),
        cost_estimate=NOTHING,
    )(w_down, other)


def join_kernel(*refs):
    pass


def joined(x, *after):
    anywhere = pl.BlockSpec(memory_space=pl.ANY)
    return pl.pallas_call(
        join_kernel,
        in_specs=[anywhere] * (1 + len(after)),
        out_specs=anywhere,
        out_shape=jax.ShapeDtypeStruct(x.shape, x.dtype),
        input_output_aliases={0: 0},
        compiler_params=params(),
        cost_estimate=NOTHING,
    )(x, *after)


def hidden_kernel(n_pieces, *refs):
    pieces, weights, (out_ref, x_ref, coef_ref) = refs[:n_pieces], refs[n_pieces:-3], refs[-3:]
    _, depth, block = weights[0].shape
    rows, width = x_ref.shape
    tall = rows // n_pieces
    pair, core, row = position()

    @pl.when(pl.program_id(0) == 0)
    def _():
        for n, p in enumerate(pieces):
            x_ref[n * tall : (n + 1) * tall] = p[:, :width]
            coef = p[:, width:].astype(jnp.float32)
            lane = lax.broadcasted_iota(jnp.int32, coef.shape, 1)
            coef = jnp.sum(jnp.where(lane == 2 * row + core, coef, 0.0), axis=1, keepdims=True)
            coef_ref[n * tall : (n + 1) * tall] = jnp.broadcast_to(coef, (tall, LANES))

    tile = min(rows, 512)
    for top in range(0, rows, tile):
        gate = jnp.zeros((tile, block), jnp.float32)
        up = jnp.zeros((tile, block), jnp.float32)
        for i, w in enumerate(weights):
            start = (2 * (pair ^ (i // 2)) + (core ^ (i % 2))) * depth
            x = x_ref[top : top + tile, pl.ds(pl.multiple_of(start, LANES), depth)]
            gate += jnp.dot(x, w[0], preferred_element_type=jnp.float32)
            up += jnp.dot(x, w[1], preferred_element_type=jnp.float32)
        coef = coef_ref[top : top + tile, :1]
        hidden = gate / (1.0 + jnp.exp(-gate)) * up * coef
        out_ref[top : top + tile] = hidden.astype(out_ref.dtype)


def hidden_of(pieces, weights):
    _, depth, ff = weights[0].shape
    block = 256
    tall, wide = pieces[0].shape
    rows = tall * len(pieces)
    return pl.pallas_call(
        functools.partial(hidden_kernel, len(pieces)),
        grid=(ff // block,),
        in_specs=[pl.BlockSpec((tall, wide), lambda f: (0, 0))] * len(pieces)
        + [pl.BlockSpec((2, depth, block), lambda f: (0, 0, f))] * len(weights),
        out_specs=pl.BlockSpec((rows, block), lambda f: (0, f)),
        out_shape=jax.ShapeDtypeStruct((rows, ff), pieces[0].dtype),
        scratch_shapes=[
            pltpu.VMEM((rows, wide - LANES), pieces[0].dtype),
            pltpu.VMEM((rows, LANES), jnp.float32),
        ],
        compiler_params=params(),
        cost_estimate=pl.CostEstimate(flops=1, bytes_accessed=1, transcendentals=0),
    )(*pieces, *weights)


def down_kernel(n_downs, hidden_ref, *refs):
    downs, (kept_ref, sent_ref) = refs[:n_downs], refs[-2:]
    rows = kept_ref.shape[0]
    tile = min(rows, 512)
    contract = (((1,), (1,)), ((), ()))
    left = 0
    for w in downs:
        right = left + w.shape[0]
        for out, base in ((kept_ref, 0), (sent_ref, rows)):
            for top in range(0, rows, tile):
                part = lax.dot_general(
                    hidden_ref[base + top : base + top + tile], w[...], contract,
                    preferred_element_type=jnp.float32,
                )
                out[top : top + tile, left:right] = part.astype(out.dtype)
        left = right


def down_of(hidden, downs, after):
    rows = hidden.shape[0] // 2
    vmem = pl.BlockSpec(memory_space=pltpu.VMEM)
    out = jax.ShapeDtypeStruct((rows, sum(d.shape[0] for d in downs)), hidden.dtype)
    return pl.pallas_call(
        functools.partial(down_kernel, len(downs)),
        in_specs=[vmem] * (1 + len(downs)) + [pl.BlockSpec(memory_space=pl.ANY)] * len(after),
        out_specs=(vmem, vmem),
        out_shape=(out, out),
        compiler_params=params(),
        cost_estimate=pl.CostEstimate(flops=1, bytes_accessed=1, transcendentals=0),
    )(hidden, *downs, *after)


def over_core(kept, sent, tok):
    total = kept.astype(jnp.float32) + swap(sent, "shard", 1).astype(jnp.float32)
    return total.reshape(-1, 2 * tok, total.shape[-1])


def step_z(total, bit):
    pairs = total.reshape((-1, 2) + total.shape[1:])
    return pairs[:, 0] + flip_z(pairs[:, 1].astype(jnp.bfloat16), bit).astype(jnp.float32)


def over_x(total):
    halves = total.reshape(total.shape[0], 2, -1, total.shape[-1])
    return halves[:, 0] + swap(halves[:, 1].astype(jnp.bfloat16), "dp", 1).astype(jnp.float32)


def over_z(total, bit):
    while total.shape[0] > 1:
        total = step_z(total, bit)
        bit *= 2
    return total[0].astype(jnp.bfloat16)


def place_kernel(depth, *refs):
    (first_ref, second_ref), out_ref = refs[:2], refs[2]
    pair, _, _ = position()
    cut = cut_of(depth)

    def put(j, offset, block):
        start = pl.multiple_of(2 * (pair ^ j) * depth + offset, LANES)
        out_ref[:, pl.ds(start, block.shape[1])] = block

    put(0, 0, first_ref[:, : 2 * depth])
    rest = 2 * depth - cut
    for j in range(1, second_ref.shape[1] // rest + 1):
        left = 2 * depth + (j - 1) * cut
        put(j, 0, first_ref[:, left : left + cut])
        put(j, cut, second_ref[:, (j - 1) * rest : j * rest])


def placed(parts, depth, width):
    vmem = pl.BlockSpec(memory_space=pltpu.VMEM)
    return pl.pallas_call(
        functools.partial(place_kernel, depth),
        in_specs=[vmem] * len(parts),
        out_specs=vmem,
        out_shape=jax.ShapeDtypeStruct((parts[0].shape[0], width), parts[0].dtype),
        compiler_params=params(),
        cost_estimate=NOTHING,
    )(*parts)


def local(tokens, router_probs, expert_ids, old_place, new_place, w_gate, w_up, w_down):
    tok, width = tokens.shape
    depth = w_gate.shape[1]
    n_z = lax.axis_size("dp") // 2
    places = (old_place, new_place)

    mine, theirs = copies(
        ((0, "mine", 0, 0), (1, "mine", 0, 1), (0, "theirs", 1, 0), (1, "theirs", 1, 1)),
        places, (w_gate, w_up), (2, 2),
    )
    (theirs_down,) = copies(((0, "theirs", 0, 0),), places, (w_down,), (1,), (mine,))
    near_weights = [mine, swap(theirs, "shard", 1)]
    weights = spread(near_weights)
    downs = [spread([d]) for d in in_order(w_down, swap(theirs_down, "shard", 1))]

    own = first(tokens, router_probs, expert_ids, old_place)
    columns = [own] + [flip_z(own, j) for j in range(1, n_z)]
    across = [swap(own, "dp", 1)]
    for c in columns[1:]:
        across.append(swap(joined(c, across[-1]), "dp", 1))
    near = [joined(jnp.concatenate(p, axis=0), weights[2]) for p in zip(columns, across)]
    far = [swap(p, "shard", 1) for p in near]

    hidden = hidden_of(near + far, weights)
    (leave,) = copies(
        tuple((i, "leaves", 0, i) for i in range(3)), places, (w_gate, w_up, w_down), (3,), across
    )
    arrive = passed_along(leave, "dp", 1)
    news = copies(
        tuple((0, i, i, "leaves") for i in range(3))
        + tuple((i + 1, "stays", i, "stays") for i in range(3)),
        places, (arrive, w_gate, w_up, w_down), (2, 2, 2),
    )

    kept, sent = down_of(hidden, [d[0] for d in downs], ())
    own_rows = step_z(over_core(kept, sent, tok), 1)
    kept, sent = down_of(hidden, downs[0][1:], (sent,))
    first_rows = step_z(over_core(kept, sent, tok), 1)
    kept, sent = down_of(hidden, downs[1][1:], (sent, news[0], own_rows, first_rows))
    early = over_x(jnp.concatenate([own_rows, first_rows], axis=-1))
    late = over_x(step_z(over_core(kept, sent, tok), 1))
    parts = [over_z(early, 2), over_z(late, 2)]
    moe_output = placed(parts, depth, width)

    return (moe_output, *news)


def solution(mesh):
    in_specs = (
        P(("dp", "shard"), None),
        P(("dp", "shard"), None),
        P(("dp", "shard"), None),
        P(),
        P(),
        P("dp", "shard", None),
        P("dp", "shard", None),
        P("dp", "shard", None),
    )
    out_specs = (
        P(("dp", "shard"), None),
        P("dp", "shard", None),
        P("dp", "shard", None),
        P("dp", "shard", None),
    )
    return jax.shard_map(local, mesh=mesh, in_specs=in_specs, out_specs=out_specs, check_vma=False)
```

```python
import functools

import jax
import jax.numpy as jnp
from jax import lax
from jax.experimental import pallas as pl
from jax.experimental.pallas import tpu as pltpu
from jax.sharding import PartitionSpec as P

LANES = 128
VMEM_BYTES = 32 * 1024 * 1024
MOST = 56 * 1024 * 1024
NOTHING = pl.CostEstimate(flops=0, bytes_accessed=0, transcendentals=0)


def swap(x, axis, bit):
    return lax.ppermute(x, axis, [(i, i ^ bit) for i in range(lax.axis_size(axis))])


def passed_along(x, axis, by):
    size = lax.axis_size(axis)
    return lax.ppermute(x, axis, [(i, (i + by) % size) for i in range(size)])


def flip_z(x, bits):
    return swap(x, "dp", 2 * bits)


def spread(pieces):
    bit = 2
    while bit < lax.axis_size("shard"):
        pieces = pieces + [swap(p, "shard", bit) for p in pieces]
        bit *= 2
    return pieces


def params(amount=VMEM_BYTES):
    return pltpu.CompilerParams(vmem_limit_bytes=amount)


def position():
    column = lax.axis_index("shard")
    return lax.div(column, 2), lax.rem(column, 2), lax.axis_index("dp")


def first_kernel(tokens_ref, probs_ref, ids_ref, place_ref, out_ref, coef_ref):
    probs = probs_ref[...]
    weights = (probs / jnp.sum(probs, axis=0, keepdims=True)).astype(jnp.bfloat16)
    weights = weights.astype(jnp.float32)
    ids = ids_ref[...]
    tok, width = tokens_ref.shape
    coef_ref[...] = jnp.zeros_like(coef_ref)
    for slot in range(place_ref.shape[0]):
        named = jnp.where(ids == place_ref[slot], weights, 0.0)
        coef_ref[slot : slot + 1, :tok] = jnp.sum(named, axis=0, keepdims=True)
    out_ref[:, :width] = tokens_ref[...]
    out_ref[:, width:] = jnp.transpose(coef_ref[...])[:tok].astype(jnp.bfloat16)


def first(tokens, probs, ids, old_place):
    vmem = pl.BlockSpec(memory_space=pltpu.VMEM)
    return pl.pallas_call(
        first_kernel,
        in_specs=[vmem] * 3 + [pl.BlockSpec(memory_space=pltpu.SMEM)],
        out_specs=vmem,
        out_shape=jax.ShapeDtypeStruct((tokens.shape[0], tokens.shape[1] + LANES), tokens.dtype),
        scratch_shapes=[pltpu.VMEM((LANES, LANES), jnp.float32)],
        compiler_params=params(),
        cost_estimate=NOTHING,
    )(tokens, probs.T, ids.T, old_place)


def copy_kernel(plan, n_in, n_out, *refs):
    old_ref, new_ref = refs[:2]
    ins, refs = refs[2 : 2 + n_in], refs[-n_out - 3 :]
    outs, (held, in_sems, out_sems) = refs[:n_out], refs[n_out:]
    _, core, row = position()
    second = 2 * row + 1
    moved = (old_ref[second] != new_ref[second]).astype(jnp.int32)
    slots = {"mine": core, "theirs": 1 - core, "leaves": moved, "stays": 1 - moved}
    slots.update({i: i for i in range(3)})
    loads = [
        pltpu.make_async_copy(ins[i].at[slots[a]], held.at[n], in_sems.at[n])
        for n, (i, a, o, b) in enumerate(plan)
    ]
    stores = [
        pltpu.make_async_copy(held.at[n], outs[o].at[slots[b]], out_sems.at[n])
        for n, (i, a, o, b) in enumerate(plan)
    ]
    for c in loads:
        c.start()
    for n, c in enumerate(stores):
        loads[n].wait()
        c.start()
    for c in stores:
        c.wait()


def copies(plan, places, ins, counts, after=(), aliases=()):
    slot, kind = ins[0].shape[1:], ins[0].dtype
    smem, anywhere = pl.BlockSpec(memory_space=pltpu.SMEM), pl.BlockSpec(memory_space=pl.ANY)
    return pl.pallas_call(
        functools.partial(copy_kernel, plan, len(ins), len(counts)),
        in_specs=[smem] * 2 + [anywhere] * (len(ins) + len(aliases) + len(after)),
        out_specs=(anywhere,) * len(counts),
        out_shape=tuple(jax.ShapeDtypeStruct((n,) + slot, kind) for n in counts),
        input_output_aliases={2 + len(ins) + i: i for i in range(len(aliases))},
        scratch_shapes=[
            pltpu.VMEM((len(plan),) + slot, kind),
            pltpu.SemaphoreType.DMA((len(plan),)),
            pltpu.SemaphoreType.DMA((len(plan),)),
        ],
        compiler_params=params(MOST),
        cost_estimate=NOTHING,
    )(*places, *ins, *aliases, *after)


def order_kernel(mine_ref, other_ref, first_ref, second_ref, held, in_sems, out_sems):
    _, core, _ = position()
    loads = [
        pltpu.make_async_copy(mine_ref.at[core], held.at[core], in_sems.at[0]),
        pltpu.make_async_copy(other_ref.at[0], held.at[1 - core], in_sems.at[1]),
    ]
    stores = [
        pltpu.make_async_copy(held.at[n], out, out_sems.at[n])
        for n, out in enumerate((first_ref, second_ref))
    ]
    for c in loads:
        c.start()
    for c in loads:
        c.wait()
    for c in stores:
        c.start()
    for c in stores:
        c.wait()


def in_order(w_down, other):
    anywhere = pl.BlockSpec(memory_space=pl.ANY)
    slot = w_down.shape[1:]
    return pl.pallas_call(
        order_kernel,
        in_specs=[anywhere] * 2,
        out_specs=(anywhere,) * 2,
        out_shape=(jax.ShapeDtypeStruct(slot, w_down.dtype),) * 2,
        scratch_shapes=[
            pltpu.VMEM((2,) + slot, w_down.dtype),
            pltpu.SemaphoreType.DMA((2,)),
            pltpu.SemaphoreType.DMA((2,)),
        ],
        compiler_params=params(MOST),
        cost_estimate=NOTHING,
    )(w_down, other)


def join_kernel(*refs):
    pass


def joined(x, *after):
    anywhere = pl.BlockSpec(memory_space=pl.ANY)
    return pl.pallas_call(
        join_kernel,
        in_specs=[anywhere] * (1 + len(after)),
        out_specs=anywhere,
        out_shape=jax.ShapeDtypeStruct(x.shape, x.dtype),
        input_output_aliases={0: 0},
        compiler_params=params(),
        cost_estimate=NOTHING,
    )(x, *after)


def hidden_kernel(n_pieces, *refs):
    pieces, weights, (out_ref, x_ref, coef_ref) = refs[:n_pieces], refs[n_pieces:-3], refs[-3:]
    _, depth, block = weights[0].shape
    rows, width = x_ref.shape
    tall = rows // n_pieces
    pair, core, row = position()

    @pl.when(pl.program_id(0) == 0)
    def _():
        for n, p in enumerate(pieces):
            x_ref[n * tall : (n + 1) * tall] = p[:, :width]
            coef = p[:, width:].astype(jnp.float32)
            lane = lax.broadcasted_iota(jnp.int32, coef.shape, 1)
            coef = jnp.sum(jnp.where(lane == 2 * row + core, coef, 0.0), axis=1, keepdims=True)
            coef_ref[n * tall : (n + 1) * tall] = jnp.broadcast_to(coef, (tall, LANES))

    tile = min(rows, 512)
    for top in range(0, rows, tile):
        gate = jnp.zeros((tile, block), jnp.float32)
        up = jnp.zeros((tile, block), jnp.float32)
        for i, w in enumerate(weights):
            start = (2 * (pair ^ (i // 2)) + (core ^ (i % 2))) * depth
            x = x_ref[top : top + tile, pl.ds(pl.multiple_of(start, LANES), depth)]
            gate += jnp.dot(x, w[0], preferred_element_type=jnp.float32)
            up += jnp.dot(x, w[1], preferred_element_type=jnp.float32)
        coef = coef_ref[top : top + tile, :1]
        hidden = gate / (1.0 + jnp.exp(-gate)) * up * coef
        out_ref[top : top + tile] = hidden.astype(out_ref.dtype)


def hidden_of(pieces, weights):
    _, depth, ff = weights[0].shape
    block = 256
    tall, wide = pieces[0].shape
    rows = tall * len(pieces)
    return pl.pallas_call(
        functools.partial(hidden_kernel, len(pieces)),
        grid=(ff // block,),
        in_specs=[pl.BlockSpec((tall, wide), lambda f: (0, 0))] * len(pieces)
        + [pl.BlockSpec((2, depth, block), lambda f: (0, 0, f))] * len(weights),
        out_specs=pl.BlockSpec((rows, block), lambda f: (0, f)),
        out_shape=jax.ShapeDtypeStruct((rows, ff), pieces[0].dtype),
        scratch_shapes=[
            pltpu.VMEM((rows, wide - LANES), pieces[0].dtype),
            pltpu.VMEM((rows, LANES), jnp.float32),
        ],
        compiler_params=params(),
        cost_estimate=pl.CostEstimate(flops=1, bytes_accessed=1, transcendentals=0),
    )(*pieces, *weights)


def down_kernel(n_downs, hidden_ref, *refs):
    downs, (kept_ref, sent_ref) = refs[:n_downs], refs[-2:]
    depth = downs[0].shape[0]
    rows = kept_ref.shape[0]
    tile = min(rows, 512)
    contract = (((1,), (1,)), ((), ()))
    for i, w in enumerate(downs):
        for out, base in ((kept_ref, 0), (sent_ref, rows)):
            for top in range(0, rows, tile):
                part = lax.dot_general(
                    hidden_ref[base + top : base + top + tile], w[...], contract,
                    preferred_element_type=jnp.float32,
                )
                out[top : top + tile, i * depth : (i + 1) * depth] = part.astype(out.dtype)


def down_of(hidden, downs, after):
    depth, ff = downs[0].shape
    rows = hidden.shape[0] // 2
    vmem = pl.BlockSpec(memory_space=pltpu.VMEM)
    out = jax.ShapeDtypeStruct((rows, len(downs) * depth), hidden.dtype)
    return pl.pallas_call(
        functools.partial(down_kernel, len(downs)),
        in_specs=[vmem] * (1 + len(downs)) + [pl.BlockSpec(memory_space=pl.ANY)] * len(after),
        out_specs=(vmem, vmem),
        out_shape=(out, out),
        compiler_params=params(),
        cost_estimate=pl.CostEstimate(flops=1, bytes_accessed=1, transcendentals=0),
    )(hidden, *downs, *after)


def over_core(kept, sent, tok):
    total = kept.astype(jnp.float32) + swap(sent, "shard", 1).astype(jnp.float32)
    return total.reshape(-1, 2 * tok, total.shape[-1])


def step_z(total, bit):
    pairs = total.reshape((-1, 2) + total.shape[1:])
    return pairs[:, 0] + flip_z(pairs[:, 1].astype(jnp.bfloat16), bit).astype(jnp.float32)


def over_x(total):
    halves = total.reshape(total.shape[0], 2, -1, total.shape[-1])
    return halves[:, 0] + swap(halves[:, 1].astype(jnp.bfloat16), "dp", 1).astype(jnp.float32)


def over_z(total, bit):
    while total.shape[0] > 1:
        total = step_z(total, bit)
        bit *= 2
    return total[0].astype(jnp.bfloat16)


def place_kernel(depth, *refs):
    parts, out_ref = refs[:-1], refs[-1]
    pair, _, _ = position()
    for part, blocks in zip(parts, out_blocks(depth, [p.shape[1] for p in parts])):
        for n, (j, core) in enumerate(blocks):
            start = pl.multiple_of((2 * (pair ^ j) + core) * depth, LANES)
            out_ref[:, pl.ds(start, depth)] = part[:, n * depth : (n + 1) * depth]


def out_blocks(depth, widths):
    others = range(1, widths[1] // (2 * depth) + 1)
    return [[(0, 0), (0, 1)], [(j, core) for core in range(2) for j in others]]


def placed(parts, depth, width):
    vmem = pl.BlockSpec(memory_space=pltpu.VMEM)
    return pl.pallas_call(
        functools.partial(place_kernel, depth),
        in_specs=[vmem] * len(parts),
        out_specs=vmem,
        out_shape=jax.ShapeDtypeStruct((parts[0].shape[0], width), parts[0].dtype),
        compiler_params=params(),
        cost_estimate=NOTHING,
    )(*parts)


def local(tokens, router_probs, expert_ids, old_place, new_place, w_gate, w_up, w_down):
    tok, width = tokens.shape
    depth = w_gate.shape[1]
    n_z = lax.axis_size("dp") // 2
    places = (old_place, new_place)

    mine, theirs = copies(
        ((0, "mine", 0, 0), (1, "mine", 0, 1), (0, "theirs", 1, 0), (1, "theirs", 1, 1)),
        places, (w_gate, w_up), (2, 2),
    )
    (theirs_down,) = copies(((0, "theirs", 0, 0),), places, (w_down,), (1,), (mine,))
    near_weights = [mine, swap(theirs, "shard", 1)]
    weights = spread(near_weights)
    downs = [spread([d]) for d in in_order(w_down, swap(theirs_down, "shard", 1))]

    own = first(tokens, router_probs, expert_ids, old_place)
    columns = [own] + [flip_z(own, j) for j in range(1, n_z)]
    across = [swap(own, "dp", 1)]
    for c in columns[1:]:
        across.append(swap(joined(c, across[-1]), "dp", 1))
    near = [joined(jnp.concatenate(p, axis=0), weights[2]) for p in zip(columns, across)]
    far = [swap(p, "shard", 1) for p in near]

    hidden = hidden_of(near + far, weights)
    (leave,) = copies(
        tuple((i, "leaves", 0, i) for i in range(3)), places, (w_gate, w_up, w_down), (3,), across
    )
    arrive = passed_along(leave, "dp", 1)
    news = copies(
        tuple((0, i, i, "leaves") for i in range(3))
        + tuple((i + 1, "stays", i, "stays") for i in range(3)),
        places, (arrive, w_gate, w_up, w_down), (2, 2, 2),
    )

    groups = [[d[0] for d in downs]] + [d[1:] for d in downs]
    kept, sent = down_of(hidden, groups[0], ())
    own_rows = step_z(over_core(kept, sent, tok), 1)
    kept, sent = down_of(hidden, groups[1], (sent,))
    first_rows = over_core(kept, sent, tok)
    kept, sent = down_of(hidden, groups[2], (sent, news[0], own_rows, first_rows))
    second_rows = over_core(kept, sent, tok)
    late = over_x(step_z(jnp.concatenate([first_rows, second_rows], axis=-1), 1))
    parts = [over_z(over_x(own_rows), 2), over_z(late, 2)]
    moe_output = placed(parts, depth, width)

    return (moe_output, *news)


def solution(mesh):
    in_specs = (
        P(("dp", "shard"), None),
        P(("dp", "shard"), None),
        P(("dp", "shard"), None),
        P(),
        P(),
        P("dp", "shard", None),
        P("dp", "shard", None),
        P("dp", "shard", None),
    )
    out_specs = (
        P(("dp", "shard"), None),
        P("dp", "shard", None),
        P("dp", "shard", None),
        P("dp", "shard", None),
    )
    return jax.shard_map(local, mesh=mesh, in_specs=in_specs, out_specs=out_specs, check_vma=False)
```

```python
import functools

import jax
import jax.numpy as jnp
from jax import lax
from jax.experimental import pallas as pl
from jax.experimental.pallas import tpu as pltpu
from jax.sharding import PartitionSpec as P

LANES = 128
VMEM_BYTES = 32 * 1024 * 1024
MOST = 56 * 1024 * 1024
NOTHING = pl.CostEstimate(flops=0, bytes_accessed=0, transcendentals=0)


def swap(x, axis, bit):
    return lax.ppermute(x, axis, [(i, i ^ bit) for i in range(lax.axis_size(axis))])


def passed_along(x, axis, by):
    size = lax.axis_size(axis)
    return lax.ppermute(x, axis, [(i, (i + by) % size) for i in range(size)])


def flip_z(x, bits):
    return swap(x, "dp", 2 * bits)


def spread(pieces):
    bit = 2
    while bit < lax.axis_size("shard"):
        pieces = pieces + [swap(p, "shard", bit) for p in pieces]
        bit *= 2
    return pieces


def params(amount=VMEM_BYTES):
    return pltpu.CompilerParams(vmem_limit_bytes=amount)


def position():
    column = lax.axis_index("shard")
    return lax.div(column, 2), lax.rem(column, 2), lax.axis_index("dp")


def first_kernel(tokens_ref, probs_ref, ids_ref, place_ref, out_ref, coef_ref):
    probs = probs_ref[...]
    weights = (probs / jnp.sum(probs, axis=0, keepdims=True)).astype(jnp.bfloat16)
    weights = weights.astype(jnp.float32)
    ids = ids_ref[...]
    tok, width = tokens_ref.shape
    coef_ref[...] = jnp.zeros_like(coef_ref)
    for slot in range(place_ref.shape[0]):
        named = jnp.where(ids == place_ref[slot], weights, 0.0)
        coef_ref[slot : slot + 1, :tok] = jnp.sum(named, axis=0, keepdims=True)
    out_ref[:, :width] = tokens_ref[...]
    out_ref[:, width:] = jnp.transpose(coef_ref[...])[:tok].astype(jnp.bfloat16)


def first(tokens, probs, ids, old_place):
    vmem = pl.BlockSpec(memory_space=pltpu.VMEM)
    return pl.pallas_call(
        first_kernel,
        in_specs=[vmem] * 3 + [pl.BlockSpec(memory_space=pltpu.SMEM)],
        out_specs=vmem,
        out_shape=jax.ShapeDtypeStruct((tokens.shape[0], tokens.shape[1] + LANES), tokens.dtype),
        scratch_shapes=[pltpu.VMEM((LANES, LANES), jnp.float32)],
        compiler_params=params(),
        cost_estimate=NOTHING,
    )(tokens, probs.T, ids.T, old_place)


def copy_kernel(plan, n_in, n_out, *refs):
    old_ref, new_ref = refs[:2]
    ins, refs = refs[2 : 2 + n_in], refs[-n_out - 3 :]
    outs, (held, in_sems, out_sems) = refs[:n_out], refs[n_out:]
    _, core, row = position()
    second = 2 * row + 1
    moved = (old_ref[second] != new_ref[second]).astype(jnp.int32)
    slots = {"mine": core, "theirs": 1 - core, "leaves": moved, "stays": 1 - moved}
    slots.update({i: i for i in range(3)})
    tall = held.shape[1] // 2
    parts = [(n, pl.ds(h * tall, tall)) for n in range(len(plan)) for h in range(2)]
    loads, stores = [], []
    for k, (n, part) in enumerate(parts):
        i, a, o, b = plan[n]
        here = held.at[n, part]
        loads.append(pltpu.make_async_copy(ins[i].at[slots[a], part], here, in_sems.at[k]))
        stores.append(pltpu.make_async_copy(here, outs[o].at[slots[b], part], out_sems.at[k]))
    for c in loads:
        c.start()
    for n, c in enumerate(stores):
        loads[n].wait()
        c.start()
    for c in stores:
        c.wait()


def copies(plan, places, ins, counts, after=(), aliases=()):
    slot, kind = ins[0].shape[1:], ins[0].dtype
    smem, anywhere = pl.BlockSpec(memory_space=pltpu.SMEM), pl.BlockSpec(memory_space=pl.ANY)
    return pl.pallas_call(
        functools.partial(copy_kernel, plan, len(ins), len(counts)),
        in_specs=[smem] * 2 + [anywhere] * (len(ins) + len(aliases) + len(after)),
        out_specs=(anywhere,) * len(counts),
        out_shape=tuple(jax.ShapeDtypeStruct((n,) + slot, kind) for n in counts),
        input_output_aliases={2 + len(ins) + i: i for i in range(len(aliases))},
        scratch_shapes=[
            pltpu.VMEM((len(plan),) + slot, kind),
            pltpu.SemaphoreType.DMA((2 * len(plan),)),
            pltpu.SemaphoreType.DMA((2 * len(plan),)),
        ],
        compiler_params=params(MOST),
        cost_estimate=NOTHING,
    )(*places, *ins, *aliases, *after)


def order_kernel(mine_ref, other_ref, first_ref, second_ref, held, in_sems, out_sems):
    _, core, _ = position()
    loads = [
        pltpu.make_async_copy(mine_ref.at[core], held.at[core], in_sems.at[0]),
        pltpu.make_async_copy(other_ref.at[0], held.at[1 - core], in_sems.at[1]),
    ]
    stores = [
        pltpu.make_async_copy(held.at[n], out, out_sems.at[n])
        for n, out in enumerate((first_ref, second_ref))
    ]
    for c in loads:
        c.start()
    for c in loads:
        c.wait()
    for c in stores:
        c.start()
    for c in stores:
        c.wait()


def in_order(w_down, other):
    anywhere = pl.BlockSpec(memory_space=pl.ANY)
    slot = w_down.shape[1:]
    return pl.pallas_call(
        order_kernel,
        in_specs=[anywhere] * 2,
        out_specs=(anywhere,) * 2,
        out_shape=(jax.ShapeDtypeStruct(slot, w_down.dtype),) * 2,
        scratch_shapes=[
            pltpu.VMEM((2,) + slot, w_down.dtype),
            pltpu.SemaphoreType.DMA((2,)),
            pltpu.SemaphoreType.DMA((2,)),
        ],
        compiler_params=params(MOST),
        cost_estimate=NOTHING,
    )(w_down, other)


def join_kernel(*refs):
    pass


def joined(x, *after):
    anywhere = pl.BlockSpec(memory_space=pl.ANY)
    return pl.pallas_call(
        join_kernel,
        in_specs=[anywhere] * (1 + len(after)),
        out_specs=anywhere,
        out_shape=jax.ShapeDtypeStruct(x.shape, x.dtype),
        input_output_aliases={0: 0},
        compiler_params=params(),
        cost_estimate=NOTHING,
    )(x, *after)


def hidden_kernel(n_pieces, *refs):
    pieces, weights, (out_ref, x_ref, coef_ref) = refs[:n_pieces], refs[n_pieces:-3], refs[-3:]
    _, depth, block = weights[0].shape
    rows, width = x_ref.shape
    tall = rows // n_pieces
    pair, core, row = position()

    @pl.when(pl.program_id(0) == 0)
    def _():
        for n, p in enumerate(pieces):
            x_ref[n * tall : (n + 1) * tall] = p[:, :width]
            coef = p[:, width:].astype(jnp.float32)
            lane = lax.broadcasted_iota(jnp.int32, coef.shape, 1)
            coef = jnp.sum(jnp.where(lane == 2 * row + core, coef, 0.0), axis=1, keepdims=True)
            coef_ref[n * tall : (n + 1) * tall] = jnp.broadcast_to(coef, (tall, LANES))

    tile = min(rows, 512)
    for top in range(0, rows, tile):
        gate = jnp.zeros((tile, block), jnp.float32)
        up = jnp.zeros((tile, block), jnp.float32)
        for i, w in enumerate(weights):
            start = (2 * (pair ^ (i // 2)) + (core ^ (i % 2))) * depth
            x = x_ref[top : top + tile, pl.ds(pl.multiple_of(start, LANES), depth)]
            gate += jnp.dot(x, w[0], preferred_element_type=jnp.float32)
            up += jnp.dot(x, w[1], preferred_element_type=jnp.float32)
        coef = coef_ref[top : top + tile, :1]
        hidden = gate / (1.0 + jnp.exp(-gate)) * up * coef
        out_ref[top : top + tile] = hidden.astype(out_ref.dtype)


def hidden_of(pieces, weights):
    _, depth, ff = weights[0].shape
    block = 256
    tall, wide = pieces[0].shape
    rows = tall * len(pieces)
    return pl.pallas_call(
        functools.partial(hidden_kernel, len(pieces)),
        grid=(ff // block,),
        in_specs=[pl.BlockSpec((tall, wide), lambda f: (0, 0))] * len(pieces)
        + [pl.BlockSpec((2, depth, block), lambda f: (0, 0, f))] * len(weights),
        out_specs=pl.BlockSpec((rows, block), lambda f: (0, f)),
        out_shape=jax.ShapeDtypeStruct((rows, ff), pieces[0].dtype),
        scratch_shapes=[
            pltpu.VMEM((rows, wide - LANES), pieces[0].dtype),
            pltpu.VMEM((rows, LANES), jnp.float32),
        ],
        compiler_params=params(),
        cost_estimate=pl.CostEstimate(flops=1, bytes_accessed=1, transcendentals=0),
    )(*pieces, *weights)


def down_kernel(n_downs, hidden_ref, *refs):
    downs, (kept_ref, sent_ref) = refs[:n_downs], refs[-2:]
    depth = downs[0].shape[0]
    rows = kept_ref.shape[0]
    tile = min(rows, 512)
    contract = (((1,), (1,)), ((), ()))
    for i, w in enumerate(downs):
        for out, base in ((kept_ref, 0), (sent_ref, rows)):
            for top in range(0, rows, tile):
                part = lax.dot_general(
                    hidden_ref[base + top : base + top + tile], w[...], contract,
                    preferred_element_type=jnp.float32,
                )
                out[top : top + tile, i * depth : (i + 1) * depth] = part.astype(out.dtype)


def down_of(hidden, downs, after):
    depth, ff = downs[0].shape
    rows = hidden.shape[0] // 2
    vmem = pl.BlockSpec(memory_space=pltpu.VMEM)
    out = jax.ShapeDtypeStruct((rows, len(downs) * depth), hidden.dtype)
    return pl.pallas_call(
        functools.partial(down_kernel, len(downs)),
        in_specs=[vmem] * (1 + len(downs)) + [pl.BlockSpec(memory_space=pl.ANY)] * len(after),
        out_specs=(vmem, vmem),
        out_shape=(out, out),
        compiler_params=params(),
        cost_estimate=pl.CostEstimate(flops=1, bytes_accessed=1, transcendentals=0),
    )(hidden, *downs, *after)


def over_core(kept, sent, tok):
    total = kept.astype(jnp.float32) + swap(sent, "shard", 1).astype(jnp.float32)
    return total.reshape(-1, 2 * tok, total.shape[-1])


def step_z(total, bit):
    pairs = total.reshape((-1, 2) + total.shape[1:])
    return pairs[:, 0] + flip_z(pairs[:, 1].astype(jnp.bfloat16), bit).astype(jnp.float32)


def over_x(total):
    halves = total.reshape(total.shape[0], 2, -1, total.shape[-1])
    return halves[:, 0] + swap(halves[:, 1].astype(jnp.bfloat16), "dp", 1).astype(jnp.float32)


def over_z(total, bit):
    while total.shape[0] > 1:
        total = step_z(total, bit)
        bit *= 2
    return total[0].astype(jnp.bfloat16)


def place_kernel(depth, *refs):
    parts, out_ref = refs[:-1], refs[-1]
    pair, _, _ = position()
    for part, blocks in zip(parts, out_blocks(depth, [p.shape[1] for p in parts])):
        for n, (j, core) in enumerate(blocks):
            start = pl.multiple_of((2 * (pair ^ j) + core) * depth, LANES)
            out_ref[:, pl.ds(start, depth)] = part[:, n * depth : (n + 1) * depth]


def out_blocks(depth, widths):
    others = range(1, widths[1] // depth + 1)
    return [[(0, 0), (0, 1)] + [(j, 0) for j in others], [(j, 1) for j in others]]


def placed(parts, depth, width):
    vmem = pl.BlockSpec(memory_space=pltpu.VMEM)
    return pl.pallas_call(
        functools.partial(place_kernel, depth),
        in_specs=[vmem] * len(parts),
        out_specs=vmem,
        out_shape=jax.ShapeDtypeStruct((parts[0].shape[0], width), parts[0].dtype),
        compiler_params=params(),
        cost_estimate=NOTHING,
    )(*parts)


def local(tokens, router_probs, expert_ids, old_place, new_place, w_gate, w_up, w_down):
    tok, width = tokens.shape
    depth = w_gate.shape[1]
    n_z = lax.axis_size("dp") // 2
    places = (old_place, new_place)

    mine, theirs = copies(
        ((0, "mine", 0, 0), (1, "mine", 0, 1), (0, "theirs", 1, 0), (1, "theirs", 1, 1)),
        places, (w_gate, w_up), (2, 2),
    )
    (theirs_down,) = copies(((0, "theirs", 0, 0),), places, (w_down,), (1,), (mine,))
    near_weights = [mine, swap(theirs, "shard", 1)]
    weights = spread(near_weights)
    downs = [spread([d]) for d in in_order(w_down, swap(theirs_down, "shard", 1))]

    own = first(tokens, router_probs, expert_ids, old_place)
    columns = [own] + [flip_z(own, j) for j in range(1, n_z)]
    across = [swap(own, "dp", 1)]
    for c in columns[1:]:
        across.append(swap(joined(c, across[-1]), "dp", 1))
    near = [joined(jnp.concatenate(p, axis=0), weights[2]) for p in zip(columns, across)]
    far = [swap(p, "shard", 1) for p in near]

    hidden = hidden_of(near + far, weights)
    (leave,) = copies(
        tuple((i, "leaves", 0, i) for i in range(3)), places, (w_gate, w_up, w_down), (3,), across
    )
    arrive = passed_along(leave, "dp", 1)
    news = copies(
        tuple((0, i, i, "leaves") for i in range(3))
        + tuple((i + 1, "stays", i, "stays") for i in range(3)),
        places, (arrive, w_gate, w_up, w_down), (2, 2, 2),
    )

    groups = [[d[0] for d in downs]] + [d[1:] for d in downs]
    kept, sent = down_of(hidden, groups[0], ())
    own_rows = step_z(over_core(kept, sent, tok), 1)
    kept, sent = down_of(hidden, groups[1], (sent,))
    first_rows = step_z(over_core(kept, sent, tok), 1)
    kept, sent = down_of(hidden, groups[2], (sent, news[0], own_rows, first_rows))
    early = over_x(jnp.concatenate([own_rows, first_rows], axis=-1))
    late = over_x(step_z(over_core(kept, sent, tok), 1))
    parts = [over_z(early, 2), over_z(late, 2)]
    moe_output = placed(parts, depth, width)

    return (moe_output, *news)


def solution(mesh):
    in_specs = (
        P(("dp", "shard"), None),
        P(("dp", "shard"), None),
        P(("dp", "shard"), None),
        P(),
        P(),
        P("dp", "shard", None),
        P("dp", "shard", None),
        P("dp", "shard", None),
    )
    out_specs = (
        P(("dp", "shard"), None),
        P("dp", "shard", None),
        P("dp", "shard", None),
        P("dp", "shard", None),
    )
    return jax.shard_map(local, mesh=mesh, in_specs=in_specs, out_specs=out_specs, check_vma=False)
```
